32 devices in a mesh: dp: 8 (over z, core), expert: 4 (over y, x).
Axes of the slice: x: 2, y: 2, z: 4, core: 2. Of those that a mesh axis runs over, the one named last changes fastest.
Arguments:
- tokens: bfloat16 [4096, 2048], P(('dp', 'expert'))
- targets: bfloat16 [4096, 2048], P(('dp', 'expert'))
- routes: int32 [4096, 8], P(('dp', 'expert')), may hold values from 0 to 15, all different within a row; in each aligned block of 128 rows (0 to 127, 128 to 255, ...) at most 64 rows name the same one
- route_logits: float32 [4096, 8], P(('dp', 'expert')), may hold values from -3 to 3
- slot_order: int32 [4096, 8], P(('dp', 'expert')), may hold values from 0 to 7, each once within a row
- seq_ids: int32 [4096], P(('dp', 'expert')), may hold values from 0 to 63, as said below
- w_gate: bfloat16 [16, 2048, 384], P('expert')
- w_up: bfloat16 [16, 2048, 384], P('expert')
- w_down: bfloat16 [2048, 16, 384], P('dp', 'expert')
Outputs:
- mixed: bfloat16 [4096, 2048], P(('dp', 'expert'))
- seq_loss: float32 [64], replicated
- dual_weight: float32 [64], replicated
- grad_down: float32 [2048, 16, 384], P('dp', 'expert')
The draws below stay inside these ranges and needn't reach their ends.
Inputs may be any that keep to these rules, and one draw needn't show every extreme that they name: `routes`: in each aligned block of 128 rows (the rows of one device) every expert is named by exactly 64 rows; the 8 numbers of a row differ. `slot_order`: each row is a permutation of 0 to 7. `seq_ids`: sequence numbers never fall along the tokens, and every number names one or more tokens.
All inputs are finite; a program needn't handle non-finite values.
Results may differ from the reference program's by a relative error of at most 0.0046.
Values may be sent and summed in bfloat16 or wider, within the bound.
No kernel may reach another device: no remote copies, remote signals or barrier semaphores. Data moves between devices by JAX's collectives and lax.ppermute only.
A program may use at most 64 MiB of HBM per device.

```python
import math
import jax
import jax.numpy as jnp
import numpy as np
from jax import lax

D = 2048
H = 384
EXPERTS = 16
TOP = 8
NSEQ = 64
BISECT_STEPS = 40
TOK_DEV = 128
TOKENS = 4096
CAP = 64
GRAD_SCALE = 512


shared_part = 0.9


own_part = 0.4359


def sequence_numbers(key):
    span = TOKENS // NSEQ
    reach = max(span // 4, 1)
    shifts = jax.random.randint(jax.random.fold_in(key, 7), (NSEQ - 1,), 0, reach + 1)
    bounds = jnp.arange(1, NSEQ, dtype=jnp.int32) * span + shifts.astype(jnp.int32)
    positions = jnp.arange(TOKENS, dtype=jnp.int32)
    return jnp.sum((positions[:, None] >= bounds[None, :]).astype(jnp.int32), axis=1).astype(jnp.int32)


def blended(key, full_shape, common_shape, fan_in):
    common = jax.random.normal(jax.random.fold_in(key, 1), common_shape, jnp.float32)
    own = jax.random.normal(jax.random.fold_in(key, 2), full_shape, jnp.float32)
    mixture = jnp.clip(shared_part * common + own_part * own, -6.0, 6.0)
    return (mixture * float(fan_in) ** (-0.5)).astype(jnp.bfloat16)


def draw_seq_ids(key, part):
    return sequence_numbers(key)


def draw_tokens(key, part):
    seq_number = sequence_numbers(key)
    key = jax.random.fold_in(key, 19)
    scales = jnp.exp(jax.random.uniform(jax.random.fold_in(key, 1), (NSEQ,), jnp.float32, -0.35, 0.35))
    noise = jnp.clip(jax.random.normal(jax.random.fold_in(key, 2), (TOKENS, D), jnp.float32), -6.0, 6.0)
    return (noise * scales[seq_number][:, None]).astype(jnp.bfloat16)


def draw_targets(key, part):
    seq_number = sequence_numbers(key)
    key = jax.random.fold_in(key, 23)
    levels = 0.7 * jnp.exp(jax.random.uniform(jax.random.fold_in(key, 11), (NSEQ,), jnp.float32, -0.7, 0.7))
    noise = jax.random.normal(jax.random.fold_in(key, 13), (TOKENS, D), jnp.float32)
    return (noise * levels[seq_number][:, None]).astype(jnp.bfloat16)


def draw_w_gate(key, part):
    key = jax.random.fold_in(key, 29)
    return blended(key, (EXPERTS, D, H), (1, D, H), D)


def draw_w_up(key, part):
    key = jax.random.fold_in(key, 31)
    return blended(key, (EXPERTS, D, H), (1, D, H), D)


def draw_w_down(key, part):
    key = jax.random.fold_in(key, 37)
    return blended(key, (D, EXPERTS, H), (D, 1, H), H)


def shard_levels(key, dims, cuts, low, largest):
    factor_of = 1.0
    for position, parts in cuts:
        steps = jax.random.uniform(jax.random.fold_in(jax.random.fold_in(key, 6), position), (parts,), jnp.float32, low / len(cuts), largest / len(cuts))
        factor_of = factor_of * jnp.repeat(jnp.exp(steps), dims[position] // parts).reshape((-1,) + (1,) * (len(dims) - 1 - position))
    return factor_of


def assign_block(stream_key, own, number, rows, count, top, most, skew):
    ranking = jax.random.permutation(stream_key, count)
    packed, usual = shares(count, rows * top, most, skew, True), shares(count, rows * top, most, skew, False)
    places = jnp.arange(count)

    def named(lengths, offset_by):
        used = int((lengths > 0).sum())
        fixed = max(1, used // 4)
        passed = fixed + (places - fixed + offset_by * (used - fixed)) % max(1, count - fixed)
        return jnp.zeros((count,), jnp.int32).at[ranking[jnp.where(places < fixed, places, passed)]].set(jnp.asarray(lengths, jnp.int32))

    lengths = jnp.where(number % 4 == 0, named(packed, number // 4), named(usual, number - number // 4 - 1))
    mixed = jax.random.permutation(jax.random.fold_in(own, 3), count)
    donor, taker = mixed[0:count // 2 * 2:2], mixed[1:count // 2 * 2:2]
    room = jnp.minimum(lengths[donor] - 1, most - lengths[taker]) // 2
    room = jnp.where((donor == ranking[0]) | (taker == ranking[0]) | (lengths[taker] == 0), 0, jnp.maximum(room, 0))
    passed = jax.random.randint(jax.random.fold_in(own, 4), (count // 2,), 0, 1 << 20) % (room + 1)
    lengths = lengths.at[donor].add(-passed).at[taker].add(passed)
    members = jnp.searchsorted(jnp.cumsum(lengths), jnp.arange(rows * top), side="right").astype(jnp.int32)
    grid = members.reshape(top, rows).T
    grid = grid[jax.random.permutation(jax.random.fold_in(own, 1), rows)]
    offset_by = jax.random.randint(jax.random.fold_in(own, 2), (rows, 1), 0, top)
    return jnp.take_along_axis(grid, (jnp.arange(top)[None, :] + offset_by) % top, axis=1)


def shares(amount, total, most, skew, full):
    loads = [(1 << 20) // math.isqrt(grade ** skew) + 1 for grade in range(1, amount + 1)]
    largest = most if full else min(most, max(-(-total // amount), total * loads[0] // sum(loads)))
    least = 1 if total - largest >= amount - 1 else 0
    counts, rest = [largest] + [least] * (amount - 1), total - largest - least * (amount - 1)
    while rest > 0:
        free = [i for i in range(1, amount) if counts[i] < largest] or [i for i in range(1, amount) if counts[i] < most]
        mass, left = sum([loads[i] for i in free]), rest
        for i in free:
            more = min(most - counts[i], max(1, left * loads[i] // mass), rest)
            counts[i] = counts[i] + more
            rest = rest - more
    return np.array(counts)


def setup_inputs(seed: int = 0) -> dict:
    splits = jax.random.split(jax.random.key(seed), 10)
    tokens = draw_tokens(jax.random.fold_in(splits[9], 71), 0)
    targets = draw_targets(jax.random.fold_in(splits[9], 71), 0)
    routes_keys = jax.random.split(jax.random.fold_in(splits[2], 1), TOKENS // TOK_DEV)
    routes_turns = jax.random.permutation(jax.random.fold_in(splits[2], 3), TOKENS // TOK_DEV)
    routes = jax.vmap(lambda own, number: assign_block(jax.random.fold_in(splits[2], 2), own, number, TOK_DEV, EXPERTS, TOP, CAP, 0))(routes_keys, routes_turns).reshape((TOKENS, TOP))
    route_logits = jnp.clip(jax.random.uniform(splits[3], (TOKENS, TOP), jnp.float32, -3.0, 3.0) * shard_levels(splits[3], (TOKENS, TOP), ((0, 32),), -0.4, 0.0), -3.0, 3.0)
    slot_order = jax.vmap(lambda own: jax.random.permutation(own, TOP))(jax.random.split(splits[4], TOKENS)).reshape((TOKENS, TOP)).astype(jnp.int32)
    seq_ids = draw_seq_ids(jax.random.fold_in(splits[9], 71), 0)
    w_gate = draw_w_gate(jax.random.fold_in(splits[9], 71), 0)
    w_up = draw_w_up(jax.random.fold_in(splits[9], 71), 0)
    w_down = draw_w_down(jax.random.fold_in(splits[9], 71), 0)
    return {"tokens": tokens, "targets": targets, "routes": routes, "route_logits": route_logits, "slot_order": slot_order, "seq_ids": seq_ids, "w_gate": w_gate, "w_up": w_up, "w_down": w_down}


radius_factor = 2.0

def unchanged(single_value):
    return single_value

def dual_search(seq_loss, pair_total, one_total):
    sum_total = one_total(jnp.sum(seq_loss))

    def advance(step_index, bounds):
        lower, upper = bounds
        middle = 0.5 * (lower + upper)
        excess = jnp.maximum(seq_loss - middle, 0.0)
        square_sum, plain_sum = pair_total((jnp.sum(excess * excess), jnp.sum(excess)))
        is_above = NSEQ * square_sum - radius_factor * plain_sum * plain_sum >= 0.0
        return (jnp.where(is_above, lower, middle), jnp.where(is_above, middle, upper))
    lower, upper = lax.fori_loop(0, BISECT_STEPS, advance, (-sum_total, sum_total))
    excess = jnp.maximum(seq_loss - 0.5 * (lower + upper), 0.0)
    return excess / one_total(jnp.sum(excess))

def route_gates(route_logits, slot_order):
    picked = jnp.take_along_axis(route_logits, slot_order, axis=1)
    raised = jnp.exp(picked)
    return raised / lax.optimization_barrier(jnp.sum(raised, axis=1, keepdims=True))

def reference(tokens, targets, routes, route_logits, slot_order, seq_ids, w_gate, w_up, w_down):
    slot_count = TOKENS * TOP
    per_expert = slot_count // EXPERTS
    gate_probs = route_gates(route_logits, slot_order)
    flat_route = routes.reshape(slot_count)
    slot_sorted = jnp.argsort(flat_route, stable=True).astype(jnp.int32)
    grouped = slot_sorted.reshape(EXPERTS, per_expert)
    flat_gates = gate_probs.reshape(slot_count)

    def expert_forward(combined, expert):
        chosen = grouped[expert]
        token_rows = tokens[chosen // TOP]
        gate_proj = jnp.dot(token_rows, w_gate[expert], preferred_element_type=jnp.float32)
        up_proj = jnp.dot(token_rows, w_up[expert], preferred_element_type=jnp.float32)
        hidden = (jax.nn.silu(gate_proj) * up_proj).astype(jnp.bfloat16)
        down_slice = lax.dynamic_index_in_dim(w_down, expert, 1, keepdims=False)
        expert_out = jnp.dot(hidden, down_slice.T, preferred_element_type=jnp.float32).astype(jnp.bfloat16)
        weighted = flat_gates[chosen][:, None] * expert_out.astype(jnp.float32)
        combined = combined.at[chosen // TOP].add(weighted)
        return (combined, hidden)
    combined, hidden_all = lax.scan(expert_forward, jnp.zeros((TOKENS, D), jnp.float32), jnp.arange(EXPERTS, dtype=jnp.int32))
    error = combined - targets.astype(jnp.float32)
    seq_sq = jax.ops.segment_sum(lax.optimization_barrier(jnp.sum(error * error, axis=1)), seq_ids, num_segments=NSEQ)
    seq_len = jax.ops.segment_sum(jnp.ones((TOKENS,), jnp.float32), seq_ids, num_segments=NSEQ)
    seq_loss = seq_sq / (seq_len * D)
    dual_weight = dual_search(seq_loss, unchanged, unchanged)
    seq_rate = dual_weight / seq_len
    slot_weight = GRAD_SCALE * gate_probs * seq_rate[seq_ids][:, None]
    flat_weight = slot_weight.reshape(slot_count)
    error_low = error.astype(jnp.bfloat16)

    def expert_grad(expert):
        chosen = grouped[expert]
        scaled = (flat_weight[chosen][:, None] * hidden_all[expert].astype(jnp.float32)).astype(jnp.bfloat16)
        return jnp.dot(error_low[chosen // TOP].T, scaled, preferred_element_type=jnp.float32)
    grad_stack = lax.map(expert_grad, jnp.arange(EXPERTS, dtype=jnp.int32))
    return (combined.astype(jnp.bfloat16), seq_loss, dual_weight, jnp.transpose(grad_stack, (1, 0, 2)))
```

```python
import functools

import jax
import jax.numpy as jnp
from jax import lax
from jax.experimental import pallas as pl
from jax.experimental.pallas import tpu as pltpu
from jax.sharding import PartitionSpec as P

NSEQ = 64
BISECT_STEPS = 40


radius_factor = 2.0


def unchanged(single_value):
    return single_value


def dual_search(seq_loss, pair_total, one_total):
    sum_total = one_total(jnp.sum(seq_loss))

    def advance(step_index, bounds):
        lower, upper = bounds
        middle = 0.5 * (lower + upper)
        excess = jnp.maximum(seq_loss - middle, 0.0)
        square_sum, plain_sum = pair_total((jnp.sum(excess * excess), jnp.sum(excess)))
        is_above = NSEQ * square_sum - radius_factor * plain_sum * plain_sum >= 0.0
        return (jnp.where(is_above, lower, middle), jnp.where(is_above, middle, upper))

    lower, upper = lax.fori_loop(0, BISECT_STEPS, advance, (-sum_total, sum_total))
    excess = jnp.maximum(seq_loss - 0.5 * (lower + upper), 0.0)
    return excess / one_total(jnp.sum(excess))


def route_gates(route_logits, slot_order):
    top_k = slot_order.shape[1]
    columns = lax.broadcasted_iota(jnp.int32, (1, 1, top_k), 2)
    picked = jnp.sum(
        jnp.where(slot_order[:, :, None] == columns, route_logits[:, None, :], 0.0), axis=2
    )
    raised = jnp.exp(picked)
    return raised / jnp.sum(raised, axis=1, keepdims=True)


def by_expert(blocks, groups):
    exp_dev = blocks.shape[0] // groups
    tail_shape = blocks.shape[1:]
    split_view = blocks.reshape((groups, exp_dev) + tail_shape)
    moved_view = jnp.swapaxes(split_view, 0, 1)
    return moved_view.reshape((exp_dev, groups * tail_shape[0]) + tail_shape[1:])


def by_source(local_rows, groups):
    exp_dev = local_rows.shape[0]
    capacity = local_rows.shape[1] // groups
    tail_shape = local_rows.shape[2:]
    split_view = local_rows.reshape((exp_dev, groups, capacity) + tail_shape)
    return jnp.swapaxes(split_view, 0, 1).reshape((exp_dev * groups, capacity) + tail_shape)


def row_plan(tokens, targets, routes, route_logits, slot_order, seq_ids, w_gate, w_up, w_down):
    tok_rows, feat_width = tokens.shape
    top_k = routes.shape[1]
    groups = lax.axis_size("expert")
    exp_dev = w_gate.shape[0]
    experts = exp_dev * groups
    slot_count = tok_rows * top_k
    capacity = slot_count // experts
    grad_scale = float(tok_rows * lax.axis_size("dp") * groups // 8)
    flat_route = routes.reshape(slot_count)
    expert_hot = (flat_route[:, None] == lax.broadcasted_iota(jnp.int32, (1, experts), 1)).astype(
        jnp.int32
    )
    slot_rank = jnp.sum((jnp.cumsum(expert_hot, axis=0) - 1) * expert_hot, axis=1)
    slot_index = flat_route * capacity + slot_rank
    inverse = (
        jnp.zeros((slot_count,), jnp.int32).at[slot_index].set(lax.iota(jnp.int32, slot_count))
    )
    source_row = inverse // top_k
    gate_probs = route_gates(route_logits, slot_order)
    send_rows = tokens[source_row].reshape(experts, capacity, feat_width)
    arrived = lax.all_to_all(send_rows, "expert", split_axis=0, concat_axis=0, tiled=True)
    local_rows = by_expert(arrived, groups)
    gate_proj = jnp.einsum("erd,edh->erh", local_rows, w_gate, preferred_element_type=jnp.float32)
    up_proj = jnp.einsum("erd,edh->erh", local_rows, w_up, preferred_element_type=jnp.float32)
    hidden = (jax.nn.silu(gate_proj) * up_proj).astype(jnp.bfloat16)
    expert_out = jnp.einsum(
        "erh,neh->ern",
        hidden,
        lax.all_gather(w_down, "dp", axis=0, tiled=True),
        preferred_element_type=jnp.float32,
    ).astype(jnp.bfloat16)
    returned = lax.all_to_all(
        by_source(expert_out, groups), "expert", split_axis=0, concat_axis=0, tiled=True
    )
    per_slot = returned.reshape(slot_count, feat_width)[slot_index].reshape(
        tok_rows, top_k, feat_width
    )
    combined = jnp.sum(gate_probs[:, :, None] * per_slot.astype(jnp.float32), axis=1)
    error = combined - targets.astype(jnp.float32)
    error_low = error.astype(jnp.bfloat16)
    sent_error = lax.all_to_all(
        error_low[source_row].reshape(experts, capacity, feat_width),
        "expert",
        split_axis=0,
        concat_axis=0,
        tiled=True,
    )
    seq_hot = seq_ids[:, None] == lax.broadcasted_iota(jnp.int32, (1, NSEQ), 1)
    partial_sq = jnp.sum(jnp.where(seq_hot, jnp.sum(error * error, axis=1)[:, None], 0.0), axis=0)
    counts = jnp.sum(seq_hot.astype(jnp.float32), axis=0)
    seq_sq, seq_len = lax.psum((partial_sq, counts), ("dp", "expert"))
    seq_loss = seq_sq / (seq_len * feat_width)
    dual_weight = dual_search(seq_loss, unchanged, unchanged)
    seq_rate = dual_weight / seq_len
    scaled_gates = grad_scale * gate_probs
    token_rate = jnp.sum(jnp.where(seq_hot, seq_rate[None, :], 0.0), axis=1)
    flat_weight = (scaled_gates * token_rate[:, None]).reshape(slot_count)
    slot_weight = lax.all_to_all(
        flat_weight[inverse].reshape(experts, capacity),
        "expert",
        split_axis=0,
        concat_axis=0,
        tiled=True,
    )
    weight_local = by_expert(slot_weight, groups)
    error_local = by_expert(sent_error, groups)
    scaled = (weight_local[:, :, None] * hidden).astype(jnp.bfloat16)
    grad_down = lax.psum_scatter(
        jnp.einsum("ern,erh->neh", error_local, scaled, preferred_element_type=jnp.float32),
        "dp",
        scatter_dimension=0,
        tiled=True,
    )
    return (combined.astype(jnp.bfloat16), seq_loss, dual_weight, grad_down)


LANES = 128
FLOAT = jnp.float32
HALF = jnp.bfloat16
INFO = 16
SEQ_LINE = 8


def swap(block, axis, mask):
    size = lax.axis_size(axis)
    return lax.ppermute(block, axis, [(s, s ^ mask) for s in range(size)])


def tree_sum(terms):
    while len(terms) > 1:
        rest = terms[len(terms) // 2 * 2 :]
        terms = [a + b for a, b in zip(terms[::2], terms[1::2])] + rest
    return terms[0]


def dot_nt(a, b):
    return lax.dot_general(a, b, (((1,), (1,)), ((), ())), preferred_element_type=FLOAT)


def dot_nn(a, b):
    return jnp.dot(a, b, preferred_element_type=FLOAT)


def cost():
    return pl.CostEstimate(flops=1, bytes_accessed=1, transcendentals=0)


def params(mib=60):
    return pltpu.CompilerParams(vmem_limit_bytes=mib << 20)


def col_to_row(col):
    count = col.shape[0]
    diagonal = lax.broadcasted_iota(jnp.int32, (count, LANES), 0) == lax.broadcasted_iota(
        jnp.int32, (count, LANES), 1
    )
    return jnp.sum(jnp.where(diagonal, col, 0.0), axis=0, keepdims=True)


def row_to_col(row, count):
    diagonal = lax.broadcasted_iota(jnp.int32, (count, LANES), 0) == lax.broadcasted_iota(
        jnp.int32, (count, LANES), 1
    )
    return jnp.sum(jnp.where(diagonal, row, 0.0), axis=1, keepdims=True)


def in_vmem(count=1):
    return [pl.BlockSpec(memory_space=pltpu.VMEM)] * count


def pack_tokens_kernel(experts, tokens, routes, logits, order, seq, out):
    top_k, rows = routes.shape
    names, slots, scores = routes[...], order[...], logits[...]
    picked = jnp.zeros((top_k, rows), FLOAT)
    for k in range(top_k):
        picked += jnp.where(slots == k, scores[k : k + 1, :], 0.0)
    raised = jnp.exp(picked)
    gates = raised / jnp.sum(raised, axis=0, keepdims=True)
    expert = lax.broadcasted_iota(jnp.int32, (experts, rows), 0)
    named = jnp.zeros((experts, rows), FLOAT)
    prob = jnp.zeros((experts, rows), FLOAT)
    for k in range(top_k):
        hit = names[k : k + 1, :] == expert
        named += jnp.where(hit, 1.0, 0.0)
        prob += jnp.where(hit, gates[k : k + 1, :], 0.0)
    before = lax.broadcasted_iota(jnp.int32, (rows, rows), 0) < lax.broadcasted_iota(
        jnp.int32, (rows, rows), 1
    )
    rank = dot_nn(named.astype(HALF), jnp.where(before, 1.0, 0.0).astype(HALF))
    place = jnp.where(named > 0.5, rank, -1.0).astype(HALF)
    number = jnp.broadcast_to(seq[...].astype(FLOAT), (experts, rows)).astype(HALF)
    out[0:rows, :] = tokens[...]
    out[rows:, :] = jnp.zeros((experts, out.shape[1]), HALF)
    for b, piece in enumerate([place, *exact_pieces(prob), number]):
        out[rows:, b * rows : (b + 1) * rows] = piece


def exact_pieces(value):
    pieces = []
    for _ in range(3):
        pieces.append(value.astype(HALF))
        value = value - pieces[-1].astype(FLOAT)
    return pieces


def pack_tokens(tokens, routes, route_logits, slot_order, seq_ids, experts):
    rows, width = tokens.shape
    return pl.pallas_call(
        functools.partial(pack_tokens_kernel, experts),
        in_specs=in_vmem(5),
        out_specs=pl.BlockSpec(memory_space=pltpu.VMEM),
        out_shape=jax.ShapeDtypeStruct((rows + experts, width), HALF),
        cost_estimate=cost(),
        compiler_params=params(),
        name="pack_tokens",
    )(tokens, routes.T, route_logits.T, slot_order.T, seq_ids.reshape(1, rows))


def hidden_kernel(experts, capacity, own, x_side, y_side, upper, lower, *refs):
    w_gate, w_up, out, joined, info, picked, probs, both, arrived = refs
    exp_dev, _, units = w_gate.shape
    for e in range(exp_dev):
        pltpu.make_async_copy(w_gate.at[e], both.at[e, :, pl.ds(0, units)], arrived.at[e]).start()
        pltpu.make_async_copy(w_up.at[e], both.at[e, :, pl.ds(units, units)], arrived.at[e]).start()
    joined[0 : upper.shape[0], :] = upper[...]
    joined[joined.shape[0] - lower.shape[0] :, :] = lower[...]
    tokens = [own, x_side, y_side, joined]
    total = len(tokens) * capacity
    rows = own.shape[0] - experts
    first = lax.axis_index("expert") * exp_dev
    slot = lax.broadcasted_iota(jnp.int32, (capacity, rows), 0).astype(FLOAT)
    lane = lax.broadcasted_iota(jnp.int32, (INFO, rows), 1).astype(FLOAT).astype(HALF)
    line = lax.broadcasted_iota(jnp.int32, (INFO, total), 0)
    expert = lax.broadcasted_iota(jnp.int32, (experts, rows), 0)
    info[...] = jnp.zeros(info.shape, FLOAT)
    origins = [[] for _ in range(exp_dev)]
    for m, block in enumerate(tokens):
        place, high, middle, low, number = (
            block[rows:, b * rows : (b + 1) * rows].astype(FLOAT) for b in range(5)
        )
        prob = high + middle + low
        info[SEQ_LINE + m : SEQ_LINE + m + 1, 0:rows] = number[0:1, :]
        picks = []
        for e in range(exp_dev):
            mine = expert == first + e
            own_place = jnp.sum(jnp.where(mine, place, 0.0), axis=0, keepdims=True)
            own_prob = jnp.sum(jnp.where(mine, prob, 0.0), axis=0, keepdims=True)
            pick = jnp.where(own_place == slot, 1.0, 0.0)
            probs[e, m * capacity : (m + 1) * capacity, :] = jnp.broadcast_to(
                jnp.sum(pick * own_prob, axis=1, keepdims=True), (capacity, LANES)
            )
            picks.append(pick.astype(HALF))
            origins[e].append(picks[-1])
        rows_m = dot_nn(jnp.concatenate(picks, axis=0), block[0:rows, :]).astype(HALF)
        for e in range(exp_dev):
            picked[e, m * capacity : (m + 1) * capacity, :] = rows_m[
                e * capacity : (e + 1) * capacity, :
            ]
    for e in range(exp_dev):
        origin = dot_nt(lane, jnp.concatenate(origins[e], axis=0))
        info[:, 0:total] = jnp.where(line == e, origin, info[:, 0:total])
    out[exp_dev * total :, :] = info[...].astype(HALF)

    def one_expert(e, carry):
        chosen = picked[e]
        pltpu.make_async_copy(both.at[e], both.at[e], arrived.at[e]).wait()
        product = dot_nn(chosen, both[e])
        gate, up = product[:, :units], product[:, units:]
        hidden = (gate / (1.0 + jnp.exp(-gate)) * up).astype(HALF)
        scaled = (probs[e, :, 0:1] * hidden.astype(FLOAT)).astype(HALF)
        out[pl.ds(pl.multiple_of(e * total, total), total), :] = scaled
        return carry

    lax.fori_loop(0, exp_dev, one_expert, 0)


def hidden_rows(tokens, w_gate, w_up, experts, capacity):
    lines, width = tokens[0].shape
    exp_dev, _, units = w_gate.shape
    total = 4 * capacity
    return pl.pallas_call(
        functools.partial(hidden_kernel, experts, capacity),
        in_specs=in_vmem(5) + [pl.BlockSpec(memory_space=pl.ANY)] * 2,
        out_specs=pl.BlockSpec(memory_space=pltpu.VMEM),
        out_shape=jax.ShapeDtypeStruct((exp_dev * total + INFO, units), HALF),
        scratch_shapes=[
            pltpu.VMEM((lines, width), HALF),
            pltpu.VMEM((INFO, units), FLOAT),
            pltpu.VMEM((exp_dev, total, width), HALF),
            pltpu.VMEM((exp_dev, total, LANES), FLOAT),
            pltpu.VMEM((exp_dev, width, 2 * units), HALF),
            pltpu.SemaphoreType.DMA((exp_dev,)),
        ],
        cost_estimate=cost(),
        compiler_params=params(),
        name="hidden_rows",
    )(*tokens, w_gate, w_up)


def row_places(info, e, total, capacity, rows, sources):
    shift = (lax.broadcasted_iota(jnp.int32, (1, total), 1) // capacity * rows).astype(FLOAT)
    token = lax.broadcasted_iota(jnp.int32, (sources * rows, total), 0).astype(FLOAT)
    return jnp.where(token == info[e : e + 1, 0:total] + shift, 1.0, 0.0).astype(HALF)


def project_kernel(exp_dev, capacity, rows, sources, slots, *refs):
    blocks, (w_down, seqs), refs = refs[:slots], refs[slots : slots + 2], refs[slots + 2 :]
    partials, (packed, outs, places, arrived) = refs[:sources], refs[sources:]
    units = w_down.shape[1] // exp_dev
    total = sources * capacity
    for s in range(slots):
        pltpu.make_async_copy(blocks[s], packed.at[s], arrived.at[s]).start()

    def one_slot(s, carry):
        pltpu.make_async_copy(packed.at[s], packed.at[s], arrived.at[s]).wait()
        info = packed[s, exp_dev * total :, :].astype(FLOAT)
        seqs[s] = info[SEQ_LINE:, 0:rows]
        for e in range(exp_dev):
            here = slice(e * total, (e + 1) * total)
            outs[:, here] = dot_nt(
                w_down[:, e * units : (e + 1) * units], packed[s, here, :]
            ).astype(HALF)
            places[:, here] = row_places(info, e, total, capacity, rows, sources)
        part = dot_nt(outs[...], places[...]).astype(HALF)
        for k in range(sources):
            partials[k][s] = part[:, k * rows : (k + 1) * rows]
        return carry

    lax.fori_loop(0, slots, one_slot, 0)


def project(blocks, w_down, exp_dev, capacity, rows, sources):
    slots = len(blocks)
    feats = w_down.shape[0]
    total = exp_dev * sources * capacity
    out = pl.pallas_call(
        functools.partial(project_kernel, exp_dev, capacity, rows, sources, slots),
        in_specs=[pl.BlockSpec(memory_space=pl.ANY)] * slots + in_vmem(1),
        out_specs=in_vmem(1 + sources),
        out_shape=[jax.ShapeDtypeStruct((slots, 8, rows), FLOAT)]
        + [jax.ShapeDtypeStruct((slots, feats, rows), HALF)] * sources,
        scratch_shapes=[
            pltpu.VMEM((slots,) + blocks[0].shape, HALF),
            pltpu.VMEM((feats, total), HALF),
            pltpu.VMEM((sources * rows, total), HALF),
            pltpu.SemaphoreType.DMA((slots,)),
        ],
        cost_estimate=cost(),
        compiler_params=params(),
        name="project",
    )(*blocks, w_down)
    return out[0], out[1:]


def spread_kernel(exp_dev, capacity, rows, sources, *refs):
    slots = len(refs) - 5
    blocks, (spread, packed, held, arrived, done) = refs[:slots], refs[slots:]
    units = packed.shape[2]
    total = sources * capacity
    for s in range(slots):
        pltpu.make_async_copy(blocks[s], packed.at[s], arrived.at[s]).start()

    def one_slot(s, carry):
        pltpu.make_async_copy(packed.at[s], packed.at[s], arrived.at[s]).wait()
        info = packed[s, exp_dev * total :, :].astype(FLOAT)
        for e in range(exp_dev):
            place = row_places(info, e, total, capacity, rows, sources)
            rows_e = packed[s, e * total : (e + 1) * total, :]
            held[s, :, e * units : (e + 1) * units] = dot_nn(place, rows_e).astype(HALF)
        pltpu.make_async_copy(held.at[s], spread.at[s], done.at[s]).start()
        return carry

    lax.fori_loop(0, slots, one_slot, 0)
    for s in range(slots):
        pltpu.make_async_copy(held.at[s], spread.at[s], done.at[s]).wait()


def spread_rows(blocks, exp_dev, capacity, rows, sources):
    slots = len(blocks)
    shape = (slots, sources * rows, exp_dev * blocks[0].shape[1])
    return pl.pallas_call(
        functools.partial(spread_kernel, exp_dev, capacity, rows, sources),
        in_specs=[pl.BlockSpec(memory_space=pl.ANY)] * slots,
        out_specs=pl.BlockSpec(memory_space=pl.ANY),
        out_shape=jax.ShapeDtypeStruct(shape, HALF),
        scratch_shapes=[
            pltpu.VMEM((slots,) + blocks[0].shape, HALF),
            pltpu.VMEM(shape, HALF),
            pltpu.SemaphoreType.DMA((slots,)),
            pltpu.SemaphoreType.DMA((slots,)),
        ],
        cost_estimate=cost(),
        compiler_params=params(),
        name="spread_rows",
    )(*blocks)


def residual_kernel(first, batches, sources, *refs):
    parts, refs = refs[: sources * len(batches)], refs[sources * len(batches) :]
    seqs, (targets, *refs) = refs[: len(batches)], refs[len(batches) :]
    if first:
        before, earlier, *refs = refs
    combined, errors, squares = refs
    feats, rows = targets.shape[1:]
    me = lax.axis_index("dp")
    number = lax.broadcasted_iota(jnp.int32, (NSEQ, rows), 0).astype(FLOAT)
    squared = jnp.zeros((NSEQ, rows), FLOAT)
    if first:
        for s in range(first):
            combined[me ^ s] = earlier[s]
    slot = 0
    for b, slots in enumerate(batches):
        here = parts[b * sources : (b + 1) * sources]
        for s in range(slots):
            total = tree_sum([part[s].astype(FLOAT) for part in here])
            combined[me ^ (first + slot) if first else slot] = total.astype(HALF)
            error = total - targets[me ^ (first + slot)].astype(FLOAT)
            errors[slot * feats : (slot + 1) * feats, :] = error.astype(HALF)
            per_token = jnp.sum(error * error, axis=0, keepdims=True)
            squared += jnp.where(seqs[b][s, 0:1, :] == number, per_token, 0.0)
            slot += 1
    sums = jnp.broadcast_to(col_to_row(jnp.sum(squared, axis=1, keepdims=True)), (8, LANES))
    squares[...] = sums + before[...] if first else sums


def residual(first, parts, seqs, targets, before, earlier):
    feats, rows = targets.shape[1:]
    batches = tuple(batch[0].shape[0] for batch in parts)
    sources = len(parts[0])
    slots = sum(batches)
    extra = [before, earlier] if first else []
    return pl.pallas_call(
        functools.partial(residual_kernel, first, batches, sources),
        in_specs=in_vmem((sources + 1) * len(batches) + 1 + len(extra)),
        out_specs=in_vmem(3),
        out_shape=[
            jax.ShapeDtypeStruct((first + slots, feats, rows), HALF),
            jax.ShapeDtypeStruct((slots * feats, rows), HALF),
            jax.ShapeDtypeStruct((8, LANES), FLOAT),
        ],
        cost_estimate=cost(),
        compiler_params=params(),
        name="residual",
    )(*[part for batch in parts for part in batch], *seqs, targets, *extra)


def gradient_kernel(scale, feat_width, exp_dev, terms, batches, parts, sources, *refs):
    squares, refs = refs[:terms], refs[terms:]
    count, groups = len(batches), sum(batches)
    spreads, seqs, refs = refs[:count], refs[count : 2 * count], refs[2 * count :]
    errors, refs = refs[: sources * len(parts)], refs[sources * len(parts) :]
    grad, seq_loss, dual_weight, held, error, lines, weighted, total, rates, arrived = refs
    feats = grad.shape[0]
    rows = error.shape[2] // sources
    slot = 0
    for b, slots in enumerate(parts):
        for s in range(slots):
            for m in range(sources):
                pltpu.make_async_copy(
                    errors[b * sources + m].at[pl.ds(s * feats, feats), :],
                    error.at[slot, :, pl.ds(m * rows, rows)],
                    arrived.at[0, slot],
                ).start()
            slot += 1
    slot = 0
    for seq, spread, slots in zip(seqs, spreads, batches):
        for s in range(slots):
            lines[slot] = seq[s]
            pltpu.make_async_copy(spread.at[s], held.at[slot], arrived.at[1, slot]).start()
            slot += 1
    number = lax.broadcasted_iota(jnp.int32, (NSEQ, rows), 0).astype(FLOAT)

    def count_slot(s, found):
        for m in range(sources):
            found += jnp.where(lines[s, m : m + 1, :] == number, 1.0, 0.0)
        return found

    found = lax.fori_loop(0, groups, count_slot, jnp.zeros((NSEQ, rows), FLOAT))
    seq_len = jnp.sum(found, axis=1, keepdims=True)
    summed = tree_sum([part[0:1, :] for part in squares])
    loss = row_to_col(summed, NSEQ) / (seq_len * feat_width)
    loss = jnp.broadcast_to(loss, (NSEQ, LANES))
    weight = dual_search_rows(loss)
    rates[...] = scale * (weight / seq_len)
    seq_loss[...] = col_to_row(loss)[:, 0:NSEQ]
    dual_weight[...] = col_to_row(weight)[:, 0:NSEQ]
    total[...] = jnp.zeros(total.shape, FLOAT)
    for s in range(groups):
        pltpu.make_async_copy(error.at[s], error.at[s], arrived.at[0, s]).wait()

    def weigh(s, turn):
        for m in range(sources):
            here = slice(m * rows, (m + 1) * rows)
            hit = jnp.where(lines[s, m : m + 1, :] == number, rates[...], 0.0)
            rate = jnp.sum(hit, axis=0, keepdims=True)
            weighted[turn, :, here] = (rate * error[s, :, here].astype(FLOAT)).astype(HALF)

    def add_slot(s, carry):
        pltpu.make_async_copy(held.at[s], held.at[s], arrived.at[1, s]).wait()
        product = dot_nn(weighted[s % 2], held[s])
        weigh(jnp.minimum(s + 1, groups - 1), (s + 1) % 2)
        total[...] += product
        return carry

    weigh(0, 0)
    lax.fori_loop(0, groups, add_slot, 0)
    units = grad.shape[2]
    for e in range(exp_dev):
        grad[:, e, :] = total[:, e * units : (e + 1) * units]


def dual_search_rows(loss):
    bound = jnp.sum(loss, axis=0, keepdims=True)

    def advance(step_index, bounds):
        lower, upper = bounds
        middle = 0.5 * (lower + upper)
        excess = jnp.maximum(loss - middle, 0.0)
        square_sum = jnp.sum(excess * excess, axis=0, keepdims=True)
        plain_sum = jnp.sum(excess, axis=0, keepdims=True)
        is_above = NSEQ * square_sum - radius_factor * plain_sum * plain_sum >= 0.0
        return (jnp.where(is_above, lower, middle), jnp.where(is_above, middle, upper))

    lower, upper = lax.fori_loop(
        0, BISECT_STEPS, advance, (-bound, bound), unroll=8
    )
    excess = jnp.maximum(loss - 0.5 * (lower + upper), 0.0)
    return excess / jnp.sum(excess, axis=0, keepdims=True)


def gradient(squares, spreads, seqs, errors, batches, parts, sources, scale, feat_width, exp_dev):
    rows = errors[0].shape[1]
    feats = errors[0].shape[0] // parts[0]
    group_rows, flat = spreads[0].shape[1:]
    units = flat // exp_dev
    groups = sum(batches)
    return pl.pallas_call(
        functools.partial(
            gradient_kernel, scale, feat_width, exp_dev, len(squares), batches, parts, sources
        ),
        in_specs=in_vmem(len(squares))
        + [pl.BlockSpec(memory_space=pl.ANY)] * len(spreads)
        + in_vmem(len(seqs))
        + [pl.BlockSpec(memory_space=pl.ANY)] * len(errors),
        out_specs=in_vmem(3),
        out_shape=[
            jax.ShapeDtypeStruct((feats, exp_dev, units), FLOAT),
            jax.ShapeDtypeStruct((1, NSEQ), FLOAT),
            jax.ShapeDtypeStruct((1, NSEQ), FLOAT),
        ],
        scratch_shapes=[
            pltpu.VMEM((groups, group_rows, flat), HALF),
            pltpu.VMEM((groups, feats, group_rows), HALF),
            pltpu.VMEM((groups, 8, rows), FLOAT),
            pltpu.VMEM((2, feats, group_rows), HALF),
            pltpu.VMEM((feats, flat), FLOAT),
            pltpu.VMEM((NSEQ, rows), FLOAT),
            pltpu.SemaphoreType.DMA((2, groups)),
        ],
        cost_estimate=cost(),
        compiler_params=params(),
        name="gradient",
    )(*squares, *spreads, *seqs, *errors)


def z_near(block):
    return {2: swap(block, "dp", 2), 4: swap(block, "dp", 4)}


def z_far(blocks):
    return swap(blocks[4], "dp", 2)


def feature_plan(tokens, targets, routes, route_logits, slot_order, seq_ids, w_gate, w_up, w_down):
    rows, feat_width = tokens.shape
    groups, sources = lax.axis_size("dp"), lax.axis_size("expert")
    exp_dev, _, units = w_gate.shape
    experts = exp_dev * sources
    capacity = rows * routes.shape[1] // experts
    feats = feat_width // groups
    scale = float(rows * groups * sources // 8)
    far = range(1, sources)
    tie = lax.optimization_barrier

    own_tokens = pack_tokens(tokens, routes, route_logits, slot_order, seq_ids, experts)
    x_tokens, y_tokens = swap(own_tokens, "expert", 1), swap(own_tokens, "expert", 2)
    half = (rows + experts + 31) // 32 * 16
    diagonal = [swap(y_tokens[:half], "expert", 1), swap(x_tokens[-half:], "expert", 2)]
    turned, own_tokens = tie((targets.T, own_tokens))
    own_targets = lax.all_to_all(
        turned.reshape(groups, feats, rows), "dp", split_axis=0, concat_axis=0, tiled=True
    )
    x_tokens, y_tokens, diagonal, own_targets = tie((x_tokens, y_tokens, diagonal, own_targets))
    packed = hidden_rows(
        [own_tokens, x_tokens, y_tokens, *diagonal], w_gate, w_up, experts, capacity
    )
    blocks = {0: packed, **z_near(packed)}
    flat_down = w_down.reshape(feats, exp_dev * units)

    def expert_parts(first, slots):
        for s in range(first, first + slots, 2):
            blocks[s + 1] = swap(blocks[s], "dp", 1)
        here = [blocks[s] for s in range(first, first + slots)]
        seq, parts = project(here, flat_down, exp_dev, capacity, rows, sources)
        parts = [parts[0]] + [swap(parts[m], "expert", m) for m in far]
        spread = spread_rows(here, exp_dev, capacity, rows, sources)
        parts, spread = tie((parts, spread))
        return spread, seq, parts

    def far_errors(error):
        return [swap(error, "expert", m) for m in far]

    batches = (2, groups - 4, 2)
    spread_0, seq_0, parts_0 = expert_parts(0, batches[0])
    mixed_0, error_0, squares_0 = residual(0, [parts_0], [seq_0], own_targets, None, None)
    errors_0 = far_errors(error_0)
    blocks, errors_0 = tie((blocks, errors_0))
    blocks[6] = z_far(blocks)

    spread_1, seq_1, parts_1 = expert_parts(2, batches[1])
    spread_2, seq_2, parts_2 = expert_parts(groups - 2, batches[2])
    mixed, error_1, squares = residual(
        2, [parts_1, parts_2], [seq_1, seq_2], own_targets, squares_0, mixed_0
    )
    far_squares = [swap(squares, "expert", m) for m in far]
    error_1, far_squares = tie((error_1, far_squares))
    errors_1 = far_errors(error_1)
    squares = tree_sum([squares] + far_squares)
    squares = squares + swap(squares, "dp", 1)
    all_squares = [squares] + [swap(squares, "dp", m) for m in range(2, groups, 2)]
    mixed = lax.all_to_all(mixed, "dp", split_axis=0, concat_axis=0, tiled=True)
    grad_down, seq_loss, dual_weight = gradient(
        all_squares,
        [spread_0, spread_1, spread_2],
        [seq_0, seq_1, seq_2],
        [error_0, *errors_0, error_1, *errors_1],
        batches,
        (batches[0], batches[1] + batches[2]),
        sources,
        scale,
        feat_width,
        exp_dev,
    )
    return (
        mixed.reshape(feat_width, rows).T,
        seq_loss.reshape(NSEQ),
        dual_weight.reshape(NSEQ),
        grad_down,
    )


def local(tokens, targets, routes, route_logits, slot_order, seq_ids, w_gate, w_up, w_down):
    args = (tokens, targets, routes, route_logits, slot_order, seq_ids, w_gate, w_up, w_down)
    groups, sources = lax.axis_size("dp"), lax.axis_size("expert")
    units = w_gate.shape[2]
    exp_dev = w_gate.shape[0]
    rows, feat_width = tokens.shape
    capacity = rows * routes.shape[1] // (exp_dev * sources)
    whole_tiles = (
        feat_width % (groups * LANES) == 0
        and rows == LANES
        and units % LANES == 0
        and sources * capacity <= units
        and capacity % 16 == 0
        and exp_dev <= SEQ_LINE
        and exp_dev * sources == INFO
        and sources == 4
        and groups == 8
    )
    return (feature_plan if whole_tiles else row_plan)(*args)


def solution(mesh):
    return jax.shard_map(
        local,
        mesh=mesh,
        in_specs=(
            P(("dp", "expert"), None),
            P(("dp", "expert"), None),
            P(("dp", "expert"), None),
            P(("dp", "expert"), None),
            P(("dp", "expert"), None),
            P(("dp", "expert")),
            P("expert", None, None),
            P("expert", None, None),
            P("dp", "expert", None),
        ),
        out_specs=(P(("dp", "expert"), None), P(), P(), P("dp", "expert", None)),
        check_vma=False,
    )
```

```python
import functools

import jax
import jax.numpy as jnp
from jax import lax
from jax.experimental import pallas as pl
from jax.experimental.pallas import tpu as pltpu
from jax.sharding import PartitionSpec as P

NSEQ = 64
BISECT_STEPS = 40


radius_factor = 2.0


def unchanged(single_value):
    return single_value


def dual_search(seq_loss, pair_total, one_total):
    sum_total = one_total(jnp.sum(seq_loss))

    def advance(step_index, bounds):
        lower, upper = bounds
        middle = 0.5 * (lower + upper)
        excess = jnp.maximum(seq_loss - middle, 0.0)
        square_sum, plain_sum = pair_total((jnp.sum(excess * excess), jnp.sum(excess)))
        is_above = NSEQ * square_sum - radius_factor * plain_sum * plain_sum >= 0.0
        return (jnp.where(is_above, lower, middle), jnp.where(is_above, middle, upper))

    lower, upper = lax.fori_loop(0, BISECT_STEPS, advance, (-sum_total, sum_total))
    excess = jnp.maximum(seq_loss - 0.5 * (lower + upper), 0.0)
    return excess / one_total(jnp.sum(excess))


def route_gates(route_logits, slot_order):
    top_k = slot_order.shape[1]
    columns = lax.broadcasted_iota(jnp.int32, (1, 1, top_k), 2)
    picked = jnp.sum(
        jnp.where(slot_order[:, :, None] == columns, route_logits[:, None, :], 0.0), axis=2
    )
    raised = jnp.exp(picked)
    return raised / jnp.sum(raised, axis=1, keepdims=True)


def by_expert(blocks, groups):
    exp_dev = blocks.shape[0] // groups
    tail_shape = blocks.shape[1:]
    split_view = blocks.reshape((groups, exp_dev) + tail_shape)
    moved_view = jnp.swapaxes(split_view, 0, 1)
    return moved_view.reshape((exp_dev, groups * tail_shape[0]) + tail_shape[1:])


def by_source(local_rows, groups):
    exp_dev = local_rows.shape[0]
    capacity = local_rows.shape[1] // groups
    tail_shape = local_rows.shape[2:]
    split_view = local_rows.reshape((exp_dev, groups, capacity) + tail_shape)
    return jnp.swapaxes(split_view, 0, 1).reshape((exp_dev * groups, capacity) + tail_shape)


def row_plan(tokens, targets, routes, route_logits, slot_order, seq_ids, w_gate, w_up, w_down):
    tok_rows, feat_width = tokens.shape
    top_k = routes.shape[1]
    groups = lax.axis_size("expert")
    exp_dev = w_gate.shape[0]
    experts = exp_dev * groups
    slot_count = tok_rows * top_k
    capacity = slot_count // experts
    grad_scale = float(tok_rows * lax.axis_size("dp") * groups // 8)
    flat_route = routes.reshape(slot_count)
    expert_hot = (flat_route[:, None] == lax.broadcasted_iota(jnp.int32, (1, experts), 1)).astype(
        jnp.int32
    )
    slot_rank = jnp.sum((jnp.cumsum(expert_hot, axis=0) - 1) * expert_hot, axis=1)
    slot_index = flat_route * capacity + slot_rank
    inverse = (
        jnp.zeros((slot_count,), jnp.int32).at[slot_index].set(lax.iota(jnp.int32, slot_count))
    )
    source_row = inverse // top_k
    gate_probs = route_gates(route_logits, slot_order)
    send_rows = tokens[source_row].reshape(experts, capacity, feat_width)
    arrived = lax.all_to_all(send_rows, "expert", split_axis=0, concat_axis=0, tiled=True)
    local_rows = by_expert(arrived, groups)
    gate_proj = jnp.einsum("erd,edh->erh", local_rows, w_gate, preferred_element_type=jnp.float32)
    up_proj = jnp.einsum("erd,edh->erh", local_rows, w_up, preferred_element_type=jnp.float32)
    hidden = (jax.nn.silu(gate_proj) * up_proj).astype(jnp.bfloat16)
    expert_out = jnp.einsum(
        "erh,neh->ern",
        hidden,
        lax.all_gather(w_down, "dp", axis=0, tiled=True),
        preferred_element_type=jnp.float32,
    ).astype(jnp.bfloat16)
    returned = lax.all_to_all(
        by_source(expert_out, groups), "expert", split_axis=0, concat_axis=0, tiled=True
    )
    per_slot = returned.reshape(slot_count, feat_width)[slot_index].reshape(
        tok_rows, top_k, feat_width
    )
    combined = jnp.sum(gate_probs[:, :, None] * per_slot.astype(jnp.float32), axis=1)
    error = combined - targets.astype(jnp.float32)
    error_low = error.astype(jnp.bfloat16)
    sent_error = lax.all_to_all(
        error_low[source_row].reshape(experts, capacity, feat_width),
        "expert",
        split_axis=0,
        concat_axis=0,
        tiled=True,
    )
    seq_hot = seq_ids[:, None] == lax.broadcasted_iota(jnp.int32, (1, NSEQ), 1)
    partial_sq = jnp.sum(jnp.where(seq_hot, jnp.sum(error * error, axis=1)[:, None], 0.0), axis=0)
    counts = jnp.sum(seq_hot.astype(jnp.float32), axis=0)
    seq_sq, seq_len = lax.psum((partial_sq, counts), ("dp", "expert"))
    seq_loss = seq_sq / (seq_len * feat_width)
    dual_weight = dual_search(seq_loss, unchanged, unchanged)
    seq_rate = dual_weight / seq_len
    scaled_gates = grad_scale * gate_probs
    token_rate = jnp.sum(jnp.where(seq_hot, seq_rate[None, :], 0.0), axis=1)
    flat_weight = (scaled_gates * token_rate[:, None]).reshape(slot_count)
    slot_weight = lax.all_to_all(
        flat_weight[inverse].reshape(experts, capacity),
        "expert",
        split_axis=0,
        concat_axis=0,
        tiled=True,
    )
    weight_local = by_expert(slot_weight, groups)
    error_local = by_expert(sent_error, groups)
    scaled = (weight_local[:, :, None] * hidden).astype(jnp.bfloat16)
    grad_down = lax.psum_scatter(
        jnp.einsum("ern,erh->neh", error_local, scaled, preferred_element_type=jnp.float32),
        "dp",
        scatter_dimension=0,
        tiled=True,
    )
    return (combined.astype(jnp.bfloat16), seq_loss, dual_weight, grad_down)


LANES = 128
FLOAT = jnp.float32
HALF = jnp.bfloat16
INFO = 16
SEQ_LINE = 8


def swap(block, axis, mask):
    size = lax.axis_size(axis)
    return lax.ppermute(block, axis, [(s, s ^ mask) for s in range(size)])


def tree_sum(terms):
    while len(terms) > 1:
        rest = terms[len(terms) // 2 * 2 :]
        terms = [a + b for a, b in zip(terms[::2], terms[1::2])] + rest
    return terms[0]


def dot_nt(a, b):
    return lax.dot_general(a, b, (((1,), (1,)), ((), ())), preferred_element_type=FLOAT)


def dot_nn(a, b):
    return jnp.dot(a, b, preferred_element_type=FLOAT)


def cost():
    return pl.CostEstimate(flops=1, bytes_accessed=1, transcendentals=0)


def params(mib=60):
    return pltpu.CompilerParams(vmem_limit_bytes=mib << 20)


def col_to_row(col):
    count = col.shape[0]
    diagonal = lax.broadcasted_iota(jnp.int32, (count, LANES), 0) == lax.broadcasted_iota(
        jnp.int32, (count, LANES), 1
    )
    return jnp.sum(jnp.where(diagonal, col, 0.0), axis=0, keepdims=True)


def row_to_col(row, count):
    diagonal = lax.broadcasted_iota(jnp.int32, (count, LANES), 0) == lax.broadcasted_iota(
        jnp.int32, (count, LANES), 1
    )
    return jnp.sum(jnp.where(diagonal, row, 0.0), axis=1, keepdims=True)


def in_vmem(count=1):
    return [pl.BlockSpec(memory_space=pltpu.VMEM)] * count


def pack_tokens_kernel(experts, tokens, routes, logits, order, seq, out):
    top_k, rows = routes.shape
    names, slots, scores = routes[...], order[...], logits[...]
    picked = jnp.zeros((top_k, rows), FLOAT)
    for k in range(top_k):
        picked += jnp.where(slots == k, scores[k : k + 1, :], 0.0)
    raised = jnp.exp(picked)
    gates = raised / jnp.sum(raised, axis=0, keepdims=True)
    expert = lax.broadcasted_iota(jnp.int32, (experts, rows), 0)
    named = jnp.zeros((experts, rows), FLOAT)
    prob = jnp.zeros((experts, rows), FLOAT)
    for k in range(top_k):
        hit = names[k : k + 1, :] == expert
        named += jnp.where(hit, 1.0, 0.0)
        prob += jnp.where(hit, gates[k : k + 1, :], 0.0)
    before = lax.broadcasted_iota(jnp.int32, (rows, rows), 0) < lax.broadcasted_iota(
        jnp.int32, (rows, rows), 1
    )
    rank = dot_nn(named.astype(HALF), jnp.where(before, 1.0, 0.0).astype(HALF))
    place = jnp.where(named > 0.5, rank, -1.0).astype(HALF)
    number = jnp.broadcast_to(seq[...].astype(FLOAT), (experts, rows)).astype(HALF)
    out[0:rows, :] = tokens[...]
    out[rows:, :] = jnp.zeros((experts, out.shape[1]), HALF)
    for b, piece in enumerate([place, *exact_pieces(prob), number]):
        out[rows:, b * rows : (b + 1) * rows] = piece


def exact_pieces(value):
    pieces = []
    for _ in range(3):
        pieces.append(value.astype(HALF))
        value = value - pieces[-1].astype(FLOAT)
    return pieces


def pack_tokens(tokens, routes, route_logits, slot_order, seq_ids, experts):
    rows, width = tokens.shape
    return pl.pallas_call(
        functools.partial(pack_tokens_kernel, experts),
        in_specs=in_vmem(5),
        out_specs=pl.BlockSpec(memory_space=pltpu.VMEM),
        out_shape=jax.ShapeDtypeStruct((rows + experts, width), HALF),
        cost_estimate=cost(),
        compiler_params=params(),
        name="pack_tokens",
    )(tokens, routes.T, route_logits.T, slot_order.T, seq_ids.reshape(1, rows))


def hidden_kernel(experts, capacity, own, x_side, y_side, upper, lower, *refs):
    w_gate, w_up, out, joined, info, picked, probs, both, arrived = refs
    exp_dev, _, units = w_gate.shape
    for e in range(exp_dev):
        pltpu.make_async_copy(w_gate.at[e], both.at[e, :, pl.ds(0, units)], arrived.at[e]).start()
        pltpu.make_async_copy(w_up.at[e], both.at[e, :, pl.ds(units, units)], arrived.at[e]).start()
    joined[0 : upper.shape[0], :] = upper[...]
    joined[joined.shape[0] - lower.shape[0] :, :] = lower[...]
    tokens = [own, x_side, y_side, joined]
    total = len(tokens) * capacity
    rows = own.shape[0] - experts
    first = lax.axis_index("expert") * exp_dev
    slot = lax.broadcasted_iota(jnp.int32, (capacity, rows), 0).astype(FLOAT)
    lane = lax.broadcasted_iota(jnp.int32, (INFO, rows), 1).astype(FLOAT).astype(HALF)
    line = lax.broadcasted_iota(jnp.int32, (INFO, total), 0)
    expert = lax.broadcasted_iota(jnp.int32, (experts, rows), 0)
    info[...] = jnp.zeros(info.shape, FLOAT)
    origins = [[] for _ in range(exp_dev)]
    for m, block in enumerate(tokens):
        place, high, middle, low, number = (
            block[rows:, b * rows : (b + 1) * rows].astype(FLOAT) for b in range(5)
        )
        prob = high + middle + low
        info[SEQ_LINE + m : SEQ_LINE + m + 1, 0:rows] = number[0:1, :]
        picks = []
        for e in range(exp_dev):
            mine = expert == first + e
            own_place = jnp.sum(jnp.where(mine, place, 0.0), axis=0, keepdims=True)
            own_prob = jnp.sum(jnp.where(mine, prob, 0.0), axis=0, keepdims=True)
            pick = jnp.where(own_place == slot, 1.0, 0.0)
            probs[e, m * capacity : (m + 1) * capacity, :] = jnp.broadcast_to(
                jnp.sum(pick * own_prob, axis=1, keepdims=True), (capacity, LANES)
            )
            picks.append(pick.astype(HALF))
            origins[e].append(picks[-1])
        rows_m = dot_nn(jnp.concatenate(picks, axis=0), block[0:rows, :]).astype(HALF)
        for e in range(exp_dev):
            picked[e, m * capacity : (m + 1) * capacity, :] = rows_m[
                e * capacity : (e + 1) * capacity, :
            ]
    for e in range(exp_dev):
        origin = dot_nt(lane, jnp.concatenate(origins[e], axis=0))
        info[:, 0:total] = jnp.where(line == e, origin, info[:, 0:total])
    out[exp_dev * total :, :] = info[...].astype(HALF)

    def one_expert(e, carry):
        chosen = picked[e]
        pltpu.make_async_copy(both.at[e], both.at[e], arrived.at[e]).wait()
        product = dot_nn(chosen, both[e])
        gate, up = product[:, :units], product[:, units:]
        hidden = (gate / (1.0 + jnp.exp(-gate)) * up).astype(HALF)
        scaled = (probs[e, :, 0:1] * hidden.astype(FLOAT)).astype(HALF)
        out[pl.ds(pl.multiple_of(e * total, total), total), :] = scaled
        return carry

    lax.fori_loop(0, exp_dev, one_expert, 0)


def hidden_rows(tokens, w_gate, w_up, experts, capacity):
    lines, width = tokens[0].shape
    exp_dev, _, units = w_gate.shape
    total = 4 * capacity
    return pl.pallas_call(
        functools.partial(hidden_kernel, experts, capacity),
        in_specs=in_vmem(5) + [pl.BlockSpec(memory_space=pl.ANY)] * 2,
        out_specs=pl.BlockSpec(memory_space=pltpu.VMEM),
        out_shape=jax.ShapeDtypeStruct((exp_dev * total + INFO, units), HALF),
        scratch_shapes=[
            pltpu.VMEM((lines, width), HALF),
            pltpu.VMEM((INFO, units), FLOAT),
            pltpu.VMEM((exp_dev, total, width), HALF),
            pltpu.VMEM((exp_dev, total, LANES), FLOAT),
            pltpu.VMEM((exp_dev, width, 2 * units), HALF),
            pltpu.SemaphoreType.DMA((exp_dev,)),
        ],
        cost_estimate=cost(),
        compiler_params=params(36),
        name="hidden_rows",
    )(*tokens, w_gate, w_up)


def row_places(info, e, total, capacity, rows, sources):
    shift = (lax.broadcasted_iota(jnp.int32, (1, total), 1) // capacity * rows).astype(FLOAT)
    token = lax.broadcasted_iota(jnp.int32, (sources * rows, total), 0).astype(FLOAT)
    return jnp.where(token == info[e : e + 1, 0:total] + shift, 1.0, 0.0).astype(HALF)


def project_kernel(exp_dev, capacity, rows, sources, slots, *refs):
    blocks, (w_down, seqs), refs = refs[:slots], refs[slots : slots + 2], refs[slots + 2 :]
    partials, (packed, outs, places, arrived) = refs[:sources], refs[sources:]
    units = w_down.shape[1] // exp_dev
    total = sources * capacity
    fetches = [
        pltpu.make_async_copy(blocks[s], packed.at[s], arrived.at[s]) for s in range(slots)
    ]
    for copy in fetches:
        copy.start()

    def one_slot(s, carry):
        pltpu.make_async_copy(packed.at[s], packed.at[s], arrived.at[s]).wait()
        info = packed[s, exp_dev * total :, :].astype(FLOAT)
        seqs[s] = info[SEQ_LINE:, 0:rows]
        for e in range(exp_dev):
            here = slice(e * total, (e + 1) * total)
            outs[:, here] = dot_nt(
                w_down[:, e * units : (e + 1) * units], packed[s, here, :]
            ).astype(HALF)
            places[:, here] = row_places(info, e, total, capacity, rows, sources)
        part = dot_nt(outs[...], places[...]).astype(HALF)
        for k in range(sources):
            partials[k][s] = part[:, k * rows : (k + 1) * rows]
        return carry

    lax.fori_loop(0, slots, one_slot, 0)


def project(blocks, w_down, exp_dev, capacity, rows, sources):
    slots = len(blocks)
    feats = w_down.shape[0]
    total = exp_dev * sources * capacity
    out = pl.pallas_call(
        functools.partial(project_kernel, exp_dev, capacity, rows, sources, slots),
        in_specs=[pl.BlockSpec(memory_space=pl.ANY)] * slots + in_vmem(1),
        out_specs=in_vmem(1 + sources),
        out_shape=[jax.ShapeDtypeStruct((slots, 8, rows), FLOAT)]
        + [jax.ShapeDtypeStruct((slots, feats, rows), HALF)] * sources,
        scratch_shapes=[
            pltpu.VMEM((slots,) + blocks[0].shape, HALF),
            pltpu.VMEM((feats, total), HALF),
            pltpu.VMEM((sources * rows, total), HALF),
            pltpu.SemaphoreType.DMA((slots,)),
        ],
        cost_estimate=cost(),
        compiler_params=params(16),
        name="project",
    )(*blocks, w_down)
    return out[0], out[1:]


def spread_kernel(exp_dev, capacity, rows, sources, *refs):
    slots = len(refs) - 5
    blocks, (spread, packed, held, arrived, done) = refs[:slots], refs[slots:]
    units = packed.shape[2]
    total = sources * capacity
    fetches = [
        pltpu.make_async_copy(blocks[s], packed.at[s], arrived.at[s]) for s in range(slots)
    ]
    for copy in fetches:
        copy.start()

    def one_slot(s, carry):
        pltpu.make_async_copy(packed.at[s], packed.at[s], arrived.at[s]).wait()
        info = packed[s, exp_dev * total :, :].astype(FLOAT)
        for e in range(exp_dev):
            place = row_places(info, e, total, capacity, rows, sources)
            rows_e = packed[s, e * total : (e + 1) * total, :]
            held[s, :, e * units : (e + 1) * units] = dot_nn(place, rows_e).astype(HALF)
        pltpu.make_async_copy(held.at[s], spread.at[s], done.at[s]).start()
        return carry

    lax.fori_loop(0, slots, one_slot, 0)
    for s in range(slots):
        pltpu.make_async_copy(held.at[s], spread.at[s], done.at[s]).wait()


def spread_rows(blocks, exp_dev, capacity, rows, sources):
    slots = len(blocks)
    shape = (slots, sources * rows, exp_dev * blocks[0].shape[1])
    return pl.pallas_call(
        functools.partial(spread_kernel, exp_dev, capacity, rows, sources),
        in_specs=[pl.BlockSpec(memory_space=pl.ANY)] * slots,
        out_specs=pl.BlockSpec(memory_space=pl.ANY),
        out_shape=jax.ShapeDtypeStruct(shape, HALF),
        scratch_shapes=[
            pltpu.VMEM((slots,) + blocks[0].shape, HALF),
            pltpu.VMEM(shape, HALF),
            pltpu.SemaphoreType.DMA((slots,)),
            pltpu.SemaphoreType.DMA((slots,)),
        ],
        cost_estimate=cost(),
        compiler_params=params(24),
        name="spread_rows",
    )(*blocks)


def residual_kernel(first, batches, sources, *refs):
    parts, refs = refs[: sources * len(batches)], refs[sources * len(batches) :]
    seqs, (targets, *refs) = refs[: len(batches)], refs[len(batches) :]
    if first:
        before, refs = refs[0], refs[1:]
    combined, errors, squares = refs[-3:]
    feats, rows = targets.shape[1:]
    me = lax.axis_index("dp")
    number = lax.broadcasted_iota(jnp.int32, (NSEQ, rows), 0).astype(FLOAT)
    squared = jnp.zeros((NSEQ, rows), FLOAT)
    slot = 0
    for block in refs[:-3]:
        for s in range(block.shape[0]):
            combined[me ^ slot] = block[s]
            slot += 1
    ordered = len(refs) > 3
    slot = 0
    for b, slots in enumerate(batches):
        here = parts[b * sources : (b + 1) * sources]
        for s in range(slots):
            total = tree_sum([part[s].astype(FLOAT) for part in here])
            combined[me ^ (first + slot) if ordered else slot] = total.astype(HALF)
            error = total - targets[me ^ (first + slot)].astype(FLOAT)
            errors[slot * feats : (slot + 1) * feats, :] = error.astype(HALF)
            per_token = jnp.sum(error * error, axis=0, keepdims=True)
            squared += jnp.where(seqs[b][s, 0:1, :] == number, per_token, 0.0)
            slot += 1
    sums = jnp.broadcast_to(col_to_row(jnp.sum(squared, axis=1, keepdims=True)), (8, LANES))
    squares[...] = sums + before[...] if first else sums


def residual(first, parts, seqs, targets, before, earlier):
    feats, rows = targets.shape[1:]
    batches = tuple(batch[0].shape[0] for batch in parts)
    sources = len(parts[0])
    slots = sum(batches)
    extra = [before, *earlier] if first else []
    return pl.pallas_call(
        functools.partial(residual_kernel, first, batches, sources),
        in_specs=in_vmem((sources + 1) * len(batches) + 1 + len(extra)),
        out_specs=in_vmem(3),
        out_shape=[
            jax.ShapeDtypeStruct((slots + first * (len(earlier) > 0), feats, rows), HALF),
            jax.ShapeDtypeStruct((slots * feats, rows), HALF),
            jax.ShapeDtypeStruct((8, LANES), FLOAT),
        ],
        cost_estimate=cost(),
        compiler_params=params(16),
        name="residual",
    )(*[part for batch in parts for part in batch], *seqs, targets, *extra)


def gradient_kernel(scale, feat_width, exp_dev, terms, batches, parts, sources, *refs):
    squares, refs = refs[:terms], refs[terms:]
    count, groups = len(batches), sum(batches)
    spreads, seqs, refs = refs[:count], refs[count : 2 * count], refs[2 * count :]
    errors, refs = refs[: sources * len(parts)], refs[sources * len(parts) :]
    grad, seq_loss, dual_weight, held, error, lines, weighted, total, rates, arrived = refs
    feats = grad.shape[0]
    rows = error.shape[2] // sources
    slot = 0
    for b, slots in enumerate(parts):
        for s in range(slots):
            for m in range(sources):
                pltpu.make_async_copy(
                    errors[b * sources + m].at[pl.ds(s * feats, feats), :],
                    error.at[slot, :, pl.ds(m * rows, rows)],
                    arrived.at[0, slot],
                ).start()
            slot += 1
    slot = 0
    for seq, spread, slots in zip(seqs, spreads, batches):
        for s in range(slots):
            lines[slot] = seq[s]
            pltpu.make_async_copy(
                spread.at[s],
                held.at[slot // 2, pl.ds(slot % 2 * sources * rows, sources * rows)],
                arrived.at[1, slot // 2],
            ).start()
            slot += 1
    number = lax.broadcasted_iota(jnp.int32, (NSEQ, rows), 0).astype(FLOAT)

    def count_slot(s, found):
        for m in range(sources):
            found += jnp.where(lines[s, m : m + 1, :] == number, 1.0, 0.0)
        return found

    found = lax.fori_loop(0, groups, count_slot, jnp.zeros((NSEQ, rows), FLOAT))
    seq_len = jnp.sum(found, axis=1, keepdims=True)
    summed = tree_sum([part[0:1, :] for part in squares])
    loss = row_to_col(summed, NSEQ) / (seq_len * feat_width)
    loss = jnp.broadcast_to(loss, (NSEQ, LANES))
    weight = dual_search_rows(loss)
    rates[...] = scale * (weight / seq_len)
    seq_loss[...] = col_to_row(loss)[:, 0:NSEQ]
    dual_weight[...] = col_to_row(weight)[:, 0:NSEQ]
    total[...] = jnp.zeros(total.shape, FLOAT)
    for s in range(groups):
        pltpu.make_async_copy(error.at[s], error.at[s], arrived.at[0, s]).wait()

    def weigh(pair, turn):
        for k in range(2):
            for m in range(sources):
                here = slice(m * rows, (m + 1) * rows)
                there = slice((k * sources + m) * rows, (k * sources + m + 1) * rows)
                hit = jnp.where(lines[2 * pair + k, m : m + 1, :] == number, rates[...], 0.0)
                rate = jnp.sum(hit, axis=0, keepdims=True)
                weighted[turn, :, there] = (
                    rate * error[2 * pair + k, :, here].astype(FLOAT)
                ).astype(HALF)

    def add_pair(pair, carry):
        pltpu.make_async_copy(held.at[pair], held.at[pair], arrived.at[1, pair]).wait()
        product = dot_nn(weighted[pair % 2], held[pair])
        weigh(jnp.minimum(pair + 1, groups // 2 - 1), (pair + 1) % 2)
        total[...] += product
        return carry

    weigh(0, 0)
    lax.fori_loop(0, groups // 2, add_pair, 0)
    units = grad.shape[2]
    for e in range(exp_dev):
        grad[:, e, :] = total[:, e * units : (e + 1) * units]


def dual_search_rows(loss):
    bound = jnp.sum(loss, axis=0, keepdims=True)

    def advance(step_index, bounds):
        lower, upper = bounds
        middle = 0.5 * (lower + upper)
        excess = jnp.maximum(loss - middle, 0.0)
        square_sum = jnp.sum(excess * excess, axis=0, keepdims=True)
        plain_sum = jnp.sum(excess, axis=0, keepdims=True)
        is_above = NSEQ * square_sum - radius_factor * plain_sum * plain_sum >= 0.0
        return (jnp.where(is_above, lower, middle), jnp.where(is_above, middle, upper))

    lower, upper = lax.fori_loop(
        0, BISECT_STEPS, advance, (-bound, bound), unroll=8
    )
    excess = jnp.maximum(loss - 0.5 * (lower + upper), 0.0)
    return excess / jnp.sum(excess, axis=0, keepdims=True)


def gradient(squares, spreads, seqs, errors, batches, parts, sources, scale, feat_width, exp_dev):
    rows = errors[0].shape[1]
    feats = errors[0].shape[0] // parts[0]
    group_rows, flat = spreads[0].shape[1:]
    units = flat // exp_dev
    groups = sum(batches)
    return pl.pallas_call(
        functools.partial(
            gradient_kernel, scale, feat_width, exp_dev, len(squares), batches, parts, sources
        ),
        in_specs=in_vmem(len(squares))
        + [pl.BlockSpec(memory_space=pl.ANY)] * len(spreads)
        + in_vmem(len(seqs))
        + [pl.BlockSpec(memory_space=pl.ANY)] * len(errors),
        out_specs=in_vmem(3),
        out_shape=[
            jax.ShapeDtypeStruct((feats, exp_dev, units), FLOAT),
            jax.ShapeDtypeStruct((1, NSEQ), FLOAT),
            jax.ShapeDtypeStruct((1, NSEQ), FLOAT),
        ],
        scratch_shapes=[
            pltpu.VMEM((groups // 2, 2 * group_rows, flat), HALF),
            pltpu.VMEM((groups, feats, group_rows), HALF),
            pltpu.VMEM((groups, 8, rows), FLOAT),
            pltpu.VMEM((2, feats, 2 * group_rows), HALF),
            pltpu.VMEM((feats, flat), FLOAT),
            pltpu.VMEM((NSEQ, rows), FLOAT),
            pltpu.SemaphoreType.DMA((2, groups)),
        ],
        cost_estimate=cost(),
        compiler_params=params(),
        name="gradient",
    )(*squares, *spreads, *seqs, *errors)


def z_near(block):
    return {2: swap(block, "dp", 2), 4: swap(block, "dp", 4)}


def z_far(blocks):
    return swap(blocks[4], "dp", 2)


def feature_plan(tokens, targets, routes, route_logits, slot_order, seq_ids, w_gate, w_up, w_down):
    rows, feat_width = tokens.shape
    groups, sources = lax.axis_size("dp"), lax.axis_size("expert")
    exp_dev, _, units = w_gate.shape
    experts = exp_dev * sources
    capacity = rows * routes.shape[1] // experts
    feats = feat_width // groups
    scale = float(rows * groups * sources // 8)
    far = range(1, sources)
    tie = lax.optimization_barrier

    own_tokens = pack_tokens(tokens, routes, route_logits, slot_order, seq_ids, experts)
    x_tokens, y_tokens = swap(own_tokens, "expert", 1), swap(own_tokens, "expert", 2)
    half = (rows + experts + 31) // 32 * 16
    diagonal = [swap(y_tokens[:half], "expert", 1), swap(x_tokens[-half:], "expert", 2)]
    turned, own_tokens = tie((targets.T, own_tokens))
    own_targets = lax.all_to_all(
        turned.reshape(groups, feats, rows), "dp", split_axis=0, concat_axis=0, tiled=True
    )
    x_tokens, y_tokens, diagonal, own_targets = tie((x_tokens, y_tokens, diagonal, own_targets))
    packed = hidden_rows(
        [own_tokens, x_tokens, y_tokens, *diagonal], w_gate, w_up, experts, capacity
    )
    blocks = {0: packed, **z_near(packed)}
    flat_down = w_down.reshape(feats, exp_dev * units)

    def expert_parts(first, slots):
        for s in range(first, first + slots, 2):
            blocks[s + 1] = swap(blocks[s], "dp", 1)
        here = [blocks[s] for s in range(first, first + slots)]
        seq, parts = project(here, flat_down, exp_dev, capacity, rows, sources)
        parts = [parts[0]] + [swap(parts[m], "expert", m) for m in far]
        spread = spread_rows(here, exp_dev, capacity, rows, sources)
        parts, spread = tie((parts, spread))
        return spread, seq, parts

    def far_errors(error):
        return [swap(error, "expert", m) for m in far]

    batches = (2, groups - 4, 2)
    spread_0, seq_0, parts_0 = expert_parts(0, batches[0])
    mixed_0, error_0, squares = residual(0, [parts_0], [seq_0], own_targets, None, [])
    errors_0 = far_errors(error_0)
    blocks, errors_0 = tie((blocks, errors_0))
    blocks[6] = z_far(blocks)

    spread_1, seq_1, parts_1 = expert_parts(2, batches[1])
    blocks[6], parts_1 = tie((blocks[6], parts_1))
    spread_2, seq_2, parts_2 = expert_parts(groups - 2, batches[2])
    mixed, error_1, squares = residual(
        2, [parts_1, parts_2], [seq_1, seq_2], own_targets, squares, [mixed_0]
    )
    far_squares = [swap(squares, "expert", m) for m in far]
    error_1, far_squares = tie((error_1, far_squares))
    errors_1 = far_errors(error_1)
    squares = tree_sum([squares] + far_squares)
    squares = squares + swap(squares, "dp", 1)
    all_squares = [squares] + [swap(squares, "dp", m) for m in range(2, groups, 2)]
    mixed = lax.all_to_all(mixed, "dp", split_axis=0, concat_axis=0, tiled=True)
    grad_down, seq_loss, dual_weight = gradient(
        all_squares,
        [spread_0, spread_1, spread_2],
        [seq_0, seq_1, seq_2],
        [error_0, *errors_0, error_1, *errors_1],
        batches,
        (batches[0], batches[1] + batches[2]),
        sources,
        scale,
        feat_width,
        exp_dev,
    )
    return (
        mixed.reshape(feat_width, rows).T,
        seq_loss.reshape(NSEQ),
        dual_weight.reshape(NSEQ),
        grad_down,
    )


def local(tokens, targets, routes, route_logits, slot_order, seq_ids, w_gate, w_up, w_down):
    args = (tokens, targets, routes, route_logits, slot_order, seq_ids, w_gate, w_up, w_down)
    groups, sources = lax.axis_size("dp"), lax.axis_size("expert")
    units = w_gate.shape[2]
    exp_dev = w_gate.shape[0]
    rows, feat_width = tokens.shape
    capacity = rows * routes.shape[1] // (exp_dev * sources)
    whole_tiles = (
        feat_width % (groups * LANES) == 0
        and rows == LANES
        and units % LANES == 0
        and sources * capacity <= units
        and capacity % 16 == 0
        and exp_dev <= SEQ_LINE
        and exp_dev * sources == INFO
        and sources == 4
        and groups == 8
    )
    return (feature_plan if whole_tiles else row_plan)(*args)


def solution(mesh):
    return jax.shard_map(
        local,
        mesh=mesh,
        in_specs=(
            P(("dp", "expert"), None),
            P(("dp", "expert"), None),
            P(("dp", "expert"), None),
            P(("dp", "expert"), None),
            P(("dp", "expert"), None),
            P(("dp", "expert")),
            P("expert", None, None),
            P("expert", None, None),
            P("dp", "expert", None),
        ),
        out_specs=(P(("dp", "expert"), None), P(), P(), P("dp", "expert", None)),
        check_vma=False,
    )
```

```python
import functools

import jax
import jax.numpy as jnp
from jax import lax
from jax.experimental import pallas as pl
from jax.experimental.pallas import tpu as pltpu
from jax.sharding import PartitionSpec as P

NSEQ = 64
BISECT_STEPS = 40


radius_factor = 2.0


def unchanged(single_value):
    return single_value


def dual_search(seq_loss, pair_total, one_total):
    sum_total = one_total(jnp.sum(seq_loss))

    def advance(step_index, bounds):
        lower, upper = bounds
        middle = 0.5 * (lower + upper)
        excess = jnp.maximum(seq_loss - middle, 0.0)
        square_sum, plain_sum = pair_total((jnp.sum(excess * excess), jnp.sum(excess)))
        is_above = NSEQ * square_sum - radius_factor * plain_sum * plain_sum >= 0.0
        return (jnp.where(is_above, lower, middle), jnp.where(is_above, middle, upper))

    lower, upper = lax.fori_loop(0, BISECT_STEPS, advance, (-sum_total, sum_total))
    excess = jnp.maximum(seq_loss - 0.5 * (lower + upper), 0.0)
    return excess / one_total(jnp.sum(excess))


def route_gates(route_logits, slot_order):
    top_k = slot_order.shape[1]
    columns = lax.broadcasted_iota(jnp.int32, (1, 1, top_k), 2)
    picked = jnp.sum(
        jnp.where(slot_order[:, :, None] == columns, route_logits[:, None, :], 0.0), axis=2
    )
    raised = jnp.exp(picked)
    return raised / jnp.sum(raised, axis=1, keepdims=True)


def by_expert(blocks, groups):
    exp_dev = blocks.shape[0] // groups
    tail_shape = blocks.shape[1:]
    split_view = blocks.reshape((groups, exp_dev) + tail_shape)
    moved_view = jnp.swapaxes(split_view, 0, 1)
    return moved_view.reshape((exp_dev, groups * tail_shape[0]) + tail_shape[1:])


def by_source(local_rows, groups):
    exp_dev = local_rows.shape[0]
    capacity = local_rows.shape[1] // groups
    tail_shape = local_rows.shape[2:]
    split_view = local_rows.reshape((exp_dev, groups, capacity) + tail_shape)
    return jnp.swapaxes(split_view, 0, 1).reshape((exp_dev * groups, capacity) + tail_shape)


def row_plan(tokens, targets, routes, route_logits, slot_order, seq_ids, w_gate, w_up, w_down):
    tok_rows, feat_width = tokens.shape
    top_k = routes.shape[1]
    groups = lax.axis_size("expert")
    exp_dev = w_gate.shape[0]
    experts = exp_dev * groups
    slot_count = tok_rows * top_k
    capacity = slot_count // experts
    grad_scale = float(tok_rows * lax.axis_size("dp") * groups // 8)
    flat_route = routes.reshape(slot_count)
    expert_hot = (flat_route[:, None] == lax.broadcasted_iota(jnp.int32, (1, experts), 1)).astype(
        jnp.int32
    )
    slot_rank = jnp.sum((jnp.cumsum(expert_hot, axis=0) - 1) * expert_hot, axis=1)
    slot_index = flat_route * capacity + slot_rank
    inverse = (
        jnp.zeros((slot_count,), jnp.int32).at[slot_index].set(lax.iota(jnp.int32, slot_count))
    )
    source_row = inverse // top_k
    gate_probs = route_gates(route_logits, slot_order)
    send_rows = tokens[source_row].reshape(experts, capacity, feat_width)
    arrived = lax.all_to_all(send_rows, "expert", split_axis=0, concat_axis=0, tiled=True)
    local_rows = by_expert(arrived, groups)
    gate_proj = jnp.einsum("erd,edh->erh", local_rows, w_gate, preferred_element_type=jnp.float32)
    up_proj = jnp.einsum("erd,edh->erh", local_rows, w_up, preferred_element_type=jnp.float32)
    hidden = (jax.nn.silu(gate_proj) * up_proj).astype(jnp.bfloat16)
    expert_out = jnp.einsum(
        "erh,neh->ern",
        hidden,
        lax.all_gather(w_down, "dp", axis=0, tiled=True),
        preferred_element_type=jnp.float32,
    ).astype(jnp.bfloat16)
    returned = lax.all_to_all(
        by_source(expert_out, groups), "expert", split_axis=0, concat_axis=0, tiled=True
    )
    per_slot = returned.reshape(slot_count, feat_width)[slot_index].reshape(
        tok_rows, top_k, feat_width
    )
    combined = jnp.sum(gate_probs[:, :, None] * per_slot.astype(jnp.float32), axis=1)
    error = combined - targets.astype(jnp.float32)
    error_low = error.astype(jnp.bfloat16)
    sent_error = lax.all_to_all(
        error_low[source_row].reshape(experts, capacity, feat_width),
        "expert",
        split_axis=0,
        concat_axis=0,
        tiled=True,
    )
    seq_hot = seq_ids[:, None] == lax.broadcasted_iota(jnp.int32, (1, NSEQ), 1)
    partial_sq = jnp.sum(jnp.where(seq_hot, jnp.sum(error * error, axis=1)[:, None], 0.0), axis=0)
    counts = jnp.sum(seq_hot.astype(jnp.float32), axis=0)
    seq_sq, seq_len = lax.psum((partial_sq, counts), ("dp", "expert"))
    seq_loss = seq_sq / (seq_len * feat_width)
    dual_weight = dual_search(seq_loss, unchanged, unchanged)
    seq_rate = dual_weight / seq_len
    scaled_gates = grad_scale * gate_probs
    token_rate = jnp.sum(jnp.where(seq_hot, seq_rate[None, :], 0.0), axis=1)
    flat_weight = (scaled_gates * token_rate[:, None]).reshape(slot_count)
    slot_weight = lax.all_to_all(
        flat_weight[inverse].reshape(experts, capacity),
        "expert",
        split_axis=0,
        concat_axis=0,
        tiled=True,
    )
    weight_local = by_expert(slot_weight, groups)
    error_local = by_expert(sent_error, groups)
    scaled = (weight_local[:, :, None] * hidden).astype(jnp.bfloat16)
    grad_down = lax.psum_scatter(
        jnp.einsum("ern,erh->neh", error_local, scaled, preferred_element_type=jnp.float32),
        "dp",
        scatter_dimension=0,
        tiled=True,
    )
    return (combined.astype(jnp.bfloat16), seq_loss, dual_weight, grad_down)


LANES = 128
FLOAT = jnp.float32
HALF = jnp.bfloat16
INFO = 16
SEQ_LINE = 8


def swap(block, axis, mask):
    size = lax.axis_size(axis)
    return lax.ppermute(block, axis, [(s, s ^ mask) for s in range(size)])


def tree_sum(terms):
    while len(terms) > 1:
        rest = terms[len(terms) // 2 * 2 :]
        terms = [a + b for a, b in zip(terms[::2], terms[1::2])] + rest
    return terms[0]


def dot_nt(a, b):
    return lax.dot_general(a, b, (((1,), (1,)), ((), ())), preferred_element_type=FLOAT)


def dot_nn(a, b):
    return jnp.dot(a, b, preferred_element_type=FLOAT)


def cost():
    return pl.CostEstimate(flops=1, bytes_accessed=1, transcendentals=0)


def params(mib=60):
    return pltpu.CompilerParams(vmem_limit_bytes=mib << 20)


def col_to_row(col):
    count = col.shape[0]
    diagonal = lax.broadcasted_iota(jnp.int32, (count, LANES), 0) == lax.broadcasted_iota(
        jnp.int32, (count, LANES), 1
    )
    return jnp.sum(jnp.where(diagonal, col, 0.0), axis=0, keepdims=True)


def row_to_col(row, count):
    diagonal = lax.broadcasted_iota(jnp.int32, (count, LANES), 0) == lax.broadcasted_iota(
        jnp.int32, (count, LANES), 1
    )
    return jnp.sum(jnp.where(diagonal, row, 0.0), axis=1, keepdims=True)


def in_vmem(count=1):
    return [pl.BlockSpec(memory_space=pltpu.VMEM)] * count


def pack_tokens_kernel(experts, tokens, routes, logits, order, seq, out):
    top_k, rows = routes.shape
    names, slots, scores = routes[...], order[...], logits[...]
    picked = jnp.zeros((top_k, rows), FLOAT)
    for k in range(top_k):
        picked += jnp.where(slots == k, scores[k : k + 1, :], 0.0)
    raised = jnp.exp(picked)
    gates = raised / jnp.sum(raised, axis=0, keepdims=True)
    expert = lax.broadcasted_iota(jnp.int32, (experts, rows), 0)
    named = jnp.zeros((experts, rows), FLOAT)
    prob = jnp.zeros((experts, rows), FLOAT)
    for k in range(top_k):
        hit = names[k : k + 1, :] == expert
        named += jnp.where(hit, 1.0, 0.0)
        prob += jnp.where(hit, gates[k : k + 1, :], 0.0)
    before = lax.broadcasted_iota(jnp.int32, (rows, rows), 0) < lax.broadcasted_iota(
        jnp.int32, (rows, rows), 1
    )
    rank = dot_nn(named.astype(HALF), jnp.where(before, 1.0, 0.0).astype(HALF))
    place = jnp.where(named > 0.5, rank, -1.0).astype(HALF)
    number = jnp.broadcast_to(seq[...].astype(FLOAT), (experts, rows)).astype(HALF)
    out[0:rows, :] = tokens[...]
    out[rows:, :] = jnp.zeros((experts, out.shape[1]), HALF)
    for b, piece in enumerate([place, *exact_pieces(prob), number]):
        out[rows:, b * rows : (b + 1) * rows] = piece


def exact_pieces(value):
    pieces = []
    for _ in range(3):
        pieces.append(value.astype(HALF))
        value = value - pieces[-1].astype(FLOAT)
    return pieces


def pack_tokens(tokens, routes, route_logits, slot_order, seq_ids, experts):
    rows, width = tokens.shape
    return pl.pallas_call(
        functools.partial(pack_tokens_kernel, experts),
        in_specs=in_vmem(5),
        out_specs=pl.BlockSpec(memory_space=pltpu.VMEM),
        out_shape=jax.ShapeDtypeStruct((rows + experts, width), HALF),
        cost_estimate=cost(),
        compiler_params=params(),
        name="pack_tokens",
    )(tokens, routes.T, route_logits.T, slot_order.T, seq_ids.reshape(1, rows))


def hidden_kernel(experts, capacity, own, x_side, y_side, upper, lower, *refs):
    w_gate, w_up, out, joined, info, picked, probs, both, arrived = refs
    exp_dev, _, units = w_gate.shape
    for e in range(exp_dev):
        pltpu.make_async_copy(w_gate.at[e], both.at[e, :, pl.ds(0, units)], arrived.at[e]).start()
        pltpu.make_async_copy(w_up.at[e], both.at[e, :, pl.ds(units, units)], arrived.at[e]).start()
    joined[0 : upper.shape[0], :] = upper[...]
    joined[joined.shape[0] - lower.shape[0] :, :] = lower[...]
    tokens = [own, x_side, y_side, joined]
    total = len(tokens) * capacity
    rows = own.shape[0] - experts
    first = lax.axis_index("expert") * exp_dev
    slot = lax.broadcasted_iota(jnp.int32, (capacity, rows), 0).astype(FLOAT)
    lane = lax.broadcasted_iota(jnp.int32, (INFO, rows), 1).astype(FLOAT).astype(HALF)
    line = lax.broadcasted_iota(jnp.int32, (INFO, total), 0)
    expert = lax.broadcasted_iota(jnp.int32, (experts, rows), 0)
    info[...] = jnp.zeros(info.shape, FLOAT)
    origins = [[] for _ in range(exp_dev)]
    for m, block in enumerate(tokens):
        place, high, middle, low, number = (
            block[rows:, b * rows : (b + 1) * rows].astype(FLOAT) for b in range(5)
        )
        prob = high + middle + low
        info[SEQ_LINE + m : SEQ_LINE + m + 1, 0:rows] = number[0:1, :]
        picks = []
        for e in range(exp_dev):
            mine = expert == first + e
            own_place = jnp.sum(jnp.where(mine, place, 0.0), axis=0, keepdims=True)
            own_prob = jnp.sum(jnp.where(mine, prob, 0.0), axis=0, keepdims=True)
            pick = jnp.where(own_place == slot, 1.0, 0.0)
            probs[e, m * capacity : (m + 1) * capacity, :] = jnp.broadcast_to(
                jnp.sum(pick * own_prob, axis=1, keepdims=True), (capacity, LANES)
            )
            picks.append(pick.astype(HALF))
            origins[e].append(picks[-1])
        rows_m = dot_nn(jnp.concatenate(picks, axis=0), block[0:rows, :]).astype(HALF)
        for e in range(exp_dev):
            picked[e, m * capacity : (m + 1) * capacity, :] = rows_m[
                e * capacity : (e + 1) * capacity, :
            ]
    for e in range(exp_dev):
        origin = dot_nt(lane, jnp.concatenate(origins[e], axis=0))
        info[:, 0:total] = jnp.where(line == e, origin, info[:, 0:total])
    out[exp_dev * total :, :] = info[...].astype(HALF)

    def one_expert(e, carry):
        chosen = picked[e]
        pltpu.make_async_copy(both.at[e], both.at[e], arrived.at[e]).wait()
        product = dot_nn(chosen, both[e])
        gate, up = product[:, :units], product[:, units:]
        hidden = (gate / (1.0 + jnp.exp(-gate)) * up).astype(HALF)
        scaled = (probs[e, :, 0:1] * hidden.astype(FLOAT)).astype(HALF)
        out[pl.ds(pl.multiple_of(e * total, total), total), :] = scaled
        return carry

    lax.fori_loop(0, exp_dev, one_expert, 0)


def hidden_rows(tokens, w_gate, w_up, experts, capacity):
    lines, width = tokens[0].shape
    exp_dev, _, units = w_gate.shape
    total = 4 * capacity
    return pl.pallas_call(
        functools.partial(hidden_kernel, experts, capacity),
        in_specs=in_vmem(5) + [pl.BlockSpec(memory_space=pl.ANY)] * 2,
        out_specs=pl.BlockSpec(memory_space=pltpu.VMEM),
        out_shape=jax.ShapeDtypeStruct((exp_dev * total + INFO, units), HALF),
        scratch_shapes=[
            pltpu.VMEM((lines, width), HALF),
            pltpu.VMEM((INFO, units), FLOAT),
            pltpu.VMEM((exp_dev, total, width), HALF),
            pltpu.VMEM((exp_dev, total, LANES), FLOAT),
            pltpu.VMEM((exp_dev, width, 2 * units), HALF),
            pltpu.SemaphoreType.DMA((exp_dev,)),
        ],
        cost_estimate=cost(),
        compiler_params=params(56),
        name="hidden_rows",
    )(*tokens, w_gate, w_up)


def row_places(info, e, total, capacity, rows, sources):
    shift = (lax.broadcasted_iota(jnp.int32, (1, total), 1) // capacity * rows).astype(FLOAT)
    token = lax.broadcasted_iota(jnp.int32, (sources * rows, total), 0).astype(FLOAT)
    return jnp.where(token == info[e : e + 1, 0:total] + shift, 1.0, 0.0).astype(HALF)


def project_kernel(exp_dev, capacity, rows, sources, slots, *refs):
    blocks, (w_down, seqs), refs = refs[:slots], refs[slots : slots + 2], refs[slots + 2 :]
    partials, (packed, outs, places, arrived) = refs[:sources], refs[sources:]
    units = w_down.shape[1] // exp_dev
    total = sources * capacity
    fetches = [
        pltpu.make_async_copy(blocks[s], packed.at[s], arrived.at[s]) for s in range(slots)
    ]
    for copy in fetches:
        copy.start()

    def one_slot(s, carry):
        pltpu.make_async_copy(packed.at[s], packed.at[s], arrived.at[s]).wait()
        info = packed[s, exp_dev * total :, :].astype(FLOAT)
        seqs[s] = info[SEQ_LINE:, 0:rows]
        for e in range(exp_dev):
            here = slice(e * total, (e + 1) * total)
            outs[:, here] = dot_nt(
                w_down[:, e * units : (e + 1) * units], packed[s, here, :]
            ).astype(HALF)
            places[:, here] = row_places(info, e, total, capacity, rows, sources)
        part = dot_nt(outs[...], places[...]).astype(HALF)
        for k in range(sources):
            partials[k][s] = part[:, k * rows : (k + 1) * rows]
        return carry

    lax.fori_loop(0, slots, one_slot, 0)


def project(blocks, w_down, exp_dev, capacity, rows, sources):
    slots = len(blocks)
    feats = w_down.shape[0]
    total = exp_dev * sources * capacity
    out = pl.pallas_call(
        functools.partial(project_kernel, exp_dev, capacity, rows, sources, slots),
        in_specs=[pl.BlockSpec(memory_space=pl.ANY)] * slots + in_vmem(1),
        out_specs=in_vmem(1 + sources),
        out_shape=[jax.ShapeDtypeStruct((slots, 8, rows), FLOAT)]
        + [jax.ShapeDtypeStruct((slots, feats, rows), HALF)] * sources,
        scratch_shapes=[
            pltpu.VMEM((slots,) + blocks[0].shape, HALF),
            pltpu.VMEM((feats, total), HALF),
            pltpu.VMEM((sources * rows, total), HALF),
            pltpu.SemaphoreType.DMA((slots,)),
        ],
        cost_estimate=cost(),
        compiler_params=params(16),
        name="project",
    )(*blocks, w_down)
    return out[0], out[1:]


def spread_kernel(exp_dev, capacity, rows, sources, *refs):
    slots = len(refs) - 5
    blocks, (spread, packed, held, arrived, done) = refs[:slots], refs[slots:]
    units = packed.shape[2]
    total = sources * capacity
    fetches = [
        pltpu.make_async_copy(blocks[s], packed.at[s], arrived.at[s]) for s in range(slots)
    ]
    for copy in fetches:
        copy.start()

    def one_slot(s, carry):
        pltpu.make_async_copy(packed.at[s], packed.at[s], arrived.at[s]).wait()
        info = packed[s, exp_dev * total :, :].astype(FLOAT)
        for e in range(exp_dev):
            place = row_places(info, e, total, capacity, rows, sources)
            rows_e = packed[s, e * total : (e + 1) * total, :]
            held[s, :, e * units : (e + 1) * units] = dot_nn(place, rows_e).astype(HALF)
        pltpu.make_async_copy(held.at[s], spread.at[s], done.at[s]).start()
        return carry

    lax.fori_loop(0, slots, one_slot, 0)
    for s in range(slots):
        pltpu.make_async_copy(held.at[s], spread.at[s], done.at[s]).wait()


def spread_rows(blocks, exp_dev, capacity, rows, sources):
    slots = len(blocks)
    shape = (slots, sources * rows, exp_dev * blocks[0].shape[1])
    return pl.pallas_call(
        functools.partial(spread_kernel, exp_dev, capacity, rows, sources),
        in_specs=[pl.BlockSpec(memory_space=pl.ANY)] * slots,
        out_specs=pl.BlockSpec(memory_space=pl.ANY),
        out_shape=jax.ShapeDtypeStruct(shape, HALF),
        scratch_shapes=[
            pltpu.VMEM((slots,) + blocks[0].shape, HALF),
            pltpu.VMEM(shape, HALF),
            pltpu.SemaphoreType.DMA((slots,)),
            pltpu.SemaphoreType.DMA((slots,)),
        ],
        cost_estimate=cost(),
        compiler_params=params(24),
        name="spread_rows",
    )(*blocks)


def residual_kernel(first, batches, sources, *refs):
    parts, refs = refs[: sources * len(batches)], refs[sources * len(batches) :]
    seqs, (targets, *refs) = refs[: len(batches)], refs[len(batches) :]
    if first:
        before, refs = refs[0], refs[1:]
    combined, errors, squares = refs[-3:]
    feats, rows = targets.shape[1:]
    me = lax.axis_index("dp")
    number = lax.broadcasted_iota(jnp.int32, (NSEQ, rows), 0).astype(FLOAT)
    squared = jnp.zeros((NSEQ, rows), FLOAT)
    slot = 0
    for block in refs[:-3]:
        for s in range(block.shape[0]):
            combined[me ^ slot] = block[s]
            slot += 1
    ordered = len(refs) > 3
    slot = 0
    for b, slots in enumerate(batches):
        here = parts[b * sources : (b + 1) * sources]
        for s in range(slots):
            total = tree_sum([part[s].astype(FLOAT) for part in here])
            combined[me ^ (first + slot) if ordered else slot] = total.astype(HALF)
            error = total - targets[me ^ (first + slot)].astype(FLOAT)
            errors[slot * feats : (slot + 1) * feats, :] = error.astype(HALF)
            per_token = jnp.sum(error * error, axis=0, keepdims=True)
            squared += jnp.where(seqs[b][s, 0:1, :] == number, per_token, 0.0)
            slot += 1
    sums = jnp.broadcast_to(col_to_row(jnp.sum(squared, axis=1, keepdims=True)), (8, LANES))
    squares[...] = sums + before[...] if first else sums


def residual(first, parts, seqs, targets, before, earlier):
    feats, rows = targets.shape[1:]
    batches = tuple(batch[0].shape[0] for batch in parts)
    sources = len(parts[0])
    slots = sum(batches)
    extra = [before, *earlier] if first else []
    return pl.pallas_call(
        functools.partial(residual_kernel, first, batches, sources),
        in_specs=in_vmem((sources + 1) * len(batches) + 1 + len(extra)),
        out_specs=in_vmem(3),
        out_shape=[
            jax.ShapeDtypeStruct((slots + first * (len(earlier) > 0), feats, rows), HALF),
            jax.ShapeDtypeStruct((slots * feats, rows), HALF),
            jax.ShapeDtypeStruct((8, LANES), FLOAT),
        ],
        cost_estimate=cost(),
        compiler_params=params(16),
        name="residual",
    )(*[part for batch in parts for part in batch], *seqs, targets, *extra)


def gradient_kernel(scale, feat_width, exp_dev, terms, batches, parts, sources, *refs):
    squares, refs = refs[:terms], refs[terms:]
    count, groups = len(batches), sum(batches)
    spreads, seqs, refs = refs[:count], refs[count : 2 * count], refs[2 * count :]
    errors, refs = refs[: sources * len(parts)], refs[sources * len(parts) :]
    grad, seq_loss, dual_weight, held, error, lines, weighted, total, rates, arrived = refs
    feats = grad.shape[0]
    rows = error.shape[2] // sources
    slot = 0
    for b, slots in enumerate(parts):
        for s in range(slots):
            for m in range(sources):
                pltpu.make_async_copy(
                    errors[b * sources + m].at[pl.ds(s * feats, feats), :],
                    error.at[slot, :, pl.ds(m * rows, rows)],
                    arrived.at[0, slot],
                ).start()
            slot += 1
    slot = 0
    for seq, spread, slots in zip(seqs, spreads, batches):
        for s in range(slots):
            lines[slot] = seq[s]
            pltpu.make_async_copy(
                spread.at[s],
                held.at[slot // 2, pl.ds(slot % 2 * sources * rows, sources * rows)],
                arrived.at[1, slot // 2],
            ).start()
            slot += 1
    number = lax.broadcasted_iota(jnp.int32, (NSEQ, rows), 0).astype(FLOAT)

    def count_slot(s, found):
        for m in range(sources):
            found += jnp.where(lines[s, m : m + 1, :] == number, 1.0, 0.0)
        return found

    found = lax.fori_loop(0, groups, count_slot, jnp.zeros((NSEQ, rows), FLOAT))
    seq_len = jnp.sum(found, axis=1, keepdims=True)
    summed = tree_sum([part[0:1, :] for part in squares])
    loss = row_to_col(summed, NSEQ) / (seq_len * feat_width)
    loss = jnp.broadcast_to(loss, (NSEQ, LANES))
    weight = dual_search_rows(loss)
    rates[...] = scale * (weight / seq_len)
    seq_loss[...] = col_to_row(loss)[:, 0:NSEQ]
    dual_weight[...] = col_to_row(weight)[:, 0:NSEQ]
    total[...] = jnp.zeros(total.shape, FLOAT)
    for s in range(groups):
        pltpu.make_async_copy(error.at[s], error.at[s], arrived.at[0, s]).wait()

    def weigh(pair, turn):
        for k in range(2):
            for m in range(sources):
                here = slice(m * rows, (m + 1) * rows)
                there = slice((k * sources + m) * rows, (k * sources + m + 1) * rows)
                hit = jnp.where(lines[2 * pair + k, m : m + 1, :] == number, rates[...], 0.0)
                rate = jnp.sum(hit, axis=0, keepdims=True)
                weighted[turn, :, there] = (
                    rate * error[2 * pair + k, :, here].astype(FLOAT)
                ).astype(HALF)

    def add_pair(pair, carry):
        pltpu.make_async_copy(held.at[pair], held.at[pair], arrived.at[1, pair]).wait()
        product = dot_nn(weighted[pair % 2], held[pair])
        weigh(jnp.minimum(pair + 1, groups // 2 - 1), (pair + 1) % 2)
        total[...] += product
        return carry

    weigh(0, 0)
    lax.fori_loop(0, groups // 2, add_pair, 0)
    units = grad.shape[2]
    for e in range(exp_dev):
        grad[:, e, :] = total[:, e * units : (e + 1) * units]


def dual_search_rows(loss):
    bound = jnp.sum(loss, axis=0, keepdims=True)

    def advance(step_index, bounds):
        lower, upper = bounds
        middle = 0.5 * (lower + upper)
        excess = jnp.maximum(loss - middle, 0.0)
        square_sum = jnp.sum(excess * excess, axis=0, keepdims=True)
        plain_sum = jnp.sum(excess, axis=0, keepdims=True)
        is_above = NSEQ * square_sum - radius_factor * plain_sum * plain_sum >= 0.0
        return (jnp.where(is_above, lower, middle), jnp.where(is_above, middle, upper))

    lower, upper = lax.fori_loop(
        0, BISECT_STEPS, advance, (-bound, bound), unroll=True
    )
    excess = jnp.maximum(loss - 0.5 * (lower + upper), 0.0)
    return excess / jnp.sum(excess, axis=0, keepdims=True)


def gradient(squares, spreads, seqs, errors, batches, parts, sources, scale, feat_width, exp_dev):
    rows = errors[0].shape[1]
    feats = errors[0].shape[0] // parts[0]
    group_rows, flat = spreads[0].shape[1:]
    units = flat // exp_dev
    groups = sum(batches)
    return pl.pallas_call(
        functools.partial(
            gradient_kernel, scale, feat_width, exp_dev, len(squares), batches, parts, sources
        ),
        in_specs=in_vmem(len(squares))
        + [pl.BlockSpec(memory_space=pl.ANY)] * len(spreads)
        + in_vmem(len(seqs))
        + [pl.BlockSpec(memory_space=pl.ANY)] * len(errors),
        out_specs=in_vmem(3),
        out_shape=[
            jax.ShapeDtypeStruct((feats, exp_dev, units), FLOAT),
            jax.ShapeDtypeStruct((1, NSEQ), FLOAT),
            jax.ShapeDtypeStruct((1, NSEQ), FLOAT),
        ],
        scratch_shapes=[
            pltpu.VMEM((groups // 2, 2 * group_rows, flat), HALF),
            pltpu.VMEM((groups, feats, group_rows), HALF),
            pltpu.VMEM((groups, 8, rows), FLOAT),
            pltpu.VMEM((2, feats, 2 * group_rows), HALF),
            pltpu.VMEM((feats, flat), FLOAT),
            pltpu.VMEM((NSEQ, rows), FLOAT),
            pltpu.SemaphoreType.DMA((2, groups)),
        ],
        cost_estimate=cost(),
        compiler_params=params(),
        name="gradient",
    )(*squares, *spreads, *seqs, *errors)


def z_near(block):
    return {2: swap(block, "dp", 2), 4: swap(block, "dp", 4)}


def z_far(blocks):
    return swap(blocks[4], "dp", 2)


def feature_plan(tokens, targets, routes, route_logits, slot_order, seq_ids, w_gate, w_up, w_down):
    rows, feat_width = tokens.shape
    groups, sources = lax.axis_size("dp"), lax.axis_size("expert")
    exp_dev, _, units = w_gate.shape
    experts = exp_dev * sources
    capacity = rows * routes.shape[1] // experts
    feats = feat_width // groups
    scale = float(rows * groups * sources // 8)
    far = range(1, sources)
    tie = lax.optimization_barrier

    own_tokens = pack_tokens(tokens, routes, route_logits, slot_order, seq_ids, experts)
    x_tokens, y_tokens = swap(own_tokens, "expert", 1), swap(own_tokens, "expert", 2)
    half = (rows + experts + 31) // 32 * 16
    diagonal = [swap(y_tokens[:half], "expert", 1), swap(x_tokens[-half:], "expert", 2)]
    turned, own_tokens = tie((targets.T, own_tokens))
    own_targets = lax.all_to_all(
        turned.reshape(groups, feats, rows), "dp", split_axis=0, concat_axis=0, tiled=True
    )
    x_tokens, y_tokens, diagonal, own_targets = tie((x_tokens, y_tokens, diagonal, own_targets))
    packed = hidden_rows(
        [own_tokens, x_tokens, y_tokens, *diagonal], w_gate, w_up, experts, capacity
    )
    blocks = {0: packed, **z_near(packed)}
    flat_down = w_down.reshape(feats, exp_dev * units)

    def expert_parts(first, slots):
        for s in range(first, first + slots, 2):
            blocks[s + 1] = swap(blocks[s], "dp", 1)
        here = [blocks[s] for s in range(first, first + slots)]
        seq, parts = project(here, flat_down, exp_dev, capacity, rows, sources)
        parts = [parts[0]] + [swap(parts[m], "expert", m) for m in far]
        spread = spread_rows(here, exp_dev, capacity, rows, sources)
        parts, spread = tie((parts, spread))
        return spread, seq, parts

    def far_errors(error):
        return [swap(error, "expert", m) for m in far]

    batches = (2, groups - 4, 2)
    spread_0, seq_0, parts_0 = expert_parts(0, batches[0])
    mixed_0, error_0, squares = residual(0, [parts_0], [seq_0], own_targets, None, [])
    errors_0 = far_errors(error_0)
    blocks, errors_0 = tie((blocks, errors_0))
    blocks[6] = z_far(blocks)

    spread_1, seq_1, parts_1 = expert_parts(2, batches[1])
    blocks[6], parts_1 = tie((blocks[6], parts_1))
    spread_2, seq_2, parts_2 = expert_parts(groups - 2, batches[2])
    mixed, error_1, squares = residual(
        2, [parts_1, parts_2], [seq_1, seq_2], own_targets, squares, [mixed_0]
    )
    far_squares = [swap(squares, "expert", m) for m in far]
    error_1, far_squares = tie((error_1, far_squares))
    errors_1 = far_errors(error_1)
    squares = tree_sum([squares] + far_squares)
    squares = squares + swap(squares, "dp", 1)
    all_squares = [squares] + [swap(squares, "dp", m) for m in range(2, groups, 2)]
    mixed = lax.all_to_all(mixed, "dp", split_axis=0, concat_axis=0, tiled=True)
    grad_down, seq_loss, dual_weight = gradient(
        all_squares,
        [spread_0, spread_1, spread_2],
        [seq_0, seq_1, seq_2],
        [error_0, *errors_0, error_1, *errors_1],
        batches,
        (batches[0], batches[1] + batches[2]),
        sources,
        scale,
        feat_width,
        exp_dev,
    )
    return (
        mixed.reshape(feat_width, rows).T,
        seq_loss.reshape(NSEQ),
        dual_weight.reshape(NSEQ),
        grad_down,
    )


def local(tokens, targets, routes, route_logits, slot_order, seq_ids, w_gate, w_up, w_down):
    args = (tokens, targets, routes, route_logits, slot_order, seq_ids, w_gate, w_up, w_down)
    groups, sources = lax.axis_size("dp"), lax.axis_size("expert")
    units = w_gate.shape[2]
    exp_dev = w_gate.shape[0]
    rows, feat_width = tokens.shape
    capacity = rows * routes.shape[1] // (exp_dev * sources)
    whole_tiles = (
        feat_width % (groups * LANES) == 0
        and rows == LANES
        and units % LANES == 0
        and sources * capacity <= units
        and capacity % 16 == 0
        and exp_dev <= SEQ_LINE
        and exp_dev * sources == INFO
        and sources == 4
        and groups == 8
    )
    return (feature_plan if whole_tiles else row_plan)(*args)


def solution(mesh):
    return jax.shard_map(
        local,
        mesh=mesh,
        in_specs=(
            P(("dp", "expert"), None),
            P(("dp", "expert"), None),
            P(("dp", "expert"), None),
            P(("dp", "expert"), None),
            P(("dp", "expert"), None),
            P(("dp", "expert")),
            P("expert", None, None),
            P("expert", None, None),
            P("dp", "expert", None),
        ),
        out_specs=(P(("dp", "expert"), None), P(), P(), P("dp", "expert", None)),
        check_vma=False,
    )
```

```python
import functools

import jax
import jax.numpy as jnp
from jax import lax
from jax.experimental import pallas as pl
from jax.experimental.pallas import tpu as pltpu
from jax.sharding import PartitionSpec as P

NSEQ = 64
BISECT_STEPS = 40


radius_factor = 2.0


def unchanged(single_value):
    return single_value


def dual_search(seq_loss, pair_total, one_total):
    sum_total = one_total(jnp.sum(seq_loss))

    def advance(step_index, bounds):
        lower, upper = bounds
        middle = 0.5 * (lower + upper)
        excess = jnp.maximum(seq_loss - middle, 0.0)
        square_sum, plain_sum = pair_total((jnp.sum(excess * excess), jnp.sum(excess)))
        is_above = NSEQ * square_sum - radius_factor * plain_sum * plain_sum >= 0.0
        return (jnp.where(is_above, lower, middle), jnp.where(is_above, middle, upper))

    lower, upper = lax.fori_loop(0, BISECT_STEPS, advance, (-sum_total, sum_total))
    excess = jnp.maximum(seq_loss - 0.5 * (lower + upper), 0.0)
    return excess / one_total(jnp.sum(excess))


def route_gates(route_logits, slot_order):
    top_k = slot_order.shape[1]
    columns = lax.broadcasted_iota(jnp.int32, (1, 1, top_k), 2)
    picked = jnp.sum(
        jnp.where(slot_order[:, :, None] == columns, route_logits[:, None, :], 0.0), axis=2
    )
    raised = jnp.exp(picked)
    return raised / jnp.sum(raised, axis=1, keepdims=True)


def by_expert(blocks, groups):
    exp_dev = blocks.shape[0] // groups
    tail_shape = blocks.shape[1:]
    split_view = blocks.reshape((groups, exp_dev) + tail_shape)
    moved_view = jnp.swapaxes(split_view, 0, 1)
    return moved_view.reshape((exp_dev, groups * tail_shape[0]) + tail_shape[1:])


def by_source(local_rows, groups):
    exp_dev = local_rows.shape[0]
    capacity = local_rows.shape[1] // groups
    tail_shape = local_rows.shape[2:]
    split_view = local_rows.reshape((exp_dev, groups, capacity) + tail_shape)
    return jnp.swapaxes(split_view, 0, 1).reshape((exp_dev * groups, capacity) + tail_shape)


def row_plan(tokens, targets, routes, route_logits, slot_order, seq_ids, w_gate, w_up, w_down):
    tok_rows, feat_width = tokens.shape
    top_k = routes.shape[1]
    groups = lax.axis_size("expert")
    exp_dev = w_gate.shape[0]
    experts = exp_dev * groups
    slot_count = tok_rows * top_k
    capacity = slot_count // experts
    grad_scale = float(tok_rows * lax.axis_size("dp") * groups // 8)
    flat_route = routes.reshape(slot_count)
    expert_hot = (flat_route[:, None] == lax.broadcasted_iota(jnp.int32, (1, experts), 1)).astype(
        jnp.int32
    )
    slot_rank = jnp.sum((jnp.cumsum(expert_hot, axis=0) - 1) * expert_hot, axis=1)
    slot_index = flat_route * capacity + slot_rank
    inverse = (
        jnp.zeros((slot_count,), jnp.int32).at[slot_index].set(lax.iota(jnp.int32, slot_count))
    )
    source_row = inverse // top_k
    gate_probs = route_gates(route_logits, slot_order)
    send_rows = tokens[source_row].reshape(experts, capacity, feat_width)
    arrived = lax.all_to_all(send_rows, "expert", split_axis=0, concat_axis=0, tiled=True)
    local_rows = by_expert(arrived, groups)
    gate_proj = jnp.einsum("erd,edh->erh", local_rows, w_gate, preferred_element_type=jnp.float32)
    up_proj = jnp.einsum("erd,edh->erh", local_rows, w_up, preferred_element_type=jnp.float32)
    hidden = (jax.nn.silu(gate_proj) * up_proj).astype(jnp.bfloat16)
    expert_out = jnp.einsum(
        "erh,neh->ern",
        hidden,
        lax.all_gather(w_down, "dp", axis=0, tiled=True),
        preferred_element_type=jnp.float32,
    ).astype(jnp.bfloat16)
    returned = lax.all_to_all(
        by_source(expert_out, groups), "expert", split_axis=0, concat_axis=0, tiled=True
    )
    per_slot = returned.reshape(slot_count, feat_width)[slot_index].reshape(
        tok_rows, top_k, feat_width
    )
    combined = jnp.sum(gate_probs[:, :, None] * per_slot.astype(jnp.float32), axis=1)
    error = combined - targets.astype(jnp.float32)
    error_low = error.astype(jnp.bfloat16)
    sent_error = lax.all_to_all(
        error_low[source_row].reshape(experts, capacity, feat_width),
        "expert",
        split_axis=0,
        concat_axis=0,
        tiled=True,
    )
    seq_hot = seq_ids[:, None] == lax.broadcasted_iota(jnp.int32, (1, NSEQ), 1)
    partial_sq = jnp.sum(jnp.where(seq_hot, jnp.sum(error * error, axis=1)[:, None], 0.0), axis=0)
    counts = jnp.sum(seq_hot.astype(jnp.float32), axis=0)
    seq_sq, seq_len = lax.psum((partial_sq, counts), ("dp", "expert"))
    seq_loss = seq_sq / (seq_len * feat_width)
    dual_weight = dual_search(seq_loss, unchanged, unchanged)
    seq_rate = dual_weight / seq_len
    scaled_gates = grad_scale * gate_probs
    token_rate = jnp.sum(jnp.where(seq_hot, seq_rate[None, :], 0.0), axis=1)
    flat_weight = (scaled_gates * token_rate[:, None]).reshape(slot_count)
    slot_weight = lax.all_to_all(
        flat_weight[inverse].reshape(experts, capacity),
        "expert",
        split_axis=0,
        concat_axis=0,
        tiled=True,
    )
    weight_local = by_expert(slot_weight, groups)
    error_local = by_expert(sent_error, groups)
    scaled = (weight_local[:, :, None] * hidden).astype(jnp.bfloat16)
    grad_down = lax.psum_scatter(
        jnp.einsum("ern,erh->neh", error_local, scaled, preferred_element_type=jnp.float32),
        "dp",
        scatter_dimension=0,
        tiled=True,
    )
    return (combined.astype(jnp.bfloat16), seq_loss, dual_weight, grad_down)


LANES = 128
FLOAT = jnp.float32
HALF = jnp.bfloat16
INFO = 16
SEQ_LINE = 8


def swap(block, axis, mask):
    size = lax.axis_size(axis)
    return lax.ppermute(block, axis, [(s, s ^ mask) for s in range(size)])


def tree_sum(terms):
    while len(terms) > 1:
        rest = terms[len(terms) // 2 * 2 :]
        terms = [a + b for a, b in zip(terms[::2], terms[1::2])] + rest
    return terms[0]


def dot_nt(a, b):
    return lax.dot_general(a, b, (((1,), (1,)), ((), ())), preferred_element_type=FLOAT)


def dot_nn(a, b):
    return jnp.dot(a, b, preferred_element_type=FLOAT)


def cost():
    return pl.CostEstimate(flops=1, bytes_accessed=1, transcendentals=0)


def params(mib=60):
    return pltpu.CompilerParams(vmem_limit_bytes=mib << 20)


def col_to_row(col):
    count = col.shape[0]
    diagonal = lax.broadcasted_iota(jnp.int32, (count, LANES), 0) == lax.broadcasted_iota(
        jnp.int32, (count, LANES), 1
    )
    return jnp.sum(jnp.where(diagonal, col, 0.0), axis=0, keepdims=True)


def row_to_col(row, count):
    diagonal = lax.broadcasted_iota(jnp.int32, (count, LANES), 0) == lax.broadcasted_iota(
        jnp.int32, (count, LANES), 1
    )
    return jnp.sum(jnp.where(diagonal, row, 0.0), axis=1, keepdims=True)


def in_vmem(count=1):
    return [pl.BlockSpec(memory_space=pltpu.VMEM)] * count


def pack_tokens_kernel(experts, tokens, routes, logits, order, seq, out):
    top_k, rows = routes.shape
    names, slots, scores = routes[...], order[...], logits[...]
    picked = jnp.zeros((top_k, rows), FLOAT)
    for k in range(top_k):
        picked += jnp.where(slots == k, scores[k : k + 1, :], 0.0)
    raised = jnp.exp(picked)
    gates = raised / jnp.sum(raised, axis=0, keepdims=True)
    expert = lax.broadcasted_iota(jnp.int32, (experts, rows), 0)
    named = jnp.zeros((experts, rows), FLOAT)
    prob = jnp.zeros((experts, rows), FLOAT)
    for k in range(top_k):
        hit = names[k : k + 1, :] == expert
        named += jnp.where(hit, 1.0, 0.0)
        prob += jnp.where(hit, gates[k : k + 1, :], 0.0)
    before = lax.broadcasted_iota(jnp.int32, (rows, rows), 0) < lax.broadcasted_iota(
        jnp.int32, (rows, rows), 1
    )
    rank = dot_nn(named.astype(HALF), jnp.where(before, 1.0, 0.0).astype(HALF))
    place = jnp.where(named > 0.5, rank, -1.0).astype(HALF)
    number = jnp.broadcast_to(seq[...].astype(FLOAT), (experts, rows)).astype(HALF)
    out[0:rows, :] = tokens[...]
    out[rows:, :] = jnp.zeros((experts, out.shape[1]), HALF)
    for b, piece in enumerate([place, *exact_pieces(prob), number]):
        out[rows:, b * rows : (b + 1) * rows] = piece


def exact_pieces(value):
    pieces = []
    for _ in range(3):
        pieces.append(value.astype(HALF))
        value = value - pieces[-1].astype(FLOAT)
    return pieces


def pack_tokens(tokens, routes, route_logits, slot_order, seq_ids, experts):
    rows, width = tokens.shape
    return pl.pallas_call(
        functools.partial(pack_tokens_kernel, experts),
        in_specs=in_vmem(5),
        out_specs=pl.BlockSpec(memory_space=pltpu.VMEM),
        out_shape=jax.ShapeDtypeStruct((rows + experts, width), HALF),
        cost_estimate=cost(),
        compiler_params=params(),
        name="pack_tokens",
    )(tokens, routes.T, route_logits.T, slot_order.T, seq_ids.reshape(1, rows))


def hidden_kernel(experts, capacity, own, x_side, y_side, upper, lower, *refs):
    w_gate, w_up, out, joined, info, picked, probs, both, arrived = refs
    exp_dev, _, units = w_gate.shape
    for e in range(exp_dev):
        pltpu.make_async_copy(w_gate.at[e], both.at[e, :, pl.ds(0, units)], arrived.at[e]).start()
        pltpu.make_async_copy(w_up.at[e], both.at[e, :, pl.ds(units, units)], arrived.at[e]).start()
    joined[0 : upper.shape[0], :] = upper[...]
    joined[joined.shape[0] - lower.shape[0] :, :] = lower[...]
    tokens = [own, x_side, y_side, joined]
    total = len(tokens) * capacity
    rows = own.shape[0] - experts
    first = lax.axis_index("expert") * exp_dev
    slot = lax.broadcasted_iota(jnp.int32, (capacity, rows), 0).astype(FLOAT)
    lane = lax.broadcasted_iota(jnp.int32, (INFO, rows), 1).astype(FLOAT).astype(HALF)
    line = lax.broadcasted_iota(jnp.int32, (INFO, total), 0)
    expert = lax.broadcasted_iota(jnp.int32, (experts, rows), 0)
    info[...] = jnp.zeros(info.shape, FLOAT)
    origins = [[] for _ in range(exp_dev)]
    for m, block in enumerate(tokens):
        place, high, middle, low, number = (
            block[rows:, b * rows : (b + 1) * rows].astype(FLOAT) for b in range(5)
        )
        prob = high + middle + low
        info[SEQ_LINE + m : SEQ_LINE + m + 1, 0:rows] = number[0:1, :]
        picks = []
        for e in range(exp_dev):
            mine = expert == first + e
            own_place = jnp.sum(jnp.where(mine, place, 0.0), axis=0, keepdims=True)
            own_prob = jnp.sum(jnp.where(mine, prob, 0.0), axis=0, keepdims=True)
            pick = jnp.where(own_place == slot, 1.0, 0.0)
            probs[e, m * capacity : (m + 1) * capacity, :] = jnp.broadcast_to(
                jnp.sum(pick * own_prob, axis=1, keepdims=True), (capacity, LANES)
            )
            picks.append(pick.astype(HALF))
            origins[e].append(picks[-1])
        rows_m = dot_nn(jnp.concatenate(picks, axis=0), block[0:rows, :]).astype(HALF)
        for e in range(exp_dev):
            picked[e, m * capacity : (m + 1) * capacity, :] = rows_m[
                e * capacity : (e + 1) * capacity, :
            ]
    for e in range(exp_dev):
        origin = dot_nt(lane, jnp.concatenate(origins[e], axis=0))
        info[:, 0:total] = jnp.where(line == e, origin, info[:, 0:total])
    out[exp_dev * total :, :] = info[...].astype(HALF)

    def one_expert(e, carry):
        chosen = picked[e]
        pltpu.make_async_copy(both.at[e], both.at[e], arrived.at[e]).wait()
        product = dot_nn(chosen, both[e])
        gate, up = product[:, :units], product[:, units:]
        hidden = (gate / (1.0 + jnp.exp(-gate)) * up).astype(HALF)
        scaled = (probs[e, :, 0:1] * hidden.astype(FLOAT)).astype(HALF)
        out[pl.ds(pl.multiple_of(e * total, total), total), :] = scaled
        return carry

    lax.fori_loop(0, exp_dev, one_expert, 0)


def hidden_rows(tokens, w_gate, w_up, experts, capacity):
    lines, width = tokens[0].shape
    exp_dev, _, units = w_gate.shape
    total = 4 * capacity
    return pl.pallas_call(
        functools.partial(hidden_kernel, experts, capacity),
        in_specs=in_vmem(5) + [pl.BlockSpec(memory_space=pl.ANY)] * 2,
        out_specs=pl.BlockSpec(memory_space=pltpu.VMEM),
        out_shape=jax.ShapeDtypeStruct((exp_dev * total + INFO, units), HALF),
        scratch_shapes=[
            pltpu.VMEM((lines, width), HALF),
            pltpu.VMEM((INFO, units), FLOAT),
            pltpu.VMEM((exp_dev, total, width), HALF),
            pltpu.VMEM((exp_dev, total, LANES), FLOAT),
            pltpu.VMEM((exp_dev, width, 2 * units), HALF),
            pltpu.SemaphoreType.DMA((exp_dev,)),
        ],
        cost_estimate=cost(),
        compiler_params=params(56),
        name="hidden_rows",
    )(*tokens, w_gate, w_up)


def row_places(info, e, total, capacity, rows, sources):
    shift = (lax.broadcasted_iota(jnp.int32, (1, total), 1) // capacity * rows).astype(FLOAT)
    token = lax.broadcasted_iota(jnp.int32, (sources * rows, total), 0).astype(FLOAT)
    return jnp.where(token == info[e : e + 1, 0:total] + shift, 1.0, 0.0).astype(HALF)


def project_kernel(exp_dev, capacity, rows, sources, slots, *refs):
    blocks, (w_down, seqs), refs = refs[:slots], refs[slots : slots + 2], refs[slots + 2 :]
    partials, (packed, outs, places, arrived) = refs[:sources], refs[sources:]
    units = w_down.shape[1] // exp_dev
    total = sources * capacity
    fetches = [
        pltpu.make_async_copy(blocks[s], packed.at[s], arrived.at[s]) for s in range(slots)
    ]
    for copy in fetches:
        copy.start()

    def one_slot(s, carry):
        pltpu.make_async_copy(packed.at[s], packed.at[s], arrived.at[s]).wait()
        info = packed[s, exp_dev * total :, :].astype(FLOAT)
        seqs[s] = info[SEQ_LINE:, 0:rows]
        for e in range(exp_dev):
            here = slice(e * total, (e + 1) * total)
            outs[:, here] = dot_nt(
                w_down[:, e * units : (e + 1) * units], packed[s, here, :]
            ).astype(HALF)
            places[:, here] = row_places(info, e, total, capacity, rows, sources)
        part = dot_nt(outs[...], places[...]).astype(HALF)
        for k in range(sources):
            partials[k][s] = part[:, k * rows : (k + 1) * rows]
        return carry

    lax.fori_loop(0, slots, one_slot, 0)


def project(blocks, w_down, exp_dev, capacity, rows, sources):
    slots = len(blocks)
    feats = w_down.shape[0]
    total = exp_dev * sources * capacity
    out = pl.pallas_call(
        functools.partial(project_kernel, exp_dev, capacity, rows, sources, slots),
        in_specs=[pl.BlockSpec(memory_space=pl.ANY)] * slots + in_vmem(1),
        out_specs=in_vmem(1 + sources),
        out_shape=[jax.ShapeDtypeStruct((slots, 8, rows), FLOAT)]
        + [jax.ShapeDtypeStruct((slots, feats, rows), HALF)] * sources,
        scratch_shapes=[
            pltpu.VMEM((slots,) + blocks[0].shape, HALF),
            pltpu.VMEM((feats, total), HALF),
            pltpu.VMEM((sources * rows, total), HALF),
            pltpu.SemaphoreType.DMA((slots,)),
        ],
        cost_estimate=cost(),
        compiler_params=params(16),
        name="project",
    )(*blocks, w_down)
    return out[0], out[1:]


def spread_kernel(exp_dev, capacity, rows, sources, *refs):
    slots = len(refs) - 5
    blocks, (spread, packed, held, arrived, done) = refs[:slots], refs[slots:]
    units = packed.shape[2]
    total = sources * capacity
    fetches = [
        pltpu.make_async_copy(blocks[s], packed.at[s], arrived.at[s]) for s in range(slots)
    ]
    for copy in fetches:
        copy.start()

    def one_slot(s, carry):
        pltpu.make_async_copy(packed.at[s], packed.at[s], arrived.at[s]).wait()
        info = packed[s, exp_dev * total :, :].astype(FLOAT)
        for e in range(exp_dev):
            place = row_places(info, e, total, capacity, rows, sources)
            rows_e = packed[s, e * total : (e + 1) * total, :]
            held[s, :, e * units : (e + 1) * units] = dot_nn(place, rows_e).astype(HALF)
        pltpu.make_async_copy(held.at[s], spread.at[s], done.at[s]).start()
        return carry

    lax.fori_loop(0, slots, one_slot, 0)
    for s in range(slots):
        pltpu.make_async_copy(held.at[s], spread.at[s], done.at[s]).wait()


def spread_rows(blocks, exp_dev, capacity, rows, sources):
    slots = len(blocks)
    shape = (slots, sources * rows, exp_dev * blocks[0].shape[1])
    return pl.pallas_call(
        functools.partial(spread_kernel, exp_dev, capacity, rows, sources),
        in_specs=[pl.BlockSpec(memory_space=pl.ANY)] * slots,
        out_specs=pl.BlockSpec(memory_space=pl.ANY),
        out_shape=jax.ShapeDtypeStruct(shape, HALF),
        scratch_shapes=[
            pltpu.VMEM((slots,) + blocks[0].shape, HALF),
            pltpu.VMEM(shape, HALF),
            pltpu.SemaphoreType.DMA((slots,)),
            pltpu.SemaphoreType.DMA((slots,)),
        ],
        cost_estimate=cost(),
        compiler_params=params(24),
        name="spread_rows",
    )(*blocks)


def residual_kernel(first, slots, sources, carried, ordered, *refs):
    parts, (seq, targets, *refs) = refs[:sources], refs[sources:]
    if first:
        before, refs = refs[0], refs[1:]
    if carried:
        refs[-2][0:carried, :] = refs[0][...]
        refs = refs[1:]
    *blocks, errors, squares = refs
    feats, rows = targets.shape[1:]
    me = lax.axis_index("dp")
    number = lax.broadcasted_iota(jnp.int32, (NSEQ, rows), 0).astype(FLOAT)
    squared = jnp.zeros((NSEQ, rows), FLOAT)
    if ordered:
        for s in range(first):
            blocks[-1][me ^ s] = blocks[s][...]
    for s in range(slots):
        total = tree_sum([part[s].astype(FLOAT) for part in parts])
        if ordered:
            blocks[-1][me ^ (first + s)] = total.astype(HALF)
        else:
            blocks[s][...] = total.astype(HALF)
        error = total - targets[me ^ (first + s)].astype(FLOAT)
        errors[carried + s * feats : carried + (s + 1) * feats, :] = error.astype(HALF)
        per_token = jnp.sum(error * error, axis=0, keepdims=True)
        squared += jnp.where(seq[s, 0:1, :] == number, per_token, 0.0)
    sums = jnp.broadcast_to(col_to_row(jnp.sum(squared, axis=1, keepdims=True)), (8, LANES))
    squares[...] = sums + before[...] if first else sums


def residual(first, parts, seq, targets, before=(), errors=(), earlier=()):
    groups, feats, rows = targets.shape
    slots = parts[0].shape[0]
    sources = len(parts)
    ordered = len(earlier) > 0
    carried = sum(block.shape[0] for block in errors)
    if ordered:
        blocks = [jax.ShapeDtypeStruct((groups, feats, rows), HALF)]
    else:
        blocks = [jax.ShapeDtypeStruct((feats, rows), HALF)] * slots
    extra = [*before, *errors, *earlier]
    *combined, errors, squares = pl.pallas_call(
        functools.partial(residual_kernel, first, slots, sources, carried, ordered),
        in_specs=in_vmem(sources + 2 + len(extra)),
        out_specs=in_vmem(len(blocks) + 2),
        out_shape=blocks
        + [
            jax.ShapeDtypeStruct((carried + slots * feats, rows), HALF),
            jax.ShapeDtypeStruct((8, LANES), FLOAT),
        ],
        cost_estimate=cost(),
        compiler_params=params(16),
        name="residual",
    )(*parts, seq, targets, *extra)
    return combined, errors, squares


def gather_features_kernel(first, whole, *refs):
    late, out = refs[:-1], refs[-1]
    groups, feats, _ = whole.shape
    me = lax.axis_index("dp")
    for g in range(groups):
        out[:, g * feats : (g + 1) * feats] = whole[g].T
    for k, block in enumerate(late):
        start = pl.multiple_of((me ^ (first + k)) * feats, feats)
        out[:, pl.ds(start, feats)] = block[...].T


def gather_features(first, whole, late):
    groups, feats, rows = whole.shape
    return pl.pallas_call(
        functools.partial(gather_features_kernel, first),
        in_specs=in_vmem(1 + len(late)),
        out_specs=pl.BlockSpec(memory_space=pltpu.VMEM),
        out_shape=jax.ShapeDtypeStruct((rows, feats * groups), HALF),
        cost_estimate=cost(),
        compiler_params=params(16),
        name="gather_features",
    )(whole, *late)


def gradient_kernel(scale, feat_width, exp_dev, terms, batches, parts, sources, *refs):
    squares, refs = refs[:terms], refs[terms:]
    count, groups = len(batches), sum(batches)
    spreads, seqs, refs = refs[:count], refs[count : 2 * count], refs[2 * count :]
    errors, refs = refs[: sources * len(parts)], refs[sources * len(parts) :]
    grad, seq_loss, dual_weight, held, error, lines, weighted, total, rates, arrived = refs
    feats = grad.shape[0]
    rows = error.shape[2] // sources
    slot = 0
    for b, slots in enumerate(parts):
        for s in range(slots):
            for m in range(sources):
                pltpu.make_async_copy(
                    errors[b * sources + m].at[pl.ds(s * feats, feats), :],
                    error.at[slot, :, pl.ds(m * rows, rows)],
                    arrived.at[0, slot],
                ).start()
            slot += 1
    slot = 0
    for seq, spread, slots in zip(seqs, spreads, batches):
        for s in range(slots):
            lines[slot] = seq[s]
            pltpu.make_async_copy(
                spread.at[s],
                held.at[slot // 2, pl.ds(slot % 2 * sources * rows, sources * rows)],
                arrived.at[1, slot // 2],
            ).start()
            slot += 1
    number = lax.broadcasted_iota(jnp.int32, (NSEQ, rows), 0).astype(FLOAT)

    def count_slot(s, found):
        for m in range(sources):
            found += jnp.where(lines[s, m : m + 1, :] == number, 1.0, 0.0)
        return found

    found = lax.fori_loop(0, groups, count_slot, jnp.zeros((NSEQ, rows), FLOAT))
    seq_len = jnp.sum(found, axis=1, keepdims=True)
    summed = tree_sum([part[0:1, :] for part in squares])
    loss = row_to_col(summed, NSEQ) / (seq_len * feat_width)
    loss = jnp.broadcast_to(loss, (NSEQ, LANES))
    weight = dual_search_rows(loss)
    rates[...] = scale * (weight / seq_len)
    seq_loss[...] = col_to_row(loss)[:, 0:NSEQ]
    dual_weight[...] = col_to_row(weight)[:, 0:NSEQ]
    total[...] = jnp.zeros(total.shape, FLOAT)
    for s in range(groups):
        pltpu.make_async_copy(error.at[s], error.at[s], arrived.at[0, s]).wait()

    def weigh(pair, turn):
        for k in range(2):
            for m in range(sources):
                here = slice(m * rows, (m + 1) * rows)
                there = slice((k * sources + m) * rows, (k * sources + m + 1) * rows)
                hit = jnp.where(lines[2 * pair + k, m : m + 1, :] == number, rates[...], 0.0)
                rate = jnp.sum(hit, axis=0, keepdims=True)
                weighted[turn, :, there] = (
                    rate * error[2 * pair + k, :, here].astype(FLOAT)
                ).astype(HALF)

    def add_pair(pair, carry):
        pltpu.make_async_copy(held.at[pair], held.at[pair], arrived.at[1, pair]).wait()
        product = dot_nn(weighted[pair % 2], held[pair])
        weigh(jnp.minimum(pair + 1, groups // 2 - 1), (pair + 1) % 2)
        total[...] += product
        return carry

    weigh(0, 0)
    lax.fori_loop(0, groups // 2, add_pair, 0)
    units = grad.shape[2]
    for e in range(exp_dev):
        grad[:, e, :] = total[:, e * units : (e + 1) * units]


def dual_search_rows(loss):
    bound = jnp.sum(loss, axis=0, keepdims=True)

    def advance(step_index, bounds):
        lower, upper = bounds
        middle = 0.5 * (lower + upper)
        excess = jnp.maximum(loss - middle, 0.0)
        square_sum = jnp.sum(excess * excess, axis=0, keepdims=True)
        plain_sum = jnp.sum(excess, axis=0, keepdims=True)
        is_above = NSEQ * square_sum - radius_factor * plain_sum * plain_sum >= 0.0
        return (jnp.where(is_above, lower, middle), jnp.where(is_above, middle, upper))

    lower, upper = lax.fori_loop(
        0, BISECT_STEPS, advance, (-bound, bound), unroll=True
    )
    excess = jnp.maximum(loss - 0.5 * (lower + upper), 0.0)
    return excess / jnp.sum(excess, axis=0, keepdims=True)


def gradient(squares, spreads, seqs, errors, batches, parts, sources, scale, feat_width, exp_dev):
    rows = errors[0].shape[1]
    feats = errors[0].shape[0] // parts[0]
    group_rows, flat = spreads[0].shape[1:]
    units = flat // exp_dev
    groups = sum(batches)
    return pl.pallas_call(
        functools.partial(
            gradient_kernel, scale, feat_width, exp_dev, len(squares), batches, parts, sources
        ),
        in_specs=in_vmem(len(squares))
        + [pl.BlockSpec(memory_space=pl.ANY)] * len(spreads)
        + in_vmem(len(seqs))
        + [pl.BlockSpec(memory_space=pl.ANY)] * (len(errors) - sources)
        + in_vmem(sources),
        out_specs=in_vmem(3),
        out_shape=[
            jax.ShapeDtypeStruct((feats, exp_dev, units), FLOAT),
            jax.ShapeDtypeStruct((1, NSEQ), FLOAT),
            jax.ShapeDtypeStruct((1, NSEQ), FLOAT),
        ],
        scratch_shapes=[
            pltpu.VMEM((groups // 2, 2 * group_rows, flat), HALF),
            pltpu.VMEM((groups, feats, group_rows), HALF),
            pltpu.VMEM((groups, 8, rows), FLOAT),
            pltpu.VMEM((2, feats, 2 * group_rows), HALF),
            pltpu.VMEM((feats, flat), FLOAT),
            pltpu.VMEM((NSEQ, rows), FLOAT),
            pltpu.SemaphoreType.DMA((2, groups)),
        ],
        cost_estimate=cost(),
        compiler_params=params(58),
        name="gradient",
    )(*squares, *spreads, *seqs, *errors)


def z_near(block):
    return {2: swap(block, "dp", 2), 4: swap(block, "dp", 4)}


def z_far(blocks):
    return swap(blocks[4], "dp", 2)


def feature_plan(tokens, targets, routes, route_logits, slot_order, seq_ids, w_gate, w_up, w_down):
    rows, feat_width = tokens.shape
    groups, sources = lax.axis_size("dp"), lax.axis_size("expert")
    exp_dev, _, units = w_gate.shape
    experts = exp_dev * sources
    capacity = rows * routes.shape[1] // experts
    feats = feat_width // groups
    scale = float(rows * groups * sources // 8)
    far = range(1, sources)
    tie = lax.optimization_barrier

    own_tokens = pack_tokens(tokens, routes, route_logits, slot_order, seq_ids, experts)
    x_tokens, y_tokens = swap(own_tokens, "expert", 1), swap(own_tokens, "expert", 2)
    half = (rows + experts + 31) // 32 * 16
    diagonal = [swap(y_tokens[:half], "expert", 1), swap(x_tokens[-half:], "expert", 2)]
    turned, own_tokens = tie((targets.T, own_tokens))
    own_targets = lax.all_to_all(
        turned.reshape(groups, feats, rows), "dp", split_axis=0, concat_axis=0, tiled=True
    )
    x_tokens, y_tokens, diagonal, own_targets = tie((x_tokens, y_tokens, diagonal, own_targets))
    packed = hidden_rows(
        [own_tokens, x_tokens, y_tokens, *diagonal], w_gate, w_up, experts, capacity
    )
    blocks = {0: packed, **z_near(packed)}
    flat_down = w_down.reshape(feats, exp_dev * units)

    def expert_parts(first, slots):
        for s in range(first, first + slots, 2):
            blocks[s + 1] = swap(blocks[s], "dp", 1)
        here = [blocks[s] for s in range(first, first + slots)]
        seq, parts = project(here, flat_down, exp_dev, capacity, rows, sources)
        parts = [parts[0]] + [swap(parts[m], "expert", m) for m in far]
        spread = spread_rows(here, exp_dev, capacity, rows, sources)
        parts, spread = tie((parts, spread))
        return spread, seq, parts

    def far_errors(error):
        return [swap(error, "expert", m) for m in far]

    batches = (2, groups - 4, 2)
    spread_0, seq_0, parts_0 = expert_parts(0, batches[0])
    mixed_0, error_0, squares = residual(0, parts_0, seq_0, own_targets)
    errors_0 = far_errors(error_0)
    blocks, errors_0 = tie((blocks, errors_0))
    blocks[6] = z_far(blocks)

    spread_1, seq_1, parts_1 = expert_parts(2, batches[1])
    blocks[6], parts_1 = tie((blocks[6], parts_1))
    mixed_1, error_1, squares = residual(
        2, parts_1, seq_1, own_targets, before=[squares], earlier=mixed_0
    )
    mixed_1 = lax.all_to_all(mixed_1[0], "dp", split_axis=0, concat_axis=0, tiled=True)
    spread_2, seq_2, parts_2 = expert_parts(groups - 2, batches[2])
    mixed_2, error_1, squares = residual(
        groups - 2, parts_2, seq_2, own_targets, before=[squares], errors=[error_1]
    )
    errors_1 = far_errors(error_1)
    mixed_2 = [swap(block, "dp", groups - 2 + s) for s, block in enumerate(mixed_2)]
    mixed = gather_features(groups - 2, mixed_1, mixed_2)
    squares = squares + swap(squares, "dp", 1)
    squares = tree_sum([squares] + [swap(squares, "dp", m) for m in range(2, groups, 2)])
    squares, mixed = tie((squares, mixed))
    all_squares = [squares] + [swap(squares, "expert", m) for m in far]
    grad_down, seq_loss, dual_weight = gradient(
        all_squares,
        [spread_0, spread_1, spread_2],
        [seq_0, seq_1, seq_2],
        [error_0, *errors_0, error_1, *errors_1],
        batches,
        (batches[0], batches[1] + batches[2]),
        sources,
        scale,
        feat_width,
        exp_dev,
    )
    return (
        mixed,
        seq_loss.reshape(NSEQ),
        dual_weight.reshape(NSEQ),
        grad_down,
    )


def local(tokens, targets, routes, route_logits, slot_order, seq_ids, w_gate, w_up, w_down):
    args = (tokens, targets, routes, route_logits, slot_order, seq_ids, w_gate, w_up, w_down)
    groups, sources = lax.axis_size("dp"), lax.axis_size("expert")
    units = w_gate.shape[2]
    exp_dev = w_gate.shape[0]
    rows, feat_width = tokens.shape
    capacity = rows * routes.shape[1] // (exp_dev * sources)
    whole_tiles = (
        feat_width % (groups * LANES) == 0
        and rows == LANES
        and units % LANES == 0
        and sources * capacity <= units
        and capacity % 16 == 0
        and exp_dev <= SEQ_LINE
        and exp_dev * sources == INFO
        and sources == 4
        and groups == 8
    )
    return (feature_plan if whole_tiles else row_plan)(*args)


def solution(mesh):
    return jax.shard_map(
        local,
        mesh=mesh,
        in_specs=(
            P(("dp", "expert"), None),
            P(("dp", "expert"), None),
            P(("dp", "expert"), None),
            P(("dp", "expert"), None),
            P(("dp", "expert"), None),
            P(("dp", "expert")),
            P("expert", None, None),
            P("expert", None, None),
            P("dp", "expert", None),
        ),
        out_specs=(P(("dp", "expert"), None), P(), P(), P("dp", "expert", None)),
        check_vma=False,
    )
```

```python
import functools

import jax
import jax.numpy as jnp
from jax import lax
from jax.experimental import pallas as pl
from jax.experimental.pallas import tpu as pltpu
from jax.sharding import PartitionSpec as P

NSEQ = 64
BISECT_STEPS = 40


radius_factor = 2.0


def unchanged(single_value):
    return single_value


def dual_search(seq_loss, pair_total, one_total):
    sum_total = one_total(jnp.sum(seq_loss))

    def advance(step_index, bounds):
        lower, upper = bounds
        middle = 0.5 * (lower + upper)
        excess = jnp.maximum(seq_loss - middle, 0.0)
        square_sum, plain_sum = pair_total((jnp.sum(excess * excess), jnp.sum(excess)))
        is_above = NSEQ * square_sum - radius_factor * plain_sum * plain_sum >= 0.0
        return (jnp.where(is_above, lower, middle), jnp.where(is_above, middle, upper))

    lower, upper = lax.fori_loop(0, BISECT_STEPS, advance, (-sum_total, sum_total))
    excess = jnp.maximum(seq_loss - 0.5 * (lower + upper), 0.0)
    return excess / one_total(jnp.sum(excess))


def route_gates(route_logits, slot_order):
    top_k = slot_order.shape[1]
    columns = lax.broadcasted_iota(jnp.int32, (1, 1, top_k), 2)
    picked = jnp.sum(
        jnp.where(slot_order[:, :, None] == columns, route_logits[:, None, :], 0.0), axis=2
    )
    raised = jnp.exp(picked)
    return raised / jnp.sum(raised, axis=1, keepdims=True)


def by_expert(blocks, groups):
    exp_dev = blocks.shape[0] // groups
    tail_shape = blocks.shape[1:]
    split_view = blocks.reshape((groups, exp_dev) + tail_shape)
    moved_view = jnp.swapaxes(split_view, 0, 1)
    return moved_view.reshape((exp_dev, groups * tail_shape[0]) + tail_shape[1:])


def by_source(local_rows, groups):
    exp_dev = local_rows.shape[0]
    capacity = local_rows.shape[1] // groups
    tail_shape = local_rows.shape[2:]
    split_view = local_rows.reshape((exp_dev, groups, capacity) + tail_shape)
    return jnp.swapaxes(split_view, 0, 1).reshape((exp_dev * groups, capacity) + tail_shape)


def row_plan(tokens, targets, routes, route_logits, slot_order, seq_ids, w_gate, w_up, w_down):
    tok_rows, feat_width = tokens.shape
    top_k = routes.shape[1]
    groups = lax.axis_size("expert")
    exp_dev = w_gate.shape[0]
    experts = exp_dev * groups
    slot_count = tok_rows * top_k
    capacity = slot_count // experts
    grad_scale = float(tok_rows * lax.axis_size("dp") * groups // 8)
    flat_route = routes.reshape(slot_count)
    expert_hot = (flat_route[:, None] == lax.broadcasted_iota(jnp.int32, (1, experts), 1)).astype(
        jnp.int32
    )
    slot_rank = jnp.sum((jnp.cumsum(expert_hot, axis=0) - 1) * expert_hot, axis=1)
    slot_index = flat_route * capacity + slot_rank
    inverse = (
        jnp.zeros((slot_count,), jnp.int32).at[slot_index].set(lax.iota(jnp.int32, slot_count))
    )
    source_row = inverse // top_k
    gate_probs = route_gates(route_logits, slot_order)
    send_rows = tokens[source_row].reshape(experts, capacity, feat_width)
    arrived = lax.all_to_all(send_rows, "expert", split_axis=0, concat_axis=0, tiled=True)
    local_rows = by_expert(arrived, groups)
    gate_proj = jnp.einsum("erd,edh->erh", local_rows, w_gate, preferred_element_type=jnp.float32)
    up_proj = jnp.einsum("erd,edh->erh", local_rows, w_up, preferred_element_type=jnp.float32)
    hidden = (jax.nn.silu(gate_proj) * up_proj).astype(jnp.bfloat16)
    expert_out = jnp.einsum(
        "erh,neh->ern",
        hidden,
        lax.all_gather(w_down, "dp", axis=0, tiled=True),
        preferred_element_type=jnp.float32,
    ).astype(jnp.bfloat16)
    returned = lax.all_to_all(
        by_source(expert_out, groups), "expert", split_axis=0, concat_axis=0, tiled=True
    )
    per_slot = returned.reshape(slot_count, feat_width)[slot_index].reshape(
        tok_rows, top_k, feat_width
    )
    combined = jnp.sum(gate_probs[:, :, None] * per_slot.astype(jnp.float32), axis=1)
    error = combined - targets.astype(jnp.float32)
    error_low = error.astype(jnp.bfloat16)
    sent_error = lax.all_to_all(
        error_low[source_row].reshape(experts, capacity, feat_width),
        "expert",
        split_axis=0,
        concat_axis=0,
        tiled=True,
    )
    seq_hot = seq_ids[:, None] == lax.broadcasted_iota(jnp.int32, (1, NSEQ), 1)
    partial_sq = jnp.sum(jnp.where(seq_hot, jnp.sum(error * error, axis=1)[:, None], 0.0), axis=0)
    counts = jnp.sum(seq_hot.astype(jnp.float32), axis=0)
    seq_sq, seq_len = lax.psum((partial_sq, counts), ("dp", "expert"))
    seq_loss = seq_sq / (seq_len * feat_width)
    dual_weight = dual_search(seq_loss, unchanged, unchanged)
    seq_rate = dual_weight / seq_len
    scaled_gates = grad_scale * gate_probs
    token_rate = jnp.sum(jnp.where(seq_hot, seq_rate[None, :], 0.0), axis=1)
    flat_weight = (scaled_gates * token_rate[:, None]).reshape(slot_count)
    slot_weight = lax.all_to_all(
        flat_weight[inverse].reshape(experts, capacity),
        "expert",
        split_axis=0,
        concat_axis=0,
        tiled=True,
    )
    weight_local = by_expert(slot_weight, groups)
    error_local = by_expert(sent_error, groups)
    scaled = (weight_local[:, :, None] * hidden).astype(jnp.bfloat16)
    grad_down = lax.psum_scatter(
        jnp.einsum("ern,erh->neh", error_local, scaled, preferred_element_type=jnp.float32),
        "dp",
        scatter_dimension=0,
        tiled=True,
    )
    return (combined.astype(jnp.bfloat16), seq_loss, dual_weight, grad_down)


LANES = 128
FLOAT = jnp.float32
HALF = jnp.bfloat16
INFO = 16
SEQ_LINE = 8


def swap(block, axis, mask):
    size = lax.axis_size(axis)
    return lax.ppermute(block, axis, [(s, s ^ mask) for s in range(size)])


def tree_sum(terms):
    while len(terms) > 1:
        rest = terms[len(terms) // 2 * 2 :]
        terms = [a + b for a, b in zip(terms[::2], terms[1::2])] + rest
    return terms[0]


def dot_nt(a, b):
    return lax.dot_general(a, b, (((1,), (1,)), ((), ())), preferred_element_type=FLOAT)


def dot_nn(a, b):
    return jnp.dot(a, b, preferred_element_type=FLOAT)


def cost():
    return pl.CostEstimate(flops=1, bytes_accessed=1, transcendentals=0)


def params(mib=60):
    return pltpu.CompilerParams(vmem_limit_bytes=mib << 20)


def col_to_row(col):
    count = col.shape[0]
    diagonal = lax.broadcasted_iota(jnp.int32, (count, LANES), 0) == lax.broadcasted_iota(
        jnp.int32, (count, LANES), 1
    )
    return jnp.sum(jnp.where(diagonal, col, 0.0), axis=0, keepdims=True)


def row_to_col(row, count):
    diagonal = lax.broadcasted_iota(jnp.int32, (count, LANES), 0) == lax.broadcasted_iota(
        jnp.int32, (count, LANES), 1
    )
    return jnp.sum(jnp.where(diagonal, row, 0.0), axis=1, keepdims=True)


def in_vmem(count=1):
    return [pl.BlockSpec(memory_space=pltpu.VMEM)] * count


def pack_tokens_kernel(experts, tokens, routes, logits, order, seq, out):
    top_k, rows = routes.shape
    names, slots, scores = routes[...], order[...], logits[...]
    picked = jnp.zeros((top_k, rows), FLOAT)
    for k in range(top_k):
        picked += jnp.where(slots == k, scores[k : k + 1, :], 0.0)
    raised = jnp.exp(picked)
    gates = raised / jnp.sum(raised, axis=0, keepdims=True)
    expert = lax.broadcasted_iota(jnp.int32, (experts, rows), 0)
    named = jnp.zeros((experts, rows), FLOAT)
    prob = jnp.zeros((experts, rows), FLOAT)
    for k in range(top_k):
        hit = names[k : k + 1, :] == expert
        named += jnp.where(hit, 1.0, 0.0)
        prob += jnp.where(hit, gates[k : k + 1, :], 0.0)
    before = lax.broadcasted_iota(jnp.int32, (rows, rows), 0) < lax.broadcasted_iota(
        jnp.int32, (rows, rows), 1
    )
    rank = dot_nn(named.astype(HALF), jnp.where(before, 1.0, 0.0).astype(HALF))
    place = jnp.where(named > 0.5, rank, -1.0).astype(HALF)
    number = jnp.broadcast_to(seq[...].astype(FLOAT), (experts, rows)).astype(HALF)
    out[0:rows, :] = tokens[...]
    out[rows:, :] = jnp.zeros((experts, out.shape[1]), HALF)
    for b, piece in enumerate([place, *exact_pieces(prob), number]):
        out[rows:, b * rows : (b + 1) * rows] = piece


def exact_pieces(value):
    pieces = []
    for _ in range(3):
        pieces.append(value.astype(HALF))
        value = value - pieces[-1].astype(FLOAT)
    return pieces


def pack_tokens(tokens, routes, route_logits, slot_order, seq_ids, experts):
    rows, width = tokens.shape
    return pl.pallas_call(
        functools.partial(pack_tokens_kernel, experts),
        in_specs=in_vmem(5),
        out_specs=pl.BlockSpec(memory_space=pltpu.VMEM),
        out_shape=jax.ShapeDtypeStruct((rows + experts, width), HALF),
        cost_estimate=cost(),
        compiler_params=params(),
        name="pack_tokens",
    )(tokens, routes.T, route_logits.T, slot_order.T, seq_ids.reshape(1, rows))


def hidden_kernel(experts, capacity, own, x_side, y_side, upper, lower, *refs):
    w_gate, w_up, out, joined, info, picked, probs, both, arrived = refs
    exp_dev, _, units = w_gate.shape
    for e in range(exp_dev):
        pltpu.make_async_copy(w_gate.at[e], both.at[e, :, pl.ds(0, units)], arrived.at[e]).start()
        pltpu.make_async_copy(w_up.at[e], both.at[e, :, pl.ds(units, units)], arrived.at[e]).start()
    joined[0 : upper.shape[0], :] = upper[...]
    joined[joined.shape[0] - lower.shape[0] :, :] = lower[...]
    tokens = [own, x_side, y_side, joined]
    total = len(tokens) * capacity
    rows = own.shape[0] - experts
    first = lax.axis_index("expert") * exp_dev
    slot = lax.broadcasted_iota(jnp.int32, (capacity, rows), 0).astype(FLOAT)
    lane = lax.broadcasted_iota(jnp.int32, (INFO, rows), 1).astype(FLOAT).astype(HALF)
    line = lax.broadcasted_iota(jnp.int32, (INFO, total), 0)
    expert = lax.broadcasted_iota(jnp.int32, (experts, rows), 0)
    info[...] = jnp.zeros(info.shape, FLOAT)
    origins = [[] for _ in range(exp_dev)]
    for m, block in enumerate(tokens):
        place, high, middle, low, number = (
            block[rows:, b * rows : (b + 1) * rows].astype(FLOAT) for b in range(5)
        )
        prob = high + middle + low
        info[SEQ_LINE + m : SEQ_LINE + m + 1, 0:rows] = number[0:1, :]
        picks = []
        for e in range(exp_dev):
            mine = expert == first + e
            own_place = jnp.sum(jnp.where(mine, place, 0.0), axis=0, keepdims=True)
            own_prob = jnp.sum(jnp.where(mine, prob, 0.0), axis=0, keepdims=True)
            pick = jnp.where(own_place == slot, 1.0, 0.0)
            probs[e, m * capacity : (m + 1) * capacity, :] = jnp.broadcast_to(
                jnp.sum(pick * own_prob, axis=1, keepdims=True), (capacity, LANES)
            )
            picks.append(pick.astype(HALF))
            origins[e].append(picks[-1])
        rows_m = dot_nn(jnp.concatenate(picks, axis=0), block[0:rows, :]).astype(HALF)
        for e in range(exp_dev):
            picked[e, m * capacity : (m + 1) * capacity, :] = rows_m[
                e * capacity : (e + 1) * capacity, :
            ]
    for e in range(exp_dev):
        origin = dot_nt(lane, jnp.concatenate(origins[e], axis=0))
        info[:, 0:total] = jnp.where(line == e, origin, info[:, 0:total])
    out[exp_dev * total :, :] = info[...].astype(HALF)

    def one_expert(e, carry):
        chosen = picked[e]
        pltpu.make_async_copy(both.at[e], both.at[e], arrived.at[e]).wait()
        product = dot_nn(chosen, both[e])
        gate, up = product[:, :units], product[:, units:]
        hidden = (gate / (1.0 + jnp.exp(-gate)) * up).astype(HALF)
        scaled = (probs[e, :, 0:1] * hidden.astype(FLOAT)).astype(HALF)
        out[pl.ds(pl.multiple_of(e * total, total), total), :] = scaled
        return carry

    lax.fori_loop(0, exp_dev, one_expert, 0)


def hidden_rows(tokens, w_gate, w_up, experts, capacity):
    lines, width = tokens[0].shape
    exp_dev, _, units = w_gate.shape
    total = 4 * capacity
    return pl.pallas_call(
        functools.partial(hidden_kernel, experts, capacity),
        in_specs=in_vmem(5) + [pl.BlockSpec(memory_space=pl.ANY)] * 2,
        out_specs=pl.BlockSpec(memory_space=pltpu.VMEM),
        out_shape=jax.ShapeDtypeStruct((exp_dev * total + INFO, units), HALF),
        scratch_shapes=[
            pltpu.VMEM((lines, width), HALF),
            pltpu.VMEM((INFO, units), FLOAT),
            pltpu.VMEM((exp_dev, total, width), HALF),
            pltpu.VMEM((exp_dev, total, LANES), FLOAT),
            pltpu.VMEM((exp_dev, width, 2 * units), HALF),
            pltpu.SemaphoreType.DMA((exp_dev,)),
        ],
        cost_estimate=cost(),
        compiler_params=params(56),
        name="hidden_rows",
    )(*tokens, w_gate, w_up)


def row_places(info, e, total, capacity, rows, sources):
    shift = (lax.broadcasted_iota(jnp.int32, (1, total), 1) // capacity * rows).astype(FLOAT)
    token = lax.broadcasted_iota(jnp.int32, (sources * rows, total), 0).astype(FLOAT)
    return jnp.where(token == info[e : e + 1, 0:total] + shift, 1.0, 0.0).astype(HALF)


def project_kernel(exp_dev, capacity, rows, sources, slots, *refs):
    blocks, (w_down, seqs), refs = refs[:slots], refs[slots : slots + 2], refs[slots + 2 :]
    partials, (packed, outs, places, arrived) = refs[:sources], refs[sources:]
    units = w_down.shape[1] // exp_dev
    total = sources * capacity
    fetches = [
        pltpu.make_async_copy(blocks[s], packed.at[s], arrived.at[s]) for s in range(slots)
    ]
    for copy in fetches:
        copy.start()

    def one_slot(s, carry):
        pltpu.make_async_copy(packed.at[s], packed.at[s], arrived.at[s]).wait()
        info = packed[s, exp_dev * total :, :].astype(FLOAT)
        seqs[s] = info[SEQ_LINE:, 0:rows]
        for e in range(exp_dev):
            here = slice(e * total, (e + 1) * total)
            outs[:, here] = dot_nt(
                w_down[:, e * units : (e + 1) * units], packed[s, here, :]
            ).astype(HALF)
            places[:, here] = row_places(info, e, total, capacity, rows, sources)
        part = dot_nt(outs[...], places[...]).astype(HALF)
        for k in range(sources):
            partials[k][s] = part[:, k * rows : (k + 1) * rows]
        return carry

    lax.fori_loop(0, slots, one_slot, 0)


def project(blocks, w_down, exp_dev, capacity, rows, sources):
    slots = len(blocks)
    feats = w_down.shape[0]
    total = exp_dev * sources * capacity
    out = pl.pallas_call(
        functools.partial(project_kernel, exp_dev, capacity, rows, sources, slots),
        in_specs=[pl.BlockSpec(memory_space=pl.ANY)] * slots + in_vmem(1),
        out_specs=in_vmem(1 + sources),
        out_shape=[jax.ShapeDtypeStruct((slots, 8, rows), FLOAT)]
        + [jax.ShapeDtypeStruct((slots, feats, rows), HALF)] * sources,
        scratch_shapes=[
            pltpu.VMEM((slots,) + blocks[0].shape, HALF),
            pltpu.VMEM((feats, total), HALF),
            pltpu.VMEM((sources * rows, total), HALF),
            pltpu.SemaphoreType.DMA((slots,)),
        ],
        cost_estimate=cost(),
        compiler_params=params(16),
        name="project",
    )(*blocks, w_down)
    return out[0], out[1:]


def spread_kernel(exp_dev, capacity, rows, sources, *refs):
    slots = len(refs) - 5
    blocks, (spread, packed, held, arrived, done) = refs[:slots], refs[slots:]
    units = packed.shape[2]
    total = sources * capacity
    fetches = [
        pltpu.make_async_copy(blocks[s], packed.at[s], arrived.at[s]) for s in range(slots)
    ]
    for copy in fetches:
        copy.start()

    def one_slot(s, carry):
        pltpu.make_async_copy(packed.at[s], packed.at[s], arrived.at[s]).wait()
        info = packed[s, exp_dev * total :, :].astype(FLOAT)
        for e in range(exp_dev):
            place = row_places(info, e, total, capacity, rows, sources)
            rows_e = packed[s, e * total : (e + 1) * total, :]
            held[s, :, e * units : (e + 1) * units] = dot_nn(place, rows_e).astype(HALF)
        pltpu.make_async_copy(held.at[s], spread.at[s], done.at[s]).start()
        return carry

    lax.fori_loop(0, slots, one_slot, 0)
    for s in range(slots):
        pltpu.make_async_copy(held.at[s], spread.at[s], done.at[s]).wait()


def spread_rows(blocks, exp_dev, capacity, rows, sources):
    slots = len(blocks)
    shape = (slots, sources * rows, exp_dev * blocks[0].shape[1])
    return pl.pallas_call(
        functools.partial(spread_kernel, exp_dev, capacity, rows, sources),
        in_specs=[pl.BlockSpec(memory_space=pl.ANY)] * slots,
        out_specs=pl.BlockSpec(memory_space=pl.ANY),
        out_shape=jax.ShapeDtypeStruct(shape, HALF),
        scratch_shapes=[
            pltpu.VMEM((slots,) + blocks[0].shape, HALF),
            pltpu.VMEM(shape, HALF),
            pltpu.SemaphoreType.DMA((slots,)),
            pltpu.SemaphoreType.DMA((slots,)),
        ],
        cost_estimate=cost(),
        compiler_params=params(24),
        name="spread_rows",
    )(*blocks)


def residual_kernel(first, slots, sources, carried, ordered, *refs):
    parts, (seq, targets, *refs) = refs[:sources], refs[sources:]
    if first:
        before, refs = refs[0], refs[1:]
    if carried:
        refs[-2][0:carried, :] = refs[0][...]
        refs = refs[1:]
    *blocks, errors, squares = refs
    feats, rows = targets.shape[1:]
    me = lax.axis_index("dp")
    number = lax.broadcasted_iota(jnp.int32, (NSEQ, rows), 0).astype(FLOAT)
    squared = jnp.zeros((NSEQ, rows), FLOAT)
    if ordered:
        for s in range(first):
            blocks[-1][me ^ s] = blocks[s][...]
    for s in range(slots):
        total = tree_sum([part[s].astype(FLOAT) for part in parts])
        if ordered:
            blocks[-1][me ^ (first + s)] = total.astype(HALF)
        else:
            blocks[s][...] = total.astype(HALF)
        error = total - targets[me ^ (first + s)].astype(FLOAT)
        errors[carried + s * feats : carried + (s + 1) * feats, :] = error.astype(HALF)
        per_token = jnp.sum(error * error, axis=0, keepdims=True)
        squared += jnp.where(seq[s, 0:1, :] == number, per_token, 0.0)
    sums = jnp.broadcast_to(col_to_row(jnp.sum(squared, axis=1, keepdims=True)), (8, LANES))
    squares[...] = sums + before[...] if first else sums


def residual(first, parts, seq, targets, before=(), errors=(), earlier=()):
    groups, feats, rows = targets.shape
    slots = parts[0].shape[0]
    sources = len(parts)
    ordered = len(earlier) > 0
    carried = sum(block.shape[0] for block in errors)
    if ordered:
        blocks = [jax.ShapeDtypeStruct((groups, feats, rows), HALF)]
    else:
        blocks = [jax.ShapeDtypeStruct((feats, rows), HALF)] * slots
    extra = [*before, *errors, *earlier]
    *combined, errors, squares = pl.pallas_call(
        functools.partial(residual_kernel, first, slots, sources, carried, ordered),
        in_specs=in_vmem(sources + 2 + len(extra)),
        out_specs=in_vmem(len(blocks) + 2),
        out_shape=blocks
        + [
            jax.ShapeDtypeStruct((carried + slots * feats, rows), HALF),
            jax.ShapeDtypeStruct((8, LANES), FLOAT),
        ],
        cost_estimate=cost(),
        compiler_params=params(16),
        name="residual",
    )(*parts, seq, targets, *extra)
    return combined, errors, squares


def gather_features_kernel(first, whole, *refs):
    late, out = refs[:-1], refs[-1]
    groups, feats, _ = whole.shape
    me = lax.axis_index("dp")
    for g in range(groups):
        out[:, g * feats : (g + 1) * feats] = whole[g].T
    for k, block in enumerate(late):
        start = pl.multiple_of((me ^ (first + k)) * feats, feats)
        out[:, pl.ds(start, feats)] = block[...].T


def gather_features(first, whole, late):
    groups, feats, rows = whole.shape
    return pl.pallas_call(
        functools.partial(gather_features_kernel, first),
        in_specs=in_vmem(1 + len(late)),
        out_specs=pl.BlockSpec(memory_space=pltpu.VMEM),
        out_shape=jax.ShapeDtypeStruct((rows, feats * groups), HALF),
        cost_estimate=cost(),
        compiler_params=params(16),
        name="gather_features",
    )(whole, *late)


def gradient_kernel(scale, feat_width, exp_dev, terms, batches, parts, sources, *refs):
    squares, refs = refs[:terms], refs[terms:]
    count, groups = len(batches), sum(batches)
    spreads, seqs, refs = refs[:count], refs[count : 2 * count], refs[2 * count :]
    errors, refs = refs[: sources * len(parts)], refs[sources * len(parts) :]
    grad, seq_loss, dual_weight, held, error, lines, weighted, total, rates, arrived = refs
    feats = grad.shape[0]
    rows = error.shape[2] // sources
    slot = 0
    for b, slots in enumerate(parts):
        for s in range(slots):
            for m in range(sources):
                pltpu.make_async_copy(
                    errors[b * sources + m].at[pl.ds(s * feats, feats), :],
                    error.at[slot, :, pl.ds(m * rows, rows)],
                    arrived.at[0, slot],
                ).start()
            slot += 1
    slot = 0
    for seq, spread, slots in zip(seqs, spreads, batches):
        for s in range(slots):
            lines[slot] = seq[s]
            pltpu.make_async_copy(
                spread.at[s],
                held.at[slot // 2, pl.ds(slot % 2 * sources * rows, sources * rows)],
                arrived.at[1, slot // 2],
            ).start()
            slot += 1
    number = lax.broadcasted_iota(jnp.int32, (NSEQ, rows), 0).astype(FLOAT)

    def count_slot(s, found):
        for m in range(sources):
            found += jnp.where(lines[s, m : m + 1, :] == number, 1.0, 0.0)
        return found

    found = lax.fori_loop(0, groups, count_slot, jnp.zeros((NSEQ, rows), FLOAT))
    seq_len = jnp.sum(found, axis=1, keepdims=True)
    summed = tree_sum([part[0:1, :] for part in squares])
    loss = row_to_col(summed, NSEQ) / (seq_len * feat_width)
    loss = jnp.broadcast_to(loss, (NSEQ, LANES))
    weight = dual_search_rows(loss)
    rates[...] = scale * (weight / seq_len)
    seq_loss[...] = col_to_row(loss)[:, 0:NSEQ]
    dual_weight[...] = col_to_row(weight)[:, 0:NSEQ]
    total[...] = jnp.zeros(total.shape, FLOAT)
    for s in range(groups):
        pltpu.make_async_copy(error.at[s], error.at[s], arrived.at[0, s]).wait()

    def weigh(pair, turn):
        for k in range(2):
            for m in range(sources):
                here = slice(m * rows, (m + 1) * rows)
                there = slice((k * sources + m) * rows, (k * sources + m + 1) * rows)
                hit = jnp.where(lines[2 * pair + k, m : m + 1, :] == number, rates[...], 0.0)
                rate = jnp.sum(hit, axis=0, keepdims=True)
                weighted[turn, :, there] = (
                    rate * error[2 * pair + k, :, here].astype(FLOAT)
                ).astype(HALF)

    def add_pair(pair, carry):
        pltpu.make_async_copy(held.at[pair], held.at[pair], arrived.at[1, pair]).wait()
        product = dot_nn(weighted[pair % 2], held[pair])
        weigh(jnp.minimum(pair + 1, groups // 2 - 1), (pair + 1) % 2)
        total[...] += product
        return carry

    weigh(0, 0)
    lax.fori_loop(0, groups // 2, add_pair, 0)
    units = grad.shape[2]
    for e in range(exp_dev):
        grad[:, e, :] = total[:, e * units : (e + 1) * units]


def dual_search_rows(loss):
    bound = jnp.sum(loss, axis=0, keepdims=True)

    def advance(step_index, bounds):
        lower, upper = bounds
        middle = 0.5 * (lower + upper)
        excess = jnp.maximum(loss - middle, 0.0)
        square_sum = jnp.sum(excess * excess, axis=0, keepdims=True)
        plain_sum = jnp.sum(excess, axis=0, keepdims=True)
        is_above = NSEQ * square_sum - radius_factor * plain_sum * plain_sum >= 0.0
        return (jnp.where(is_above, lower, middle), jnp.where(is_above, middle, upper))

    lower, upper = lax.fori_loop(
        0, BISECT_STEPS, advance, (-bound, bound), unroll=True
    )
    excess = jnp.maximum(loss - 0.5 * (lower + upper), 0.0)
    return excess / jnp.sum(excess, axis=0, keepdims=True)


def gradient(squares, spreads, seqs, errors, batches, parts, sources, scale, feat_width, exp_dev):
    rows = errors[0].shape[1]
    feats = errors[0].shape[0] // parts[0]
    group_rows, flat = spreads[0].shape[1:]
    units = flat // exp_dev
    groups = sum(batches)
    return pl.pallas_call(
        functools.partial(
            gradient_kernel, scale, feat_width, exp_dev, len(squares), batches, parts, sources
        ),
        in_specs=in_vmem(len(squares))
        + [pl.BlockSpec(memory_space=pl.ANY)] * len(spreads)
        + in_vmem(len(seqs))
        + [pl.BlockSpec(memory_space=pl.ANY)] * (len(errors) - sources)
        + in_vmem(sources),
        out_specs=in_vmem(3),
        out_shape=[
            jax.ShapeDtypeStruct((feats, exp_dev, units), FLOAT),
            jax.ShapeDtypeStruct((1, NSEQ), FLOAT),
            jax.ShapeDtypeStruct((1, NSEQ), FLOAT),
        ],
        scratch_shapes=[
            pltpu.VMEM((groups // 2, 2 * group_rows, flat), HALF),
            pltpu.VMEM((groups, feats, group_rows), HALF),
            pltpu.VMEM((groups, 8, rows), FLOAT),
            pltpu.VMEM((2, feats, 2 * group_rows), HALF),
            pltpu.VMEM((feats, flat), FLOAT),
            pltpu.VMEM((NSEQ, rows), FLOAT),
            pltpu.SemaphoreType.DMA((2, groups)),
        ],
        cost_estimate=cost(),
        compiler_params=params(58),
        name="gradient",
    )(*squares, *spreads, *seqs, *errors)


def z_near(block):
    return {2: swap(block, "dp", 2), 4: swap(block, "dp", 4)}


def z_far(blocks):
    return swap(blocks[4], "dp", 2)


def feature_plan(tokens, targets, routes, route_logits, slot_order, seq_ids, w_gate, w_up, w_down):
    rows, feat_width = tokens.shape
    groups, sources = lax.axis_size("dp"), lax.axis_size("expert")
    exp_dev, _, units = w_gate.shape
    experts = exp_dev * sources
    capacity = rows * routes.shape[1] // experts
    feats = feat_width // groups
    scale = float(rows * groups * sources // 8)
    far = range(1, sources)
    tie = lax.optimization_barrier

    own_tokens = pack_tokens(tokens, routes, route_logits, slot_order, seq_ids, experts)
    x_tokens, y_tokens = swap(own_tokens, "expert", 1), swap(own_tokens, "expert", 2)
    half = (rows + experts + 31) // 32 * 16
    diagonal = [swap(y_tokens[:half], "expert", 1), swap(x_tokens[-half:], "expert", 2)]
    turned, own_tokens = tie((targets.T, own_tokens))
    own_targets = lax.all_to_all(
        turned.reshape(groups, feats, rows), "dp", split_axis=0, concat_axis=0, tiled=True
    )
    x_tokens, y_tokens, diagonal, own_targets = tie((x_tokens, y_tokens, diagonal, own_targets))
    packed = hidden_rows(
        [own_tokens, x_tokens, y_tokens, *diagonal], w_gate, w_up, experts, capacity
    )
    blocks = {0: packed, **z_near(packed)}
    flat_down = w_down.reshape(feats, exp_dev * units)

    def expert_parts(first, slots):
        for s in range(first, first + slots, 2):
            blocks[s + 1] = swap(blocks[s], "dp", 1)
        here = [blocks[s] for s in range(first, first + slots)]
        seq, parts = project(here, flat_down, exp_dev, capacity, rows, sources)
        parts = [parts[0]] + [swap(parts[m], "expert", m) for m in far]
        spread = spread_rows(here, exp_dev, capacity, rows, sources)
        parts, spread = tie((parts, spread))
        return spread, seq, parts

    def far_errors(error):
        return [swap(error, "expert", m) for m in far]

    batches = (2, groups - 4, 2)
    spread_0, seq_0, parts_0 = expert_parts(0, batches[0])
    mixed_0, error_0, squares = residual(0, parts_0, seq_0, own_targets)
    errors_0 = far_errors(error_0)
    blocks, errors_0 = tie((blocks, errors_0))
    blocks[6] = z_far(blocks)

    spread_1, seq_1, parts_1 = expert_parts(2, batches[1])
    blocks[6], parts_1 = tie((blocks[6], parts_1))
    mixed_1, error_1, squares = residual(
        2, parts_1, seq_1, own_targets, before=[squares], earlier=mixed_0
    )
    mixed_1 = lax.all_to_all(mixed_1[0], "dp", split_axis=0, concat_axis=0, tiled=True)
    spread_2, seq_2, parts_2 = expert_parts(groups - 2, batches[2])
    mixed_2, error_1, squares = residual(
        groups - 2, parts_2, seq_2, own_targets, before=[squares], errors=[error_1]
    )
    errors_1 = far_errors(error_1)
    mixed_2 = [swap(block, "dp", groups - 2 + s) for s, block in enumerate(mixed_2)]
    mixed = gather_features(groups - 2, mixed_1, mixed_2)
    squares = squares + swap(squares, "dp", 1)
    squares = tree_sum([squares] + [swap(squares, "dp", m) for m in range(2, groups, 2)])
    all_squares = [squares] + [swap(squares, "expert", m) for m in far]
    grad_down, seq_loss, dual_weight = gradient(
        all_squares,
        [spread_0, spread_1, spread_2],
        [seq_0, seq_1, seq_2],
        [error_0, *errors_0, error_1, *errors_1],
        batches,
        (batches[0], batches[1] + batches[2]),
        sources,
        scale,
        feat_width,
        exp_dev,
    )
    return (
        mixed,
        seq_loss.reshape(NSEQ),
        dual_weight.reshape(NSEQ),
        grad_down,
    )


def local(tokens, targets, routes, route_logits, slot_order, seq_ids, w_gate, w_up, w_down):
    args = (tokens, targets, routes, route_logits, slot_order, seq_ids, w_gate, w_up, w_down)
    groups, sources = lax.axis_size("dp"), lax.axis_size("expert")
    units = w_gate.shape[2]
    exp_dev = w_gate.shape[0]
    rows, feat_width = tokens.shape
    capacity = rows * routes.shape[1] // (exp_dev * sources)
    whole_tiles = (
        feat_width % (groups * LANES) == 0
        and rows == LANES
        and units % LANES == 0
        and sources * capacity <= units
        and capacity % 16 == 0
        and exp_dev <= SEQ_LINE
        and exp_dev * sources == INFO
        and sources == 4
        and groups == 8
    )
    return (feature_plan if whole_tiles else row_plan)(*args)


def solution(mesh):
    return jax.shard_map(
        local,
        mesh=mesh,
        in_specs=(
            P(("dp", "expert"), None),
            P(("dp", "expert"), None),
            P(("dp", "expert"), None),
            P(("dp", "expert"), None),
            P(("dp", "expert"), None),
            P(("dp", "expert")),
            P("expert", None, None),
            P("expert", None, None),
            P("dp", "expert", None),
        ),
        out_specs=(P(("dp", "expert"), None), P(), P(), P("dp", "expert", None)),
        check_vma=False,
    )
```

```python
import functools

import jax
import jax.numpy as jnp
from jax import lax
from jax.experimental import pallas as pl
from jax.experimental.pallas import tpu as pltpu
from jax.sharding import PartitionSpec as P

NSEQ = 64
BISECT_STEPS = 40


radius_factor = 2.0


def unchanged(single_value):
    return single_value


def dual_search(seq_loss, pair_total, one_total):
    sum_total = one_total(jnp.sum(seq_loss))

    def advance(step_index, bounds):
        lower, upper = bounds
        middle = 0.5 * (lower + upper)
        excess = jnp.maximum(seq_loss - middle, 0.0)
        square_sum, plain_sum = pair_total((jnp.sum(excess * excess), jnp.sum(excess)))
        is_above = NSEQ * square_sum - radius_factor * plain_sum * plain_sum >= 0.0
        return (jnp.where(is_above, lower, middle), jnp.where(is_above, middle, upper))

    lower, upper = lax.fori_loop(0, BISECT_STEPS, advance, (-sum_total, sum_total))
    excess = jnp.maximum(seq_loss - 0.5 * (lower + upper), 0.0)
    return excess / one_total(jnp.sum(excess))


def route_gates(route_logits, slot_order):
    top_k = slot_order.shape[1]
    columns = lax.broadcasted_iota(jnp.int32, (1, 1, top_k), 2)
    picked = jnp.sum(
        jnp.where(slot_order[:, :, None] == columns, route_logits[:, None, :], 0.0), axis=2
    )
    raised = jnp.exp(picked)
    return raised / jnp.sum(raised, axis=1, keepdims=True)


def by_expert(blocks, groups):
    exp_dev = blocks.shape[0] // groups
    tail_shape = blocks.shape[1:]
    split_view = blocks.reshape((groups, exp_dev) + tail_shape)
    moved_view = jnp.swapaxes(split_view, 0, 1)
    return moved_view.reshape((exp_dev, groups * tail_shape[0]) + tail_shape[1:])


def by_source(local_rows, groups):
    exp_dev = local_rows.shape[0]
    capacity = local_rows.shape[1] // groups
    tail_shape = local_rows.shape[2:]
    split_view = local_rows.reshape((exp_dev, groups, capacity) + tail_shape)
    return jnp.swapaxes(split_view, 0, 1).reshape((exp_dev * groups, capacity) + tail_shape)


def row_plan(tokens, targets, routes, route_logits, slot_order, seq_ids, w_gate, w_up, w_down):
    tok_rows, feat_width = tokens.shape
    top_k = routes.shape[1]
    groups = lax.axis_size("expert")
    exp_dev = w_gate.shape[0]
    experts = exp_dev * groups
    slot_count = tok_rows * top_k
    capacity = slot_count // experts
    grad_scale = float(tok_rows * lax.axis_size("dp") * groups // 8)
    flat_route = routes.reshape(slot_count)
    expert_hot = (flat_route[:, None] == lax.broadcasted_iota(jnp.int32, (1, experts), 1)).astype(
        jnp.int32
    )
    slot_rank = jnp.sum((jnp.cumsum(expert_hot, axis=0) - 1) * expert_hot, axis=1)
    slot_index = flat_route * capacity + slot_rank
    inverse = (
        jnp.zeros((slot_count,), jnp.int32).at[slot_index].set(lax.iota(jnp.int32, slot_count))
    )
    source_row = inverse // top_k
    gate_probs = route_gates(route_logits, slot_order)
    send_rows = tokens[source_row].reshape(experts, capacity, feat_width)
    arrived = lax.all_to_all(send_rows, "expert", split_axis=0, concat_axis=0, tiled=True)
    local_rows = by_expert(arrived, groups)
    gate_proj = jnp.einsum("erd,edh->erh", local_rows, w_gate, preferred_element_type=jnp.float32)
    up_proj = jnp.einsum("erd,edh->erh", local_rows, w_up, preferred_element_type=jnp.float32)
    hidden = (jax.nn.silu(gate_proj) * up_proj).astype(jnp.bfloat16)
    expert_out = jnp.einsum(
        "erh,neh->ern",
        hidden,
        lax.all_gather(w_down, "dp", axis=0, tiled=True),
        preferred_element_type=jnp.float32,
    ).astype(jnp.bfloat16)
    returned = lax.all_to_all(
        by_source(expert_out, groups), "expert", split_axis=0, concat_axis=0, tiled=True
    )
    per_slot = returned.reshape(slot_count, feat_width)[slot_index].reshape(
        tok_rows, top_k, feat_width
    )
    combined = jnp.sum(gate_probs[:, :, None] * per_slot.astype(jnp.float32), axis=1)
    error = combined - targets.astype(jnp.float32)
    error_low = error.astype(jnp.bfloat16)
    sent_error = lax.all_to_all(
        error_low[source_row].reshape(experts, capacity, feat_width),
        "expert",
        split_axis=0,
        concat_axis=0,
        tiled=True,
    )
    seq_hot = seq_ids[:, None] == lax.broadcasted_iota(jnp.int32, (1, NSEQ), 1)
    partial_sq = jnp.sum(jnp.where(seq_hot, jnp.sum(error * error, axis=1)[:, None], 0.0), axis=0)
    counts = jnp.sum(seq_hot.astype(jnp.float32), axis=0)
    seq_sq, seq_len = lax.psum((partial_sq, counts), ("dp", "expert"))
    seq_loss = seq_sq / (seq_len * feat_width)
    dual_weight = dual_search(seq_loss, unchanged, unchanged)
    seq_rate = dual_weight / seq_len
    scaled_gates = grad_scale * gate_probs
    token_rate = jnp.sum(jnp.where(seq_hot, seq_rate[None, :], 0.0), axis=1)
    flat_weight = (scaled_gates * token_rate[:, None]).reshape(slot_count)
    slot_weight = lax.all_to_all(
        flat_weight[inverse].reshape(experts, capacity),
        "expert",
        split_axis=0,
        concat_axis=0,
        tiled=True,
    )
    weight_local = by_expert(slot_weight, groups)
    error_local = by_expert(sent_error, groups)
    scaled = (weight_local[:, :, None] * hidden).astype(jnp.bfloat16)
    grad_down = lax.psum_scatter(
        jnp.einsum("ern,erh->neh", error_local, scaled, preferred_element_type=jnp.float32),
        "dp",
        scatter_dimension=0,
        tiled=True,
    )
    return (combined.astype(jnp.bfloat16), seq_loss, dual_weight, grad_down)


LANES = 128
FLOAT = jnp.float32
HALF = jnp.bfloat16
INFO = 16
SEQ_LINE = 8


def swap(block, axis, mask):
    size = lax.axis_size(axis)
    return lax.ppermute(block, axis, [(s, s ^ mask) for s in range(size)])


def tree_sum(terms):
    while len(terms) > 1:
        rest = terms[len(terms) // 2 * 2 :]
        terms = [a + b for a, b in zip(terms[::2], terms[1::2])] + rest
    return terms[0]


def dot_nt(a, b):
    return lax.dot_general(a, b, (((1,), (1,)), ((), ())), preferred_element_type=FLOAT)


def dot_nn(a, b):
    return jnp.dot(a, b, preferred_element_type=FLOAT)


def cost():
    return pl.CostEstimate(flops=1, bytes_accessed=1, transcendentals=0)


def params(mib=60):
    return pltpu.CompilerParams(vmem_limit_bytes=mib << 20)


def col_to_row(col):
    count = col.shape[0]
    diagonal = lax.broadcasted_iota(jnp.int32, (count, LANES), 0) == lax.broadcasted_iota(
        jnp.int32, (count, LANES), 1
    )
    return jnp.sum(jnp.where(diagonal, col, 0.0), axis=0, keepdims=True)


def row_to_col(row, count):
    diagonal = lax.broadcasted_iota(jnp.int32, (count, LANES), 0) == lax.broadcasted_iota(
        jnp.int32, (count, LANES), 1
    )
    return jnp.sum(jnp.where(diagonal, row, 0.0), axis=1, keepdims=True)


def in_vmem(count=1):
    return [pl.BlockSpec(memory_space=pltpu.VMEM)] * count


def pack_tokens_kernel(experts, tokens, routes, logits, order, seq, out):
    top_k, rows = routes.shape
    names, slots, scores = routes[...], order[...], logits[...]
    picked = jnp.zeros((top_k, rows), FLOAT)
    for k in range(top_k):
        picked += jnp.where(slots == k, scores[k : k + 1, :], 0.0)
    raised = jnp.exp(picked)
    gates = raised / jnp.sum(raised, axis=0, keepdims=True)
    expert = lax.broadcasted_iota(jnp.int32, (experts, rows), 0)
    named = jnp.zeros((experts, rows), FLOAT)
    prob = jnp.zeros((experts, rows), FLOAT)
    for k in range(top_k):
        hit = names[k : k + 1, :] == expert
        named += jnp.where(hit, 1.0, 0.0)
        prob += jnp.where(hit, gates[k : k + 1, :], 0.0)
    before = lax.broadcasted_iota(jnp.int32, (rows, rows), 0) < lax.broadcasted_iota(
        jnp.int32, (rows, rows), 1
    )
    rank = dot_nn(named.astype(HALF), jnp.where(before, 1.0, 0.0).astype(HALF))
    place = jnp.where(named > 0.5, rank, -1.0).astype(HALF)
    number = jnp.broadcast_to(seq[...].astype(FLOAT), (experts, rows)).astype(HALF)
    out[0:rows, :] = tokens[...]
    out[rows:, :] = jnp.zeros((experts, out.shape[1]), HALF)
    for b, piece in enumerate([place, *exact_pieces(prob), number]):
        out[rows:, b * rows : (b + 1) * rows] = piece


def exact_pieces(value):
    pieces = []
    for _ in range(3):
        pieces.append(value.astype(HALF))
        value = value - pieces[-1].astype(FLOAT)
    return pieces


def pack_tokens(tokens, routes, route_logits, slot_order, seq_ids, experts):
    rows, width = tokens.shape
    return pl.pallas_call(
        functools.partial(pack_tokens_kernel, experts),
        in_specs=in_vmem(5),
        out_specs=pl.BlockSpec(memory_space=pltpu.VMEM),
        out_shape=jax.ShapeDtypeStruct((rows + experts, width), HALF),
        cost_estimate=cost(),
        compiler_params=params(),
        name="pack_tokens",
    )(tokens, routes.T, route_logits.T, slot_order.T, seq_ids.reshape(1, rows))


def hidden_kernel(experts, capacity, own, x_side, y_side, upper, lower, *refs):
    w_gate, w_up, out, joined, info, picked, probs, both, arrived = refs
    exp_dev, _, units = w_gate.shape
    piece = both.shape[1] // 4
    for e in range(exp_dev):
        for k, weights in enumerate((w_gate, w_up)):
            for p in range(4):
                lines = pl.ds(p * piece, piece)
                pltpu.make_async_copy(
                    weights.at[e, lines], both.at[e, lines, pl.ds(k * units, units)], arrived.at[e]
                ).start()
    joined[0 : upper.shape[0], :] = upper[...]
    joined[joined.shape[0] - lower.shape[0] :, :] = lower[...]
    tokens = [own, x_side, y_side, joined]
    total = len(tokens) * capacity
    rows = own.shape[0] - experts
    first = lax.axis_index("expert") * exp_dev
    slot = lax.broadcasted_iota(jnp.int32, (capacity, rows), 0).astype(FLOAT)
    lane = lax.broadcasted_iota(jnp.int32, (INFO, rows), 1).astype(FLOAT).astype(HALF)
    line = lax.broadcasted_iota(jnp.int32, (INFO, total), 0)
    expert = lax.broadcasted_iota(jnp.int32, (experts, rows), 0)
    info[...] = jnp.zeros(info.shape, FLOAT)
    origins = [[] for _ in range(exp_dev)]
    for m, block in enumerate(tokens):
        place, high, middle, low, number = (
            block[rows:, b * rows : (b + 1) * rows].astype(FLOAT) for b in range(5)
        )
        prob = high + middle + low
        info[SEQ_LINE + m : SEQ_LINE + m + 1, 0:rows] = number[0:1, :]
        picks = []
        for e in range(exp_dev):
            mine = expert == first + e
            own_place = jnp.sum(jnp.where(mine, place, 0.0), axis=0, keepdims=True)
            own_prob = jnp.sum(jnp.where(mine, prob, 0.0), axis=0, keepdims=True)
            pick = jnp.where(own_place == slot, 1.0, 0.0)
            probs[e, m * capacity : (m + 1) * capacity, :] = jnp.broadcast_to(
                jnp.sum(pick * own_prob, axis=1, keepdims=True), (capacity, LANES)
            )
            picks.append(pick.astype(HALF))
            origins[e].append(picks[-1])
        rows_m = dot_nn(jnp.concatenate(picks, axis=0), block[0:rows, :]).astype(HALF)
        for e in range(exp_dev):
            picked[e, m * capacity : (m + 1) * capacity, :] = rows_m[
                e * capacity : (e + 1) * capacity, :
            ]
    for e in range(exp_dev):
        origin = dot_nt(lane, jnp.concatenate(origins[e], axis=0))
        info[:, 0:total] = jnp.where(line == e, origin, info[:, 0:total])
    out[exp_dev * total :, :] = info[...].astype(HALF)

    def one_expert(e, carry):
        chosen = picked[e]
        pltpu.make_async_copy(both.at[e], both.at[e], arrived.at[e]).wait()
        product = dot_nn(chosen, both[e])
        gate, up = product[:, :units], product[:, units:]
        hidden = (gate / (1.0 + jnp.exp(-gate)) * up).astype(HALF)
        scaled = (probs[e, :, 0:1] * hidden.astype(FLOAT)).astype(HALF)
        out[pl.ds(pl.multiple_of(e * total, total), total), :] = scaled
        return carry

    lax.fori_loop(0, exp_dev, one_expert, 0)


def hidden_rows(tokens, w_gate, w_up, experts, capacity):
    lines, width = tokens[0].shape
    exp_dev, _, units = w_gate.shape
    total = 4 * capacity
    return pl.pallas_call(
        functools.partial(hidden_kernel, experts, capacity),
        in_specs=in_vmem(5) + [pl.BlockSpec(memory_space=pl.ANY)] * 2,
        out_specs=pl.BlockSpec(memory_space=pltpu.VMEM),
        out_shape=jax.ShapeDtypeStruct((exp_dev * total + INFO, units), HALF),
        scratch_shapes=[
            pltpu.VMEM((lines, width), HALF),
            pltpu.VMEM((INFO, units), FLOAT),
            pltpu.VMEM((exp_dev, total, width), HALF),
            pltpu.VMEM((exp_dev, total, LANES), FLOAT),
            pltpu.VMEM((exp_dev, width, 2 * units), HALF),
            pltpu.SemaphoreType.DMA((exp_dev,)),
        ],
        cost_estimate=cost(),
        compiler_params=params(56),
        name="hidden_rows",
    )(*tokens, w_gate, w_up)


def row_places(info, e, total, capacity, rows, sources):
    shift = (lax.broadcasted_iota(jnp.int32, (1, total), 1) // capacity * rows).astype(FLOAT)
    token = lax.broadcasted_iota(jnp.int32, (sources * rows, total), 0).astype(FLOAT)
    return jnp.where(token == info[e : e + 1, 0:total] + shift, 1.0, 0.0).astype(HALF)


def project_kernel(exp_dev, capacity, rows, sources, slots, *refs):
    blocks, (w_down, seqs), refs = refs[:slots], refs[slots : slots + 2], refs[slots + 2 :]
    partials, (packed, outs, places, arrived) = refs[:sources], refs[sources:]
    units = w_down.shape[1] // exp_dev
    total = sources * capacity
    fetches = [
        pltpu.make_async_copy(blocks[s], packed.at[s], arrived.at[s]) for s in range(slots)
    ]
    for copy in fetches:
        copy.start()

    def one_slot(s, carry):
        pltpu.make_async_copy(packed.at[s], packed.at[s], arrived.at[s]).wait()
        info = packed[s, exp_dev * total :, :].astype(FLOAT)
        seqs[s] = info[SEQ_LINE:, 0:rows]
        for e in range(exp_dev):
            here = slice(e * total, (e + 1) * total)
            outs[:, here] = dot_nt(
                w_down[:, e * units : (e + 1) * units], packed[s, here, :]
            ).astype(HALF)
            places[:, here] = row_places(info, e, total, capacity, rows, sources)
        part = dot_nt(outs[...], places[...]).astype(HALF)
        for k in range(sources):
            partials[k][s] = part[:, k * rows : (k + 1) * rows]
        return carry

    lax.fori_loop(0, slots, one_slot, 0)


def project(blocks, w_down, exp_dev, capacity, rows, sources):
    slots = len(blocks)
    feats = w_down.shape[0]
    total = exp_dev * sources * capacity
    out = pl.pallas_call(
        functools.partial(project_kernel, exp_dev, capacity, rows, sources, slots),
        in_specs=[pl.BlockSpec(memory_space=pl.ANY)] * slots + in_vmem(1),
        out_specs=in_vmem(1 + sources),
        out_shape=[jax.ShapeDtypeStruct((slots, 8, rows), FLOAT)]
        + [jax.ShapeDtypeStruct((slots, feats, rows), HALF)] * sources,
        scratch_shapes=[
            pltpu.VMEM((slots,) + blocks[0].shape, HALF),
            pltpu.VMEM((feats, total), HALF),
            pltpu.VMEM((sources * rows, total), HALF),
            pltpu.SemaphoreType.DMA((slots,)),
        ],
        cost_estimate=cost(),
        compiler_params=params(16),
        name="project",
    )(*blocks, w_down)
    return out[0], out[1:]


def spread_kernel(exp_dev, capacity, rows, sources, *refs):
    slots = len(refs) - 5
    blocks, (spread, packed, held, arrived, done) = refs[:slots], refs[slots:]
    units = packed.shape[2]
    total = sources * capacity
    fetches = [
        pltpu.make_async_copy(blocks[s], packed.at[s], arrived.at[s]) for s in range(slots)
    ]
    for copy in fetches:
        copy.start()

    def one_slot(s, carry):
        pltpu.make_async_copy(packed.at[s], packed.at[s], arrived.at[s]).wait()
        info = packed[s, exp_dev * total :, :].astype(FLOAT)
        for e in range(exp_dev):
            place = row_places(info, e, total, capacity, rows, sources)
            rows_e = packed[s, e * total : (e + 1) * total, :]
            held[s, :, e * units : (e + 1) * units] = dot_nn(place, rows_e).astype(HALF)
        pltpu.make_async_copy(held.at[s], spread.at[s], done.at[s]).start()
        return carry

    lax.fori_loop(0, slots, one_slot, 0)
    for s in range(slots):
        pltpu.make_async_copy(held.at[s], spread.at[s], done.at[s]).wait()


def spread_rows(blocks, exp_dev, capacity, rows, sources):
    slots = len(blocks)
    shape = (slots, sources * rows, exp_dev * blocks[0].shape[1])
    return pl.pallas_call(
        functools.partial(spread_kernel, exp_dev, capacity, rows, sources),
        in_specs=[pl.BlockSpec(memory_space=pl.ANY)] * slots,
        out_specs=pl.BlockSpec(memory_space=pl.ANY),
        out_shape=jax.ShapeDtypeStruct(shape, HALF),
        scratch_shapes=[
            pltpu.VMEM((slots,) + blocks[0].shape, HALF),
            pltpu.VMEM(shape, HALF),
            pltpu.SemaphoreType.DMA((slots,)),
            pltpu.SemaphoreType.DMA((slots,)),
        ],
        cost_estimate=cost(),
        compiler_params=params(24),
        name="spread_rows",
    )(*blocks)


def residual_kernel(first, batches, sources, *refs):
    parts, refs = refs[: sources * len(batches)], refs[sources * len(batches) :]
    seqs, (targets, *refs) = refs[: len(batches)], refs[len(batches) :]
    if first:
        before, refs = refs[0], refs[1:]
    combined, errors, squares = refs[-3:]
    feats, rows = targets.shape[1:]
    me = lax.axis_index("dp")
    number = lax.broadcasted_iota(jnp.int32, (NSEQ, rows), 0).astype(FLOAT)
    squared = jnp.zeros((NSEQ, rows), FLOAT)
    slot = 0
    for block in refs[:-3]:
        for s in range(block.shape[0]):
            combined[me ^ slot] = block[s]
            slot += 1
    ordered = len(refs) > 3
    slot = 0
    for b, slots in enumerate(batches):
        here = parts[b * sources : (b + 1) * sources]
        for s in range(slots):
            total = tree_sum([part[s].astype(FLOAT) for part in here])
            combined[me ^ (first + slot) if ordered else slot] = total.astype(HALF)
            error = total - targets[me ^ (first + slot)].astype(FLOAT)
            errors[slot * feats : (slot + 1) * feats, :] = error.astype(HALF)
            per_token = jnp.sum(error * error, axis=0, keepdims=True)
            squared += jnp.where(seqs[b][s, 0:1, :] == number, per_token, 0.0)
            slot += 1
    sums = jnp.broadcast_to(col_to_row(jnp.sum(squared, axis=1, keepdims=True)), (8, LANES))
    squares[...] = sums + before[...] if first else sums


def residual(first, parts, seqs, targets, before, earlier):
    feats, rows = targets.shape[1:]
    batches = tuple(batch[0].shape[0] for batch in parts)
    sources = len(parts[0])
    slots = sum(batches)
    extra = [before, *earlier] if first else []
    return pl.pallas_call(
        functools.partial(residual_kernel, first, batches, sources),
        in_specs=in_vmem((sources + 1) * len(batches) + 1 + len(extra)),
        out_specs=in_vmem(3),
        out_shape=[
            jax.ShapeDtypeStruct((slots + first * (len(earlier) > 0), feats, rows), HALF),
            jax.ShapeDtypeStruct((slots * feats, rows), HALF),
            jax.ShapeDtypeStruct((8, LANES), FLOAT),
        ],
        cost_estimate=cost(),
        compiler_params=params(16),
        name="residual",
    )(*[part for batch in parts for part in batch], *seqs, targets, *extra)


def gradient_kernel(scale, feat_width, exp_dev, terms, batches, parts, sources, *refs):
    squares, refs = refs[:terms], refs[terms:]
    count, groups = len(batches), sum(batches)
    spreads, seqs, refs = refs[:count], refs[count : 2 * count], refs[2 * count :]
    errors, refs = refs[: sources * len(parts)], refs[sources * len(parts) :]
    grad, seq_loss, dual_weight, held, error, lines, weighted, total, rates, arrived = refs
    feats = grad.shape[0]
    rows = error.shape[2] // sources
    slot = 0
    for b, slots in enumerate(parts):
        for s in range(slots):
            for m in range(sources):
                pltpu.make_async_copy(
                    errors[b * sources + m].at[pl.ds(s * feats, feats), :],
                    error.at[slot, :, pl.ds(m * rows, rows)],
                    arrived.at[0, slot],
                ).start()
            slot += 1
    slot = 0
    for seq, spread, slots in zip(seqs, spreads, batches):
        for s in range(slots):
            lines[slot] = seq[s]
            pltpu.make_async_copy(
                spread.at[s],
                held.at[slot // 2, pl.ds(slot % 2 * sources * rows, sources * rows)],
                arrived.at[1, slot // 2],
            ).start()
            slot += 1
    number = lax.broadcasted_iota(jnp.int32, (NSEQ, rows), 0).astype(FLOAT)

    def count_slot(s, found):
        for m in range(sources):
            found += jnp.where(lines[s, m : m + 1, :] == number, 1.0, 0.0)
        return found

    found = lax.fori_loop(0, groups, count_slot, jnp.zeros((NSEQ, rows), FLOAT))
    seq_len = jnp.sum(found, axis=1, keepdims=True)
    summed = tree_sum([part[0:1, :] for part in squares])
    loss = row_to_col(summed, NSEQ) / (seq_len * feat_width)
    loss = jnp.broadcast_to(loss, (NSEQ, LANES))
    weight = dual_search_rows(loss)
    rates[...] = scale * (weight / seq_len)
    seq_loss[...] = col_to_row(loss)[:, 0:NSEQ]
    dual_weight[...] = col_to_row(weight)[:, 0:NSEQ]
    total[...] = jnp.zeros(total.shape, FLOAT)
    for s in range(groups):
        pltpu.make_async_copy(error.at[s], error.at[s], arrived.at[0, s]).wait()

    def weigh(pair, turn):
        for k in range(2):
            for m in range(sources):
                here = slice(m * rows, (m + 1) * rows)
                there = slice((k * sources + m) * rows, (k * sources + m + 1) * rows)
                hit = jnp.where(lines[2 * pair + k, m : m + 1, :] == number, rates[...], 0.0)
                rate = jnp.sum(hit, axis=0, keepdims=True)
                weighted[turn, :, there] = (
                    rate * error[2 * pair + k, :, here].astype(FLOAT)
                ).astype(HALF)

    def add_pair(pair, carry):
        pltpu.make_async_copy(held.at[pair], held.at[pair], arrived.at[1, pair]).wait()
        product = dot_nn(weighted[pair % 2], held[pair])
        weigh(jnp.minimum(pair + 1, groups // 2 - 1), (pair + 1) % 2)
        total[...] += product
        return carry

    weigh(0, 0)
    lax.fori_loop(0, groups // 2, add_pair, 0)
    units = grad.shape[2]
    for e in range(exp_dev):
        grad[:, e, :] = total[:, e * units : (e + 1) * units]


def dual_search_rows(loss):
    bound = jnp.sum(loss, axis=0, keepdims=True)

    def advance(step_index, bounds):
        lower, upper = bounds
        middle = 0.5 * (lower + upper)
        excess = jnp.maximum(loss - middle, 0.0)
        square_sum = jnp.sum(excess * excess, axis=0, keepdims=True)
        plain_sum = jnp.sum(excess, axis=0, keepdims=True)
        is_above = NSEQ * square_sum - radius_factor * plain_sum * plain_sum >= 0.0
        return (jnp.where(is_above, lower, middle), jnp.where(is_above, middle, upper))

    lower, upper = lax.fori_loop(
        0, BISECT_STEPS, advance, (-bound, bound), unroll=True
    )
    excess = jnp.maximum(loss - 0.5 * (lower + upper), 0.0)
    return excess / jnp.sum(excess, axis=0, keepdims=True)


def gradient(squares, spreads, seqs, errors, batches, parts, sources, scale, feat_width, exp_dev):
    rows = errors[0].shape[1]
    feats = errors[0].shape[0] // parts[0]
    group_rows, flat = spreads[0].shape[1:]
    units = flat // exp_dev
    groups = sum(batches)
    return pl.pallas_call(
        functools.partial(
            gradient_kernel, scale, feat_width, exp_dev, len(squares), batches, parts, sources
        ),
        in_specs=in_vmem(len(squares))
        + [pl.BlockSpec(memory_space=pl.ANY)] * len(spreads)
        + in_vmem(len(seqs))
        + [pl.BlockSpec(memory_space=pl.ANY)] * len(errors),
        out_specs=in_vmem(3),
        out_shape=[
            jax.ShapeDtypeStruct((feats, exp_dev, units), FLOAT),
            jax.ShapeDtypeStruct((1, NSEQ), FLOAT),
            jax.ShapeDtypeStruct((1, NSEQ), FLOAT),
        ],
        scratch_shapes=[
            pltpu.VMEM((groups // 2, 2 * group_rows, flat), HALF),
            pltpu.VMEM((groups, feats, group_rows), HALF),
            pltpu.VMEM((groups, 8, rows), FLOAT),
            pltpu.VMEM((2, feats, 2 * group_rows), HALF),
            pltpu.VMEM((feats, flat), FLOAT),
            pltpu.VMEM((NSEQ, rows), FLOAT),
            pltpu.SemaphoreType.DMA((2, groups)),
        ],
        cost_estimate=cost(),
        compiler_params=params(),
        name="gradient",
    )(*squares, *spreads, *seqs, *errors)


def z_near(block):
    return {2: swap(block, "dp", 2), 4: swap(block, "dp", 4)}


def z_far(blocks):
    return swap(blocks[4], "dp", 2)


def feature_plan(tokens, targets, routes, route_logits, slot_order, seq_ids, w_gate, w_up, w_down):
    rows, feat_width = tokens.shape
    groups, sources = lax.axis_size("dp"), lax.axis_size("expert")
    exp_dev, _, units = w_gate.shape
    experts = exp_dev * sources
    capacity = rows * routes.shape[1] // experts
    feats = feat_width // groups
    scale = float(rows * groups * sources // 8)
    far = range(1, sources)
    tie = lax.optimization_barrier

    own_tokens = pack_tokens(tokens, routes, route_logits, slot_order, seq_ids, experts)
    x_tokens, y_tokens = swap(own_tokens, "expert", 1), swap(own_tokens, "expert", 2)
    half = (rows + experts + 31) // 32 * 16
    diagonal = [swap(y_tokens[:half], "expert", 1), swap(x_tokens[-half:], "expert", 2)]
    turned, own_tokens = tie((targets.T, own_tokens))
    own_targets = lax.all_to_all(
        turned.reshape(groups, feats, rows), "dp", split_axis=0, concat_axis=0, tiled=True
    )
    x_tokens, y_tokens, diagonal, own_targets = tie((x_tokens, y_tokens, diagonal, own_targets))
    packed = hidden_rows(
        [own_tokens, x_tokens, y_tokens, *diagonal], w_gate, w_up, experts, capacity
    )
    blocks = {0: packed, **z_near(packed)}
    flat_down = w_down.reshape(feats, exp_dev * units)

    def expert_parts(first, slots):
        for s in range(first, first + slots, 2):
            blocks[s + 1] = swap(blocks[s], "dp", 1)
        here = [blocks[s] for s in range(first, first + slots)]
        seq, parts = project(here, flat_down, exp_dev, capacity, rows, sources)
        parts = [parts[0]] + [swap(parts[m], "expert", m) for m in far]
        spread = spread_rows(here, exp_dev, capacity, rows, sources)
        parts, spread = tie((parts, spread))
        return spread, seq, parts

    def far_errors(error):
        return [swap(error, "expert", m) for m in far]

    batches = (2, groups - 4, 2)
    spread_0, seq_0, parts_0 = expert_parts(0, batches[0])
    mixed_0, error_0, squares = residual(0, [parts_0], [seq_0], own_targets, None, [])
    errors_0 = far_errors(error_0)
    blocks, errors_0 = tie((blocks, errors_0))
    blocks[6] = z_far(blocks)

    spread_1, seq_1, parts_1 = expert_parts(2, batches[1])
    blocks[6], parts_1 = tie((blocks[6], parts_1))
    spread_2, seq_2, parts_2 = expert_parts(groups - 2, batches[2])
    mixed, error_1, squares = residual(
        2, [parts_1, parts_2], [seq_1, seq_2], own_targets, squares, [mixed_0]
    )
    far_squares = [swap(squares, "expert", m) for m in far]
    error_1, far_squares = tie((error_1, far_squares))
    errors_1 = far_errors(error_1)
    squares = tree_sum([squares] + far_squares)
    squares = squares + swap(squares, "dp", 1)
    all_squares = [squares] + [swap(squares, "dp", m) for m in range(2, groups, 2)]
    mixed = lax.all_to_all(mixed, "dp", split_axis=0, concat_axis=0, tiled=True)
    grad_down, seq_loss, dual_weight = gradient(
        all_squares,
        [spread_0, spread_1, spread_2],
        [seq_0, seq_1, seq_2],
        [error_0, *errors_0, error_1, *errors_1],
        batches,
        (batches[0], batches[1] + batches[2]),
        sources,
        scale,
        feat_width,
        exp_dev,
    )
    return (
        mixed.reshape(feat_width, rows).T,
        seq_loss.reshape(NSEQ),
        dual_weight.reshape(NSEQ),
        grad_down,
    )


def local(tokens, targets, routes, route_logits, slot_order, seq_ids, w_gate, w_up, w_down):
    args = (tokens, targets, routes, route_logits, slot_order, seq_ids, w_gate, w_up, w_down)
    groups, sources = lax.axis_size("dp"), lax.axis_size("expert")
    units = w_gate.shape[2]
    exp_dev = w_gate.shape[0]
    rows, feat_width = tokens.shape
    capacity = rows * routes.shape[1] // (exp_dev * sources)
    whole_tiles = (
        feat_width % (groups * LANES) == 0
        and rows == LANES
        and units % LANES == 0
        and sources * capacity <= units
        and capacity % 16 == 0
        and exp_dev <= SEQ_LINE
        and exp_dev * sources == INFO
        and sources == 4
        and groups == 8
    )
    return (feature_plan if whole_tiles else row_plan)(*args)


def solution(mesh):
    return jax.shard_map(
        local,
        mesh=mesh,
        in_specs=(
            P(("dp", "expert"), None),
            P(("dp", "expert"), None),
            P(("dp", "expert"), None),
            P(("dp", "expert"), None),
            P(("dp", "expert"), None),
            P(("dp", "expert")),
            P("expert", None, None),
            P("expert", None, None),
            P("dp", "expert", None),
        ),
        out_specs=(P(("dp", "expert"), None), P(), P(), P("dp", "expert", None)),
        check_vma=False,
    )
```
